256 devices in a mesh: dp: 4 (over x), seq: 64 (over z, y, core).
Axes of the slice: x: 4, y: 4, z: 8, core: 2. Of those that a mesh axis runs over, the one named last changes fastest.
Arguments:
- tokens: bfloat16 [4, 16384, 1024], P('dp', 'seq'), may hold values from -6 to 6
- cotangent: bfloat16 [4, 16384, 1024], P('dp', 'seq'), may hold values from -6 to 6
- gain: float32 [1024], replicated, may hold values from 0.1 to 1.9
- w_u: bfloat16 [4, 256, 256], replicated, may hold values from -0.375 to 0.375
- w_v: bfloat16 [4, 256, 256], replicated, may hold values from -0.375 to 0.375
- w_o: bfloat16 [4, 256, 256], replicated, may hold values from -0.375 to 0.375
- local_factor: bfloat16 [16384, 256], P('seq'), may hold values from -0.375 to 0.375
- butterfly: float32 [6, 2, 2, 1024], replicated, may hold values from 0.45 to 0.8
Outputs:
- mixed: bfloat16 [4, 16384, 1024], P('dp', 'seq')
- grad_tokens: bfloat16 [4, 16384, 1024], P('dp', 'seq')
- grad_w_u: float32 [4, 256, 256], replicated
- grad_w_v: float32 [4, 256, 256], replicated
- grad_w_o: float32 [4, 256, 256], replicated
- grad_gain: float32 [1024], replicated
- grad_local: float32 [16384, 256], P('seq')
- grad_butterfly: float32 [6, 2, 2, 1024], replicated
The draws below stay inside these ranges and needn't reach their ends.
All inputs are finite; a program needn't handle non-finite values.
Results may differ from the reference program's by a relative error of at most 0.015.
Values may be sent and summed in bfloat16 or wider, within the bound.
No kernel may reach another device: no remote copies, remote signals or barrier semaphores. Data moves between devices by JAX's collectives and lax.ppermute only.
A program may use at most 64 MiB of HBM per device.

```python
import jax
import jax.numpy as jnp
from jax import lax

D = 1024
BLK = 256
TOK_DEV = 256
TOKENS = 16384
BATCH = 4
GROUPS = 4
LOGSEQ = 6
N_SEQ = 64


def block_scale(own_key, shape, cuts, smallest, largest):
    def one(axis_at, shards_of):
        steps = jax.random.uniform(jax.random.fold_in(jax.random.fold_in(own_key, 6), axis_at), (shards_of,), jnp.float32, smallest / len(cuts), largest / len(cuts))
        return jnp.repeat(jnp.exp(steps), shape[axis_at] // shards_of).reshape((-1,) + (1,) * (len(shape) - axis_at - 1))

    level = one(*cuts[0])
    for cut in cuts[1:]:
        level = level * one(*cut)
    return level


def gaussian(stream_key, dims, spread, reach, shards=(), kind=jnp.bfloat16):
    level = block_scale(stream_key, dims, shards, -0.22, 0.18) if shards else 1.0
    drawn = jax.random.normal(stream_key, dims, jnp.float32) * spread * level
    return jnp.minimum(jnp.maximum(drawn, -reach), reach).astype(kind)


def setup_inputs(seed: int = 0) -> dict:
    key_list = jax.random.split(jax.random.key(seed), 9)
    return {
        "tokens": gaussian(key_list[0], (BATCH, TOKENS, D), 1.0, 6.0, ((0, 4), (1, 64))),
        "cotangent": gaussian(key_list[1], (BATCH, TOKENS, D), 1.0, 6.0, ((0, 4), (1, 64))),
        "gain": jnp.clip(1.0 + 0.18 * jax.random.normal(key_list[2], (D,), jnp.float32), 0.1, 1.9),
        "w_u": gaussian(key_list[3], (GROUPS, BLK, BLK), BLK ** -0.5, 0.375),
        "w_v": gaussian(key_list[4], (GROUPS, BLK, BLK), BLK ** -0.5, 0.375),
        "w_o": gaussian(key_list[5], (GROUPS, BLK, BLK), BLK ** -0.5, 0.375),
        "local_factor": gaussian(key_list[6], (TOKENS, TOK_DEV), TOK_DEV ** -0.5, 0.375, ((0, 64),)),
        "butterfly": jnp.clip(jax.random.uniform(key_list[7], (LOGSEQ, 2, 2, D), jnp.float32, 0.45, 0.8), 0.45, 0.8),
    }


def channel(field, weight):
    grouped = field.reshape(field.shape[0], GROUPS, BLK).astype(jnp.float32)
    return jnp.einsum('tgi,gij->tgj', grouped, weight.astype(jnp.float32)).reshape(field.shape)

def channel_back(field, weight):
    grouped = field.reshape(field.shape[0], GROUPS, BLK).astype(jnp.float32)
    return jnp.einsum('tgj,gij->tgi', grouped, weight.astype(jnp.float32)).reshape(field.shape)

def channel_grad(left, right):
    first = left.reshape(left.shape[0], GROUPS, BLK).astype(jnp.float32)
    second = right.reshape(right.shape[0], GROUPS, BLK).astype(jnp.float32)
    return jnp.einsum('tgi,tgj->gij', first, second)

def flip_blocks(field, section):
    count, rows, width = field.shape
    span = 1 << section
    return field.reshape(count // (2 * span), 2, span, rows, width)[:, ::-1].reshape(count, rows, width)

def reference(tokens, cotangent, gain, w_u, w_v, w_o, local_factor, butterfly):
    factor = local_factor.reshape(N_SEQ, TOK_DEV, TOK_DEV).astype(jnp.float32)
    blocks = jnp.arange(N_SEQ, dtype=jnp.int32)

    def one(carry, pair):
        x_row, dy_row = pair
        x = x_row.astype(jnp.float32)
        r = lax.rsqrt(lax.optimization_barrier(jnp.mean(x * x, axis=-1, keepdims=True)) + 1e-06)
        xn = (x * r * gain).astype(jnp.bfloat16)
        u = channel(xn, w_u).astype(jnp.bfloat16)
        v = channel(xn, w_v)
        ublk = u.reshape(N_SEQ, TOK_DEV, D)
        state = jnp.einsum('nts,nsd->ntd', factor, ublk.astype(jnp.float32)).astype(jnp.bfloat16)
        saved = []
        for section in range(LOGSEQ):
            saved.append(state)
            bits = (blocks >> section & 1)[:, None]
            own = jnp.where(bits == 1, butterfly[section, 1, 0], butterfly[section, 0, 0])
            other = jnp.where(bits == 1, butterfly[section, 1, 1], butterfly[section, 0, 1])
            state = (own[:, None, :] * state.astype(jnp.float32) + other[:, None, :] * flip_blocks(state, section).astype(jnp.float32)).astype(jnp.bfloat16)
        zflat = state.reshape(TOKENS, D).astype(jnp.float32)
        sig = jax.nn.sigmoid(v)
        act = v * sig
        dact = sig * (1.0 + v * (1.0 - sig))
        gated = (zflat * act).astype(jnp.bfloat16)
        mixed = channel(gated, w_o).astype(jnp.bfloat16)
        dg = channel_back(dy_row, w_o)
        grad_o = channel_grad(gated, dy_row)
        back = (dg * act).astype(jnp.bfloat16).reshape(N_SEQ, TOK_DEV, D)
        dv = (dg * zflat * dact).astype(jnp.bfloat16)
        section_grads = [None] * LOGSEQ
        for section in reversed(range(LOGSEQ)):
            prior = saved[section].astype(jnp.float32)
            bits = (blocks >> section & 1)[:, None]
            bitsf = (blocks >> section & 1).astype(jnp.float32)
            own = jnp.where(bits == 1, butterfly[section, 1, 0], butterfly[section, 0, 0])
            cross = jnp.where(bits == 1, butterfly[section, 0, 1], butterfly[section, 1, 1])
            backf = back.astype(jnp.float32)
            partner = flip_blocks(back, section).astype(jnp.float32)
            own_sum = lax.optimization_barrier(jnp.sum(backf * prior, axis=1))
            cross_sum = lax.optimization_barrier(jnp.sum(partner * prior, axis=1))
            sides = jnp.stack([1.0 - bitsf, bitsf])
            grad_own = lax.optimization_barrier(jnp.sum(sides[:, :, None] * own_sum[None], axis=1))
            grad_cross = lax.optimization_barrier(jnp.sum(sides[::-1][:, :, None] * cross_sum[None], axis=1))
            section_grads[section] = jnp.stack([grad_own, grad_cross], axis=1)
            back = (own[:, None, :] * backf + cross[:, None, :] * partner).astype(jnp.bfloat16)
        backf = back.astype(jnp.float32)
        grad_block = jnp.einsum('ntd,nsd->nts', backf, ublk.astype(jnp.float32))
        du = jnp.einsum('nts,ntd->nsd', factor, backf).astype(jnp.bfloat16).reshape(TOKENS, D)
        dxn = channel_back(du, w_u) + channel_back(dv, w_v)
        grad_u = channel_grad(xn, du)
        grad_v = channel_grad(xn, dv)
        grad_g = lax.optimization_barrier(jnp.sum(dxn * x * r, axis=0))
        scaled = dxn * gain
        dx = (r * (scaled - x * r * r * lax.optimization_barrier(jnp.mean(scaled * x, axis=-1, keepdims=True)))).astype(jnp.bfloat16)
        total = (carry[0] + grad_u, carry[1] + grad_v, carry[2] + grad_o, carry[3] + grad_g, carry[4] + grad_block, carry[5] + jnp.stack(section_grads))
        return (total, (mixed, dx))
    square = jnp.zeros((GROUPS, BLK, BLK), jnp.float32)
    start = (square, square, square, jnp.zeros((D,), jnp.float32), jnp.zeros((N_SEQ, TOK_DEV, TOK_DEV), jnp.float32), jnp.zeros((LOGSEQ, 2, 2, D), jnp.float32))
    sums, rows = lax.scan(one, start, (tokens, cotangent))
    return (rows[0], rows[1], sums[0], sums[1], sums[2], sums[3], sums[4].reshape(TOKENS, TOK_DEV), sums[5])
```

```python
import functools

import jax
import jax.numpy as jnp
from jax import lax
from jax.experimental import pallas as pl
from jax.experimental.pallas import tpu as pltpu
from jax.sharding import Mesh, PartitionSpec as P

BF = jnp.bfloat16
F32 = jnp.float32
GROUPS = 4
BLK = 256
BLOCKS = 64
PL = 16
SEQ = ("z", "y", "c")
SAME_GROUP = ("dp", "z", "c")


def dot(a, b, dims):
    return lax.dot_general(a, b, (dims, ((), ())), preferred_element_type=F32)


def mm(a, b):
    return dot(a, b, ((1,), (0,)))


def mm_nt(a, b):
    return dot(a, b, ((1,), (1,)))


def mm_tn(a, b):
    return dot(a, b, ((0,), (0,)))


def lanes(g):
    return slice(g * BLK, (g + 1) * BLK)


def inv_rms(x_ref):
    total = jnp.zeros((BLK, 1), F32)
    for g in range(GROUPS):
        x = x_ref[:, lanes(g)].astype(F32)
        total = total + jnp.sum(x * x, axis=-1, keepdims=True)
    return lax.rsqrt(total * (1.0 / (GROUPS * BLK)) + 1e-06)


def first_kernel(x_ref, cot_ref, gain_ref, local_ref, send_ref):
    r = inv_rms(x_ref)
    local = local_ref[...]
    for g in range(GROUPS):
        xn = (x_ref[:, lanes(g)].astype(F32) * r * gain_ref[:, lanes(g)]).astype(BF)
        q = mm(local, xn).astype(BF)
        for at, value in enumerate((q, xn, cot_ref[:, lanes(g)])):
            send_ref[:, g, :, at * PL : (at + 1) * PL, :] = value.reshape(8, 2, PL, BLK)


def side_kernel(x_ref, cot_ref, gain_ref, wu_ref, wv_ref, wo_ref, u_ref, act_ref, dgd_ref):
    r = inv_rms(x_ref)
    for g in range(GROUPS):
        xn = (x_ref[:, lanes(g)].astype(F32) * r * gain_ref[:, lanes(g)]).astype(BF)
        u_ref[:, lanes(g)] = mm(xn, wu_ref[g]).astype(BF)
        v = mm(xn, wv_ref[g])
        sig = jax.nn.sigmoid(v)
        act_ref[:, lanes(g)] = v * sig
        dg = mm_nt(cot_ref[:, lanes(g)], wo_ref[g])
        dgd_ref[:, lanes(g)] = dg * (sig * (1.0 + v * (1.0 - sig)))


def tiles_of(value):
    split = value.reshape(16, 2, 8, BLK)
    return split[..., :128], split[..., 128:]


def from_tiles(ref, at):
    part = ref[pl.ds(at * 16, 16)]
    return jnp.concatenate([part[:, :, 0], part[:, :, 1]], axis=-1).reshape(BLK, BLK)


def mid_kernel(
    recv_ref, coef_ref, wu_ref, wv_ref, wo_ref,
    send_ref, grad_ref,
    z0, zs, es, act_s, dgd_s, coef, acc, gsum,
):
    for row in range(24):
        for lh in range(2):
            coef[row, lh] = jnp.broadcast_to(
                coef_ref[row : row + 1, lh * 128 : (lh + 1) * 128], (8, 128)
            )
    acc[...] = jnp.zeros_like(acc)
    gsum[...] = jnp.zeros_like(gsum)

    def rows(at, which):
        return recv_ref[pl.ds(at * 16, 16), which * PL : (which + 1) * PL, :].reshape(BLK, BLK)

    @pl.loop(0, 4)
    def _(at):
        here = pl.ds(at * 16, 16)
        p = mm(rows(at, 0), wu_ref[...]).astype(BF).astype(F32)
        v = mm(rows(at, 1), wv_ref[...])
        dg = mm_nt(rows(at, 2), wo_ref[...])
        sig = jax.nn.sigmoid(v)
        act = v * sig
        e = (dg * act).astype(BF).astype(F32)
        act_s[pl.ds(at * BLK, BLK), :] = act
        dgd_s[pl.ds(at * BLK, BLK), :] = dg * (sig * (1.0 + v * (1.0 - sig)))
        for lh, (pt, et) in enumerate(zip(tiles_of(p), tiles_of(e))):
            z0[here, :, lh] = pt
            es[here, :, lh] = et

    def place(t):
        return t >> 2, (t >> 1) & 1, t & 1

    def forward(z, bits, lh):
        states = [z]
        for j, k in enumerate(bits):
            z = [
                coef[4 * k + 2 * (i >> j & 1), lh] * z[i]
                + coef[4 * k + 2 * (i >> j & 1) + 1, lh] * z[i ^ (1 << j)]
                for i in range(8)
            ]
            states.append(z)
        return states

    def backward(e, states, bits, lh):
        for j, k in reversed(tuple(enumerate(bits))):
            z = states[j]
            for b in range(2):
                at = [i for i in range(8) if (i >> j & 1) == b]
                acc[4 * k + 2 * b, lh] += sum(e[i] * z[i] for i in at)
                acc[4 * k + 2 * b + 1, lh] += sum(e[i] * z[i ^ (1 << j)] for i in at)
            e = [
                coef[4 * k + 2 * (i >> j & 1), lh] * e[i]
                + coef[4 * k + 2 * (1 - (i >> j & 1)) + 1, lh] * e[i ^ (1 << j)]
                for i in range(8)
            ]
        return e

    low, high = (0, 1, 2), (3, 4, 5)

    @pl.loop(0, 32)
    def _(t):
        hi, rh, lh = place(t)
        z = forward([z0[hi * 8 + i, rh, lh] for i in range(8)], low, lh)[-1]
        for i in range(8):
            zs[hi * 8 + i, rh, lh] = z[i]

    @pl.loop(0, 32)
    def _(t):
        lo, rh, lh = place(t)
        states = forward([zs[i * 8 + lo, rh, lh] for i in range(8)], high, lh)
        for i in range(8):
            zs[i * 8 + lo, rh, lh] = states[3][i]
        e = backward([es[i * 8 + lo, rh, lh] for i in range(8)], states, high, lh)
        for i in range(8):
            es[i * 8 + lo, rh, lh] = e[i]

    @pl.loop(0, 32)
    def _(t):
        hi, rh, lh = place(t)
        states = forward([z0[hi * 8 + i, rh, lh] for i in range(8)], low, lh)
        e = backward([es[hi * 8 + i, rh, lh] for i in range(8)], states, low, lh)
        for i in range(8):
            es[hi * 8 + i, rh, lh] = e[i]

    @pl.loop(0, 4)
    def _(at):
        here = pl.ds(at * 16, 16)
        z = from_tiles(zs, at).astype(BF)
        e = from_tiles(es, at).astype(BF)
        send_ref[here, :PL, :] = z.reshape(16, PL, BLK)
        send_ref[here, PL:, :] = e.reshape(16, PL, BLK)
        zf = z.astype(F32)
        gated = (zf * act_s[pl.ds(at * BLK, BLK), :]).astype(BF)
        dv = (zf * dgd_s[pl.ds(at * BLK, BLK), :]).astype(BF)
        gsum[0] += mm_tn(rows(at, 0), e)
        gsum[1] += mm_tn(rows(at, 1), dv)
        gsum[2] += mm_tn(gated, rows(at, 2))

    grad_ref[...] = jnp.zeros_like(grad_ref)
    for half in range(2):
        cut = slice(half * 128, (half + 1) * 128)
        for w in range(3):
            grad_ref[:, half, w] = gsum[w].reshape(32, 8, BLK)[:, :, cut].astype(BF)
        for part in range(3):
            sums = jnp.sum(acc[part * 8 : (part + 1) * 8, half], axis=1)
            grad_ref[part, half, 3] = sums.astype(BF)


def group_of(recv_ref, g, which):
    return recv_ref[:, g, :, which * PL : (which + 1) * PL, :].reshape(BLK, BLK)


def local_kernel(recv_ref, u_ref, out_ref):
    total = jnp.zeros((BLK, BLK), F32)
    for g in range(GROUPS):
        total = total + mm_nt(group_of(recv_ref, g, 1), u_ref[:, lanes(g)])
    out_ref[...] = total.astype(BF)


def last_kernel(
    recv_ref, x_ref, gain_ref, act_ref, dgd_ref, wu_ref, wv_ref, wo_ref, local_ref,
    mixed_ref, dx_ref, scaled_ref,
):
    r = inv_rms(x_ref)
    local = local_ref[...]
    inner = jnp.zeros((BLK, 1), F32)
    for g in range(GROUPS):
        z = group_of(recv_ref, g, 0).astype(F32)
        gated = (z * act_ref[:, lanes(g)]).astype(BF)
        mixed_ref[:, lanes(g)] = mm(gated, wo_ref[g]).astype(BF)
        dv = (z * dgd_ref[:, lanes(g)]).astype(BF)
        du = mm_tn(local, group_of(recv_ref, g, 1)).astype(BF)
        scaled = (mm_nt(du, wu_ref[g]) + mm_nt(dv, wv_ref[g])) * gain_ref[:, lanes(g)]
        scaled_ref[:, lanes(g)] = scaled
        inner = inner + jnp.sum(scaled * x_ref[:, lanes(g)].astype(F32), axis=-1, keepdims=True)
    shift = r * r * inner * (1.0 / (GROUPS * BLK))
    for g in range(GROUPS):
        x = x_ref[:, lanes(g)].astype(F32)
        dx_ref[:, lanes(g)] = (r * (scaled_ref[:, lanes(g)] - x * shift)).astype(BF)


def place_kernel(mine_ref, *refs):
    parts, smalls = refs[:GROUPS], refs[GROUPS : 2 * GROUPS]
    gu_ref, gv_ref, go_ref, bfly_ref = refs[2 * GROUPS :]
    for k in range(GROUPS):
        g = (mine_ref[0] + GROUPS - k) & (GROUPS - 1)
        for half in range(2):
            for w, out in enumerate((gu_ref, gv_ref, go_ref)):
                out[g, :, half * 128 : (half + 1) * 128] = (
                    parts[k][:, half, w].astype(F32).reshape(BLK, 128)
                )
            for part in range(3):
                bfly_ref[g, part, half] = smalls[k][2 * part + half].astype(F32)


def call(kernel, outs, scratch=(), flops=0, moved=0, vmem=24, smem_first=False):
    shapes = [jax.ShapeDtypeStruct(shape, dtype) for shape, dtype in outs]
    whole = pl.BlockSpec(memory_space=pltpu.VMEM)

    def run(*args):
        specs = [whole] * len(args)
        if smem_first:
            specs[0] = pl.BlockSpec(memory_space=pltpu.SMEM)
        return pl.pallas_call(
            kernel,
            out_shape=shapes,
            in_specs=specs,
            out_specs=[whole] * len(shapes),
            scratch_shapes=list(scratch),
            compiler_params=pltpu.CompilerParams(vmem_limit_bytes=vmem << 20),
            cost_estimate=pl.CostEstimate(flops=int(flops), bytes_accessed=int(moved), transcendentals=0),
        )(*args)

    return run


def rotated(value, axis):
    n = lax.axis_size(axis)
    return [
        lax.ppermute(value, axis, [(s, (s + k) % n) for s in range(n)]) for k in range(1, n)
    ]


def per_device(tokens, cotangent, gain, w_u, w_v, w_o, local_factor, butterfly):
    x = tokens.reshape(BLK, -1)
    cot = cotangent.reshape(BLK, -1)
    gain2 = gain.reshape(1, -1)
    wide = (BLK, GROUPS * BLK)
    y = lax.axis_index("y")

    send = call(first_kernel, [((8, 4, 2, 3 * PL, BLK), BF)], flops=1.4e8, moved=4e6)(
        x, cot, gain2, local_factor
    )[0]
    recv = lax.all_to_all(send.reshape(BLOCKS, 3 * PL, BLK), SEQ, 0, 0)

    u, act, dgd = call(
        side_kernel, [(wide, BF), (wide, F32), (wide, F32)], flops=4e8, moved=8e6
    )(x, cot, gain2, w_u, w_v, w_o)
    coef = lax.dynamic_index_in_dim(butterfly.reshape(24, GROUPS, BLK), y, 1, keepdims=False)
    mine = [lax.dynamic_index_in_dim(w, y, 0, keepdims=False) for w in (w_u, w_v, w_o)]

    tiled = (BLOCKS, 2, 2, 8, 128)
    back, grads = call(
        mid_kernel,
        [((BLOCKS, 2 * PL, BLK), BF), ((32, 2, 4, 8, 128), BF)],
        scratch=[
            pltpu.VMEM(tiled, F32),
            pltpu.VMEM(tiled, F32),
            pltpu.VMEM(tiled, F32),
            pltpu.VMEM((BLOCKS * PL, BLK), F32),
            pltpu.VMEM((BLOCKS * PL, BLK), F32),
            pltpu.VMEM((24, 2, 8, 128), F32),
            pltpu.VMEM((24, 2, 8, 128), F32),
            pltpu.VMEM((3, BLK, BLK), F32),
        ],
        flops=8e8,
        moved=4e6,
    )(recv, coef, *mine)

    recv2 = lax.all_to_all(back, SEQ, 0, 0).reshape(8, 4, 2, 2 * PL, BLK)

    pieces = lax.all_to_all(grads.reshape(64, 4, 8, 128), SAME_GROUP, 0, 0)
    total = jnp.sum(pieces.astype(F32), axis=0).astype(BF)
    shared = lax.all_to_all(
        jnp.broadcast_to(total[None], (64,) + total.shape), SAME_GROUP, 0, 0
    )
    square = shared[:, :3].reshape(32, 2, 3, 8, 128)
    small = shared[:6, 3]
    squares = [square] + rotated(square, "y")
    smalls = [small] + rotated(small, "y")

    part = call(local_kernel, [((BLK, BLK), BF)], flops=1.3e8, moved=1.2e6)(recv2, u)[0]
    parts = rotated(part, "dp")
    mixed, dx = call(
        last_kernel, [(wide, BF), (wide, BF)], scratch=[pltpu.VMEM(wide, F32)],
        flops=6e8, moved=8e6,
    )(recv2, x, gain2, act, dgd, w_u, w_v, w_o, local_factor)

    dp = lax.axis_index("dp")
    stacked = jnp.stack([part] + parts)
    ordered = [
        lax.dynamic_index_in_dim(stacked, (dp - s) % 4, 0, keepdims=False).astype(F32)
        for s in range(4)
    ]
    grad_local = (ordered[0] + ordered[1]) + (ordered[2] + ordered[3])

    shape = (GROUPS, BLK, BLK)
    gu, gv, go, by_group = call(
        place_kernel,
        [(shape, F32)] * 3 + [((GROUPS, 3, 2, 8, 128), F32)],
        moved=5e6,
        smem_first=True,
    )(y.reshape(1), *squares, *smalls)
    grad_gain = (
        jnp.sum(gu * w_u.astype(F32) + gv * w_v.astype(F32), axis=-1).reshape(-1) / gain
    )
    grad_bfly = by_group.transpose(1, 3, 0, 2, 4).reshape(butterfly.shape)
    return (
        mixed.reshape(tokens.shape),
        dx.reshape(tokens.shape),
        gu,
        gv,
        go,
        grad_gain,
        grad_local,
        grad_bfly,
    )


def solution(mesh):
    fine = Mesh(mesh.devices.reshape(4, 8, 4, 2), ("dp", "z", "y", "c"))
    block = P("dp", SEQ, None)
    return jax.shard_map(
        per_device,
        mesh=fine,
        in_specs=(block, block, P(), P(), P(), P(), P(SEQ, None), P()),
        out_specs=(block, block, P(), P(), P(), P(), P(SEQ, None), P()),
        check_vma=False,
    )
```

```python
import functools

import jax
import jax.numpy as jnp
from jax import lax
from jax.experimental import pallas as pl
from jax.experimental.pallas import tpu as pltpu
from jax.sharding import Mesh, PartitionSpec as P

BF = jnp.bfloat16
F32 = jnp.float32
GROUPS = 4
BLK = 256
BLOCKS = 64
PL = 16
SEQ = ("z", "y", "c")
SAME_GROUP = ("dp", "z", "c")


def dot(a, b, dims):
    return lax.dot_general(a, b, (dims, ((), ())), preferred_element_type=F32)


def mm(a, b):
    return dot(a, b, ((1,), (0,)))


def mm_nt(a, b):
    return dot(a, b, ((1,), (1,)))


def mm_tn(a, b):
    return dot(a, b, ((0,), (0,)))


def lanes(g):
    return slice(g * BLK, (g + 1) * BLK)


def inv_rms(x_ref):
    total = jnp.zeros((BLK, 1), F32)
    for g in range(GROUPS):
        x = x_ref[:, lanes(g)].astype(F32)
        total = total + jnp.sum(x * x, axis=-1, keepdims=True)
    return lax.rsqrt(total * (1.0 / (GROUPS * BLK)) + 1e-06)


def first_kernel(x_hbm, cot_hbm, gain_ref, local_hbm, send_ref, x_ref, cot_ref, local_ref, sems):
    copies = [
        pltpu.make_async_copy(src, dst, sems.at[at])
        for at, (src, dst) in enumerate(
            ((x_hbm, x_ref), (local_hbm, local_ref), (cot_hbm, cot_ref))
        )
    ]
    for copy in copies:
        copy.start()

    def put(g, at, value):
        send_ref[:, g, :, at * PL : (at + 1) * PL, :] = value.reshape(8, 2, PL, BLK)

    copies[0].wait()
    r = inv_rms(x_ref)
    copies[1].wait()
    local = local_ref[...]
    for g in range(GROUPS):
        xn = (x_ref[:, lanes(g)].astype(F32) * r * gain_ref[:, lanes(g)]).astype(BF)
        put(g, 1, xn)
        put(g, 0, mm(local, xn).astype(BF))
    copies[2].wait()
    for g in range(GROUPS):
        put(g, 2, cot_ref[:, lanes(g)])


def side_kernel(x_ref, cot_ref, gain_ref, wu_ref, wv_ref, wo_ref, u_ref, act_ref, dgd_ref):
    r = inv_rms(x_ref)
    for g in range(GROUPS):
        xn = (x_ref[:, lanes(g)].astype(F32) * r * gain_ref[:, lanes(g)]).astype(BF)
        u_ref[:, lanes(g)] = mm(xn, wu_ref[g]).astype(BF)
        v = mm(xn, wv_ref[g])
        sig = jax.nn.sigmoid(v)
        act_ref[:, lanes(g)] = v * sig
        dg = mm_nt(cot_ref[:, lanes(g)], wo_ref[g])
        dgd_ref[:, lanes(g)] = dg * (sig * (1.0 + v * (1.0 - sig)))


def tiles_of(value):
    split = value.reshape(16, 2, 8, BLK)
    return split[..., :128], split[..., 128:]


def from_tiles(ref, at):
    part = ref[pl.ds(at * 16, 16)]
    return jnp.concatenate([part[:, :, 0], part[:, :, 1]], axis=-1).reshape(BLK, BLK)


def mid_kernel(
    place_ref, recv_ref, coef_ref, wu_ref, wv_ref, wo_ref,
    send_ref, keep_ref, give_ref,
    z0, zs, es, act_s, dgd_s, coef, acc, gsum,
):
    for row in range(24):
        for lh in range(2):
            coef[row, lh] = jnp.broadcast_to(
                coef_ref[row : row + 1, lh * 128 : (lh + 1) * 128], (8, 128)
            )
    acc[...] = jnp.zeros_like(acc)
    gsum[...] = jnp.zeros_like(gsum)

    def rows(at, which):
        return recv_ref[pl.ds(at * 16, 16), which * PL : (which + 1) * PL, :].reshape(BLK, BLK)

    @pl.loop(0, 4)
    def _(at):
        here = pl.ds(at * 16, 16)
        p = mm(rows(at, 0), wu_ref[...]).astype(BF).astype(F32)
        v = mm(rows(at, 1), wv_ref[...])
        dg = mm_nt(rows(at, 2), wo_ref[...])
        sig = jax.nn.sigmoid(v)
        act = v * sig
        e = (dg * act).astype(BF).astype(F32)
        act_s[pl.ds(at * BLK, BLK), :] = act
        dgd_s[pl.ds(at * BLK, BLK), :] = dg * (sig * (1.0 + v * (1.0 - sig)))
        for lh, (pt, et) in enumerate(zip(tiles_of(p), tiles_of(e))):
            z0[here, :, lh] = pt
            es[here, :, lh] = et

    def place(t):
        return t >> 2, (t >> 1) & 1, t & 1

    def forward(z, bits, lh):
        states = [z]
        for j, k in enumerate(bits):
            z = [
                coef[4 * k + 2 * (i >> j & 1), lh] * z[i]
                + coef[4 * k + 2 * (i >> j & 1) + 1, lh] * z[i ^ (1 << j)]
                for i in range(8)
            ]
            states.append(z)
        return states

    def backward(e, states, bits, lh):
        for j, k in reversed(tuple(enumerate(bits))):
            z = states[j]
            for b in range(2):
                at = [i for i in range(8) if (i >> j & 1) == b]
                acc[4 * k + 2 * b, lh] += sum(e[i] * z[i] for i in at)
                acc[4 * k + 2 * b + 1, lh] += sum(e[i] * z[i ^ (1 << j)] for i in at)
            e = [
                coef[4 * k + 2 * (i >> j & 1), lh] * e[i]
                + coef[4 * k + 2 * (1 - (i >> j & 1)) + 1, lh] * e[i ^ (1 << j)]
                for i in range(8)
            ]
        return e

    low, high = (0, 1, 2), (3, 4, 5)

    @pl.loop(0, 32)
    def _(t):
        hi, rh, lh = place(t)
        z = forward([z0[hi * 8 + i, rh, lh] for i in range(8)], low, lh)[-1]
        for i in range(8):
            zs[hi * 8 + i, rh, lh] = z[i]

    @pl.loop(0, 32)
    def _(t):
        lo, rh, lh = place(t)
        states = forward([zs[i * 8 + lo, rh, lh] for i in range(8)], high, lh)
        for i in range(8):
            zs[i * 8 + lo, rh, lh] = states[3][i]
        e = backward([es[i * 8 + lo, rh, lh] for i in range(8)], states, high, lh)
        for i in range(8):
            es[i * 8 + lo, rh, lh] = e[i]

    @pl.loop(0, 32)
    def _(t):
        hi, rh, lh = place(t)
        states = forward([z0[hi * 8 + i, rh, lh] for i in range(8)], low, lh)
        e = backward([es[hi * 8 + i, rh, lh] for i in range(8)], states, low, lh)
        for i in range(8):
            es[hi * 8 + i, rh, lh] = e[i]

    @pl.loop(0, 4)
    def _(at):
        here = pl.ds(at * 16, 16)
        z = from_tiles(zs, at).astype(BF)
        e = from_tiles(es, at).astype(BF)
        send_ref[here, :PL, :] = z.reshape(16, PL, BLK)
        send_ref[here, PL:, :] = e.reshape(16, PL, BLK)
        zf = z.astype(F32)
        gated = (zf * act_s[pl.ds(at * BLK, BLK), :]).astype(BF)
        dv = (zf * dgd_s[pl.ds(at * BLK, BLK), :]).astype(BF)
        gsum[0] += mm_tn(rows(at, 0), e)
        gsum[1] += mm_tn(rows(at, 1), dv)
        gsum[2] += mm_tn(gated, rows(at, 2))

    own = place_ref[3]
    for ref, half in ((keep_ref, own), (give_ref, 1 - own)):
        cut = pl.ds(pl.multiple_of(half * 128, 128), 128)
        for w in range(3):
            ref[:, w * 8 : (w + 1) * 8] = (
                gsum[w, :, cut].reshape(4, 8, 8, 128).astype(ref.dtype)
            )
        for part in range(3):
            sums = jnp.sum(acc[part * 8 : (part + 1) * 8, half], axis=1)
            ref[part, 24] = sums.astype(ref.dtype)
        ref[3, 24] = jnp.zeros((8, 128), ref.dtype)


def core_sum_kernel(place_ref, keep_ref, got_ref, own_ref, *give_refs):
    def piece(k):
        d = (place_ref[0] + k) & 3
        return keep_ref[d] + got_ref[d].astype(F32)

    own_ref[...] = piece(0)
    for k, ref in enumerate(give_refs, 1):
        ref[...] = piece(k).astype(BF)


def dp_sum_kernel(own_ref, *refs):
    *got, out_ref = refs
    total = own_ref[...]
    for ref in got:
        total = total + ref[...].astype(F32)
    out_ref[...] = total.astype(BF)


def ordered_sum_kernel(axis, place_ref, *refs):
    *parts, out_ref, held = refs
    n = len(parts)
    for k, ref in enumerate(parts):
        held[(place_ref[axis] + n - k) & (n - 1)] = ref[...]
    total = held[0].astype(F32)
    for at in range(1, n):
        total = total + held[at].astype(F32)
    out_ref[...] = total.astype(out_ref.dtype)


def gather_kernel(place_ref, *refs):
    *parts, out_ref = refs
    for k, ref in enumerate(parts):
        out_ref[(place_ref[0] + 4 - k) & 3] = ref[...]


def group_of(recv_ref, g, which):
    return recv_ref[:, g, :, which * PL : (which + 1) * PL, :].reshape(BLK, BLK)


def local_kernel(recv_ref, u_ref, out_ref):
    total = jnp.zeros((BLK, BLK), F32)
    for g in range(GROUPS):
        total = total + mm_nt(group_of(recv_ref, g, 1), u_ref[:, lanes(g)])
    out_ref[...] = total.astype(BF)


def last_kernel(
    recv_ref, x_ref, gain_ref, act_ref, dgd_ref, wu_ref, wv_ref, wo_ref, local_ref,
    mixed_ref, dx_ref, scaled_ref,
):
    r = inv_rms(x_ref)
    local = local_ref[...]
    inner = jnp.zeros((BLK, 1), F32)
    for g in range(GROUPS):
        z = group_of(recv_ref, g, 0).astype(F32)
        gated = (z * act_ref[:, lanes(g)]).astype(BF)
        mixed_ref[:, lanes(g)] = mm(gated, wo_ref[g]).astype(BF)
        dv = (z * dgd_ref[:, lanes(g)]).astype(BF)
        du = mm_tn(local, group_of(recv_ref, g, 1)).astype(BF)
        scaled = (mm_nt(du, wu_ref[g]) + mm_nt(dv, wv_ref[g])) * gain_ref[:, lanes(g)]
        scaled_ref[:, lanes(g)] = scaled
        inner = inner + jnp.sum(scaled * x_ref[:, lanes(g)].astype(F32), axis=-1, keepdims=True)
    shift = r * r * inner * (1.0 / (GROUPS * BLK))
    for g in range(GROUPS):
        x = x_ref[:, lanes(g)].astype(F32)
        dx_ref[:, lanes(g)] = (r * (scaled_ref[:, lanes(g)] - x * shift)).astype(BF)


def place_kernel(place_ref, wu_ref, wv_ref, gain_ref, *refs):
    own, other = refs[:GROUPS], refs[GROUPS : 2 * GROUPS]
    gu_ref, gv_ref, go_ref, gain_out, bfly_ref = refs[2 * GROUPS :]
    for k in range(GROUPS):
        g = (place_ref[2] + GROUPS - k) & (GROUPS - 1)
        for parts, half in ((own, place_ref[3]), (other, 1 - place_ref[3])):
            cut = pl.ds(pl.multiple_of(half * 128, 128), 128)
            for w, out in enumerate((gu_ref, gv_ref, go_ref)):
                out[g, :, cut] = (
                    parts[k][:, w * 8 : (w + 1) * 8].astype(F32).reshape(BLK, 128)
                )
            wide = pl.ds(pl.multiple_of(g * BLK + half * 128, 128), 128)
            for part in range(3):
                tile = parts[k][part, 24].astype(F32)
                for s in range(8):
                    row = part * 8 + s
                    bfly_ref[row // 4, row // 2 % 2, row % 2 : row % 2 + 1, wide] = tile[s : s + 1]
    ones = jnp.ones((8, BLK), F32)
    for g in range(GROUPS):
        product = gu_ref[g] * wu_ref[g].astype(F32) + gv_ref[g] * wv_ref[g].astype(F32)
        sums = lax.dot_general(
            ones, product, (((1,), (1,)), ((), ())),
            precision=lax.Precision.HIGHEST, preferred_element_type=F32,
        )
        gain_out[:, lanes(g)] = sums[:1] / gain_ref[:, lanes(g)]


def call(kernel, outs, scratch=(), flops=0, moved=0, vmem=24, smem=(), hbm=()):
    shapes = [jax.ShapeDtypeStruct(shape, dtype) for shape, dtype in outs]
    whole = pl.BlockSpec(memory_space=pltpu.VMEM)

    def run(*args):
        specs = [whole] * len(args)
        for at in smem:
            specs[at] = pl.BlockSpec(memory_space=pltpu.SMEM)
        for at in hbm:
            specs[at] = pl.BlockSpec(memory_space=pltpu.HBM)
        return pl.pallas_call(
            kernel,
            out_shape=shapes,
            in_specs=specs,
            out_specs=[whole] * len(shapes),
            scratch_shapes=list(scratch),
            compiler_params=pltpu.CompilerParams(vmem_limit_bytes=vmem << 20),
            cost_estimate=pl.CostEstimate(
                flops=int(flops), bytes_accessed=int(moved), transcendentals=0
            ),
        )(*args)

    return run


def rotated(values, axis):
    n = lax.axis_size(axis)
    if not isinstance(values, (list, tuple)):
        values = [values] * (n - 1)
    return [
        lax.ppermute(value, axis, [(s, (s + k) % n) for s in range(n)])
        for k, value in enumerate(values, 1)
    ]


def swapped(value):
    return lax.ppermute(value, "c", [(0, 1), (1, 0)])


def per_device(tokens, cotangent, gain, w_u, w_v, w_o, local_factor, butterfly):
    x = tokens.reshape(BLK, -1)
    cot = cotangent.reshape(BLK, -1)
    gain2 = gain.reshape(1, -1)
    wide = (BLK, GROUPS * BLK)
    y = lax.axis_index("y")
    place = jnp.stack([lax.axis_index(axis) for axis in ("dp", "z", "y", "c")]).astype(jnp.int32)

    send = call(
        first_kernel,
        [((8, 4, 2, 3 * PL, BLK), BF)],
        scratch=[
            pltpu.VMEM(wide, BF),
            pltpu.VMEM(wide, BF),
            pltpu.VMEM((BLK, BLK), BF),
            pltpu.SemaphoreType.DMA((3,)),
        ],
        flops=1.4e8,
        moved=4e6,
        hbm=(0, 1, 3),
        vmem=58,
    )(x, cot, gain2, local_factor)[0]
    recv = lax.all_to_all(send.reshape(BLOCKS, 3 * PL, BLK), SEQ, 0, 0)

    u, act, dgd = call(
        side_kernel, [(wide, BF), (wide, F32), (wide, F32)], flops=4e8, moved=8e6
    )(x, cot, gain2, w_u, w_v, w_o)
    coef = lax.dynamic_index_in_dim(butterfly.reshape(24, GROUPS, BLK), y, 1, keepdims=False)
    mine = [lax.dynamic_index_in_dim(w, y, 0, keepdims=False) for w in (w_u, w_v, w_o)]

    tiled = (BLOCKS, 2, 2, 8, 128)
    quarter = (25, 8, 128)
    back, keep, give = call(
        mid_kernel,
        [((BLOCKS, 2 * PL, BLK), BF), ((4,) + quarter, F32), ((4,) + quarter, BF)],
        scratch=[
            pltpu.VMEM(tiled, F32),
            pltpu.VMEM(tiled, F32),
            pltpu.VMEM(tiled, F32),
            pltpu.VMEM((BLOCKS * PL, BLK), F32),
            pltpu.VMEM((BLOCKS * PL, BLK), F32),
            pltpu.VMEM((24, 2, 8, 128), F32),
            pltpu.VMEM((24, 2, 8, 128), F32),
            pltpu.VMEM((3, BLK, BLK), F32),
        ],
        flops=8e8,
        moved=4e6,
        smem=(0,),
    )(place, recv, coef, *mine)

    recv2 = lax.all_to_all(back, SEQ, 0, 0).reshape(8, 4, 2, 2 * PL, BLK)

    own, *gives = call(
        core_sum_kernel, [(quarter, F32)] + [(quarter, BF)] * 3, moved=1e6, smem=(0,)
    )(place, keep, swapped(give))
    part_z = call(dp_sum_kernel, [(quarter, BF)], moved=3e5)(own, *rotated(gives, "dp"))[0]
    slice_ = call(
        functools.partial(ordered_sum_kernel, 1),
        [(quarter, BF)],
        scratch=[pltpu.VMEM((8,) + quarter, BF)],
        moved=5e5,
        smem=(0,),
    )(place, part_z, *rotated(part_z, "z"))[0]
    mine_y = call(gather_kernel, [((4,) + quarter, BF)], moved=4e5, smem=(0,))(
        place, slice_, *rotated(slice_, "dp")
    )[0]
    halves = [mine_y] + rotated(mine_y, "y")
    others = [swapped(half) for half in halves]
    shape = (GROUPS, BLK, BLK)
    gu, gv, go, grad_gain, grad_bfly = call(
        place_kernel,
        [(shape, F32)] * 3 + [(gain2.shape, F32), (butterfly.shape, F32)],
        moved=5e6,
        smem=(0,),
    )(place, w_u, w_v, gain2, *halves, *others)

    part = call(local_kernel, [((BLK, BLK), BF)], flops=1.3e8, moved=1.2e6)(recv2, u)[0]
    grad_local = call(
        functools.partial(ordered_sum_kernel, 0),
        [((BLK, BLK), F32)],
        scratch=[pltpu.VMEM((4, BLK, BLK), BF)],
        moved=8e5,
        smem=(0,),
    )(place, part, *rotated(part, "dp"))[0]
    mixed, dx = call(
        last_kernel, [(wide, BF), (wide, BF)], scratch=[pltpu.VMEM(wide, F32)],
        flops=6e8, moved=8e6,
    )(recv2, x, gain2, act, dgd, w_u, w_v, w_o, local_factor)

    return (
        mixed.reshape(tokens.shape),
        dx.reshape(tokens.shape),
        gu,
        gv,
        go,
        grad_gain.reshape(gain.shape),
        grad_local,
        grad_bfly,
    )


def solution(mesh):
    fine = Mesh(mesh.devices.reshape(4, 8, 4, 2), ("dp", "z", "y", "c"))
    block = P("dp", SEQ, None)
    return jax.shard_map(
        per_device,
        mesh=fine,
        in_specs=(block, block, P(), P(), P(), P(), P(SEQ, None), P()),
        out_specs=(block, block, P(), P(), P(), P(), P(SEQ, None), P()),
        check_vma=False,
    )
```

```python
import functools

import jax
import jax.numpy as jnp
from jax import lax
from jax.experimental import pallas as pl
from jax.experimental.pallas import tpu as pltpu
from jax.sharding import Mesh, PartitionSpec as P

BF = jnp.bfloat16
F32 = jnp.float32
GROUPS = 4
BLK = 256
BLOCKS = 64
PL = 16
SEQ = ("z", "y", "c")
SAME_GROUP = ("dp", "z", "c")


def dot(a, b, dims):
    return lax.dot_general(a, b, (dims, ((), ())), preferred_element_type=F32)


def mm(a, b):
    return dot(a, b, ((1,), (0,)))


def mm_nt(a, b):
    return dot(a, b, ((1,), (1,)))


def mm_tn(a, b):
    return dot(a, b, ((0,), (0,)))


def lanes(g):
    return slice(g * BLK, (g + 1) * BLK)


def inv_rms(x_ref):
    total = jnp.zeros((BLK, 1), F32)
    for g in range(GROUPS):
        x = x_ref[:, lanes(g)].astype(F32)
        total = total + jnp.sum(x * x, axis=-1, keepdims=True)
    return lax.rsqrt(total * (1.0 / (GROUPS * BLK)) + 1e-06)


def first_kernel(x_hbm, cot_hbm, gain_ref, local_hbm, send_ref, x_ref, cot_ref, local_ref, sems):
    copies = [
        pltpu.make_async_copy(src, dst, sems.at[at])
        for at, (src, dst) in enumerate(
            ((x_hbm, x_ref), (local_hbm, local_ref), (cot_hbm, cot_ref))
        )
    ]
    for copy in copies:
        copy.start()

    def put(g, at, value):
        send_ref[:, g, :, at * PL : (at + 1) * PL, :] = value.reshape(8, 2, PL, BLK)

    copies[0].wait()
    r = inv_rms(x_ref)
    copies[1].wait()
    local = local_ref[...]
    for g in range(GROUPS):
        xn = (x_ref[:, lanes(g)].astype(F32) * r * gain_ref[:, lanes(g)]).astype(BF)
        put(g, 1, xn)
        put(g, 0, mm(local, xn).astype(BF))
    copies[2].wait()
    for g in range(GROUPS):
        put(g, 2, cot_ref[:, lanes(g)])


def side_kernel(x_ref, cot_ref, gain_ref, wu_ref, wv_ref, wo_ref, u_ref, act_ref, dgd_ref):
    r = inv_rms(x_ref)
    for g in range(GROUPS):
        xn = (x_ref[:, lanes(g)].astype(F32) * r * gain_ref[:, lanes(g)]).astype(BF)
        u_ref[:, lanes(g)] = mm(xn, wu_ref[g]).astype(BF)
        v = mm(xn, wv_ref[g])
        sig = jax.nn.sigmoid(v)
        act_ref[:, lanes(g)] = v * sig
        dg = mm_nt(cot_ref[:, lanes(g)], wo_ref[g])
        dgd_ref[:, lanes(g)] = dg * (sig * (1.0 + v * (1.0 - sig)))


def tiles_of(value):
    split = value.reshape(16, 2, 8, BLK)
    return split[..., :128], split[..., 128:]


def from_tiles(ref, at):
    part = ref[pl.ds(at * 16, 16)]
    return jnp.concatenate([part[:, :, 0], part[:, :, 1]], axis=-1).reshape(BLK, BLK)


def mid_kernel(
    place_ref, recv_hbm, coef_hbm, wu_hbm, wv_hbm, wo_hbm,
    send_hbm, keep_ref, give_ref,
    recv_ref, send_ref, coef_ref, wu_ref, wv_ref, wo_ref,
    z0, zs, es, act_s, dgd_s, coef, acc, gsum, in_sems, out_sems, sems,
):
    group = place_ref[2]

    def fetch(at):
        here = pl.ds(at * 16, 16)
        return pltpu.make_async_copy(recv_hbm.at[here], recv_ref.at[here], in_sems.at[at])

    def deliver(at):
        here = pl.ds(at * 16, 16)
        return pltpu.make_async_copy(send_ref.at[here], send_hbm.at[here], out_sems.at[at])

    mine = pl.ds(pl.multiple_of(group * BLK, BLK), BLK)
    weights = [
        pltpu.make_async_copy(src.at[group], dst, sems.at[at])
        for at, (src, dst) in enumerate(
            ((wu_hbm, wu_ref), (wv_hbm, wv_ref), (wo_hbm, wo_ref))
        )
    ]
    coefs = pltpu.make_async_copy(coef_hbm.at[:, :, :, mine], coef_ref, sems.at[3])
    for copy in (fetch(0), *weights, coefs, fetch(1), fetch(2), fetch(3)):
        copy.start()
    acc[...] = jnp.zeros_like(acc)
    gsum[...] = jnp.zeros_like(gsum)
    coefs.wait()
    for row in range(24):
        for lh in range(2):
            coef[row, lh] = jnp.broadcast_to(
                coef_ref[row // 4, row // 2 % 2, row % 2 : row % 2 + 1, lh * 128 : (lh + 1) * 128],
                (8, 128),
            )
    for copy in weights:
        copy.wait()

    def rows(at, which):
        return recv_ref[pl.ds(at * 16, 16), which * PL : (which + 1) * PL, :].reshape(BLK, BLK)

    @pl.loop(0, 4)
    def _(at):
        fetch(at).wait()
        here = pl.ds(at * 16, 16)
        p = mm(rows(at, 0), wu_ref[...]).astype(BF).astype(F32)
        v = mm(rows(at, 1), wv_ref[...])
        dg = mm_nt(rows(at, 2), wo_ref[...])
        sig = jax.nn.sigmoid(v)
        act = v * sig
        e = (dg * act).astype(BF).astype(F32)
        act_s[pl.ds(at * BLK, BLK), :] = act
        dgd_s[pl.ds(at * BLK, BLK), :] = dg * (sig * (1.0 + v * (1.0 - sig)))
        for lh, (pt, et) in enumerate(zip(tiles_of(p), tiles_of(e))):
            z0[here, :, lh] = pt
            es[here, :, lh] = et

    def place(t):
        return t >> 2, (t >> 1) & 1, t & 1

    def forward(z, bits, lh):
        states = [z]
        for j, k in enumerate(bits):
            z = [
                coef[4 * k + 2 * (i >> j & 1), lh] * z[i]
                + coef[4 * k + 2 * (i >> j & 1) + 1, lh] * z[i ^ (1 << j)]
                for i in range(8)
            ]
            states.append(z)
        return states

    def backward(e, states, bits, lh):
        for j, k in reversed(tuple(enumerate(bits))):
            z = states[j]
            for b in range(2):
                at = [i for i in range(8) if (i >> j & 1) == b]
                acc[4 * k + 2 * b, lh] += sum(e[i] * z[i] for i in at)
                acc[4 * k + 2 * b + 1, lh] += sum(e[i] * z[i ^ (1 << j)] for i in at)
            e = [
                coef[4 * k + 2 * (i >> j & 1), lh] * e[i]
                + coef[4 * k + 2 * (1 - (i >> j & 1)) + 1, lh] * e[i ^ (1 << j)]
                for i in range(8)
            ]
        return e

    low, high = (0, 1, 2), (3, 4, 5)

    @pl.loop(0, 32)
    def _(t):
        hi, rh, lh = place(t)
        z = forward([z0[hi * 8 + i, rh, lh] for i in range(8)], low, lh)[-1]
        for i in range(8):
            zs[hi * 8 + i, rh, lh] = z[i]

    @pl.loop(0, 32)
    def _(t):
        lo, rh, lh = place(t)
        states = forward([zs[i * 8 + lo, rh, lh] for i in range(8)], high, lh)
        for i in range(8):
            zs[i * 8 + lo, rh, lh] = states[3][i]
        e = backward([es[i * 8 + lo, rh, lh] for i in range(8)], states, high, lh)
        for i in range(8):
            es[i * 8 + lo, rh, lh] = e[i]

    @pl.loop(0, 32)
    def _(t):
        hi, rh, lh = place(t)
        states = forward([z0[hi * 8 + i, rh, lh] for i in range(8)], low, lh)
        e = backward([es[hi * 8 + i, rh, lh] for i in range(8)], states, low, lh)
        for i in range(8):
            es[hi * 8 + i, rh, lh] = e[i]

    @pl.loop(0, 4)
    def _(at):
        here = pl.ds(at * 16, 16)
        z = from_tiles(zs, at).astype(BF)
        e = from_tiles(es, at).astype(BF)
        send_ref[here, :PL, :] = z.reshape(16, PL, BLK)
        send_ref[here, PL:, :] = e.reshape(16, PL, BLK)
        deliver(at).start()
        zf = z.astype(F32)
        gated = (zf * act_s[pl.ds(at * BLK, BLK), :]).astype(BF)
        dv = (zf * dgd_s[pl.ds(at * BLK, BLK), :]).astype(BF)
        gsum[0] += mm_tn(rows(at, 0), e)
        gsum[1] += mm_tn(rows(at, 1), dv)
        gsum[2] += mm_tn(gated, rows(at, 2))

    own = place_ref[3]
    for ref, half in ((keep_ref, own), (give_ref, 1 - own)):
        cut = pl.ds(pl.multiple_of(half * 128, 128), 128)
        for w in range(3):
            ref[:, w * 8 : (w + 1) * 8] = (
                gsum[w, :, cut].reshape(4, 8, 8, 128).astype(ref.dtype)
            )
        for part in range(3):
            sums = jnp.sum(acc[part * 8 : (part + 1) * 8, half], axis=1)
            ref[part, 24] = sums.astype(ref.dtype)
        ref[3, 24] = jnp.zeros((8, 128), ref.dtype)
    for at in range(4):
        deliver(at).wait()


def core_sum_kernel(place_ref, keep_ref, got_ref, own_ref, *give_refs):
    def piece(k):
        d = (place_ref[0] + k) & 3
        return keep_ref[d] + got_ref[d].astype(F32)

    own_ref[...] = piece(0)
    for k, ref in enumerate(give_refs, 1):
        ref[...] = piece(k).astype(BF)


def dp_sum_kernel(own_ref, *refs):
    *got, out_ref = refs
    total = own_ref[...]
    for ref in got:
        total = total + ref[...].astype(F32)
    out_ref[...] = total.astype(BF)


def pair_sum_kernel(a_ref, b_ref, out_ref):
    out_ref[...] = (a_ref[...].astype(F32) + b_ref[...].astype(F32)).astype(out_ref.dtype)


def ordered_sum_kernel(place_ref, *refs):
    *parts, out_ref, held = refs
    for k, ref in enumerate(parts):
        held[(place_ref[0] + 4 - k) & 3] = ref[...]
    total = held[0].astype(F32)
    for at in range(1, 4):
        total = total + held[at].astype(F32)
    out_ref[...] = total


def gather_kernel(place_ref, *refs):
    *parts, out_ref = refs
    for k, ref in enumerate(parts):
        out_ref[(place_ref[0] + 4 - k) & 3] = ref[...]


def group_of(recv_ref, g, which):
    return recv_ref[:, g, :, which * PL : (which + 1) * PL, :].reshape(BLK, BLK)


def local_kernel(recv_ref, u_ref, out_ref):
    total = jnp.zeros((BLK, BLK), F32)
    for g in range(GROUPS):
        total = total + mm_nt(group_of(recv_ref, g, 1), u_ref[:, lanes(g)])
    out_ref[...] = total.astype(BF)


def last_kernel(
    recv_ref, x_ref, gain_ref, act_ref, dgd_ref, wu_ref, wv_ref, wo_ref, local_ref,
    mixed_ref, dx_ref, scaled_ref,
):
    r = inv_rms(x_ref)
    local = local_ref[...]
    inner = jnp.zeros((BLK, 1), F32)
    for g in range(GROUPS):
        z = group_of(recv_ref, g, 0).astype(F32)
        gated = (z * act_ref[:, lanes(g)]).astype(BF)
        mixed_ref[:, lanes(g)] = mm(gated, wo_ref[g]).astype(BF)
        dv = (z * dgd_ref[:, lanes(g)]).astype(BF)
        du = mm_tn(local, group_of(recv_ref, g, 1)).astype(BF)
        scaled = (mm_nt(du, wu_ref[g]) + mm_nt(dv, wv_ref[g])) * gain_ref[:, lanes(g)]
        scaled_ref[:, lanes(g)] = scaled
        inner = inner + jnp.sum(scaled * x_ref[:, lanes(g)].astype(F32), axis=-1, keepdims=True)
    shift = r * r * inner * (1.0 / (GROUPS * BLK))
    for g in range(GROUPS):
        x = x_ref[:, lanes(g)].astype(F32)
        dx_ref[:, lanes(g)] = (r * (scaled_ref[:, lanes(g)] - x * shift)).astype(BF)


def place_kernel(place_ref, wu_ref, wv_ref, gain_ref, *refs):
    own, other = refs[:GROUPS], refs[GROUPS : 2 * GROUPS]
    gu_ref, gv_ref, go_ref, gain_out, bfly_ref = refs[2 * GROUPS :]
    for k in range(GROUPS):
        g = (place_ref[2] + GROUPS - k) & (GROUPS - 1)
        for parts, half in ((own, place_ref[3]), (other, 1 - place_ref[3])):
            cut = pl.ds(pl.multiple_of(half * 128, 128), 128)
            for w, out in enumerate((gu_ref, gv_ref, go_ref)):
                out[g, :, cut] = (
                    parts[k][:, w * 8 : (w + 1) * 8].astype(F32).reshape(BLK, 128)
                )
            wide = pl.ds(pl.multiple_of(g * BLK + half * 128, 128), 128)
            for part in range(3):
                tile = parts[k][part, 24].astype(F32)
                for s in range(8):
                    row = part * 8 + s
                    bfly_ref[row // 4, row // 2 % 2, row % 2 : row % 2 + 1, wide] = tile[s : s + 1]
    ones = jnp.ones((8, BLK), F32)
    for g in range(GROUPS):
        product = gu_ref[g] * wu_ref[g].astype(F32) + gv_ref[g] * wv_ref[g].astype(F32)
        sums = lax.dot_general(
            ones, product, (((1,), (1,)), ((), ())),
            precision=lax.Precision.HIGHEST, preferred_element_type=F32,
        )
        gain_out[:, lanes(g)] = sums[:1] / gain_ref[:, lanes(g)]


def call(kernel, outs, scratch=(), flops=0, moved=0, vmem=24, smem=(), hbm=(), hbm_out=(), free=()):
    shapes = [jax.ShapeDtypeStruct(shape, dtype) for shape, dtype in outs]
    whole = pl.BlockSpec(memory_space=pltpu.VMEM)

    def run(*args):
        specs = [whole] * len(args)
        for at in smem:
            specs[at] = pl.BlockSpec(memory_space=pltpu.SMEM)
        for at in hbm:
            specs[at] = pl.BlockSpec(memory_space=pltpu.HBM)
        for at in free:
            specs[at] = pl.BlockSpec(memory_space=pl.ANY)
        return pl.pallas_call(
            kernel,
            out_shape=shapes,
            in_specs=specs,
            out_specs=[
                pl.BlockSpec(memory_space=pltpu.HBM) if at in hbm_out else whole
                for at in range(len(shapes))
            ],
            scratch_shapes=list(scratch),
            compiler_params=pltpu.CompilerParams(vmem_limit_bytes=vmem << 20),
            cost_estimate=pl.CostEstimate(
                flops=int(flops), bytes_accessed=int(moved), transcendentals=0
            ),
        )(*args)

    return run


def rotated(values, axis):
    n = lax.axis_size(axis)
    if not isinstance(values, (list, tuple)):
        values = [values] * (n - 1)
    return [
        lax.ppermute(value, axis, [(s, (s + k) % n) for s in range(n)])
        for k, value in enumerate(values, 1)
    ]


def swapped(value, axis="c", bit=1):
    return lax.ppermute(value, axis, [(s, s ^ bit) for s in range(lax.axis_size(axis))])


def per_device(tokens, cotangent, gain, w_u, w_v, w_o, local_factor, butterfly):
    x = tokens.reshape(BLK, -1)
    cot = cotangent.reshape(BLK, -1)
    gain2 = gain.reshape(1, -1)
    wide = (BLK, GROUPS * BLK)
    place = jnp.stack([lax.axis_index(axis) for axis in ("dp", "z", "y", "c")]).astype(jnp.int32)

    send = call(
        first_kernel,
        [((8, 4, 2, 3 * PL, BLK), BF)],
        scratch=[
            pltpu.VMEM(wide, BF),
            pltpu.VMEM(wide, BF),
            pltpu.VMEM((BLK, BLK), BF),
            pltpu.SemaphoreType.DMA((3,)),
        ],
        flops=1.4e8,
        moved=4e6,
        hbm=(0, 1, 3),
        vmem=58,
    )(x, cot, gain2, local_factor)[0]
    recv = lax.all_to_all(send.reshape(BLOCKS, 3 * PL, BLK), SEQ, 0, 0)

    u, act, dgd = call(
        side_kernel, [(wide, BF), (wide, F32), (wide, F32)], flops=4e8, moved=8e6, vmem=63
    )(x, cot, gain2, w_u, w_v, w_o)
    recv, u, act, dgd = lax.optimization_barrier((recv, u, act, dgd))

    tiled = (BLOCKS, 2, 2, 8, 128)
    quarter = (25, 8, 128)
    back, keep, give = call(
        mid_kernel,
        [((BLOCKS, 2 * PL, BLK), BF), ((4,) + quarter, F32), ((4,) + quarter, BF)],
        scratch=[
            pltpu.VMEM((BLOCKS, 3 * PL, BLK), BF),
            pltpu.VMEM((BLOCKS, 2 * PL, BLK), BF),
            pltpu.VMEM(butterfly.shape[:3] + (BLK,), F32),
            pltpu.VMEM((BLK, BLK), BF),
            pltpu.VMEM((BLK, BLK), BF),
            pltpu.VMEM((BLK, BLK), BF),
            pltpu.VMEM(tiled, F32),
            pltpu.VMEM(tiled, F32),
            pltpu.VMEM(tiled, F32),
            pltpu.VMEM((BLOCKS * PL, BLK), F32),
            pltpu.VMEM((BLOCKS * PL, BLK), F32),
            pltpu.VMEM((24, 2, 8, 128), F32),
            pltpu.VMEM((24, 2, 8, 128), F32),
            pltpu.VMEM((3, BLK, BLK), F32),
            pltpu.SemaphoreType.DMA((4,)),
            pltpu.SemaphoreType.DMA((4,)),
            pltpu.SemaphoreType.DMA((4,)),
        ],
        flops=8e8,
        moved=4e6,
        vmem=63,
        smem=(0,),
        hbm=(2, 3, 4, 5),
        free=(1,),
        hbm_out=(0,),
    )(place, recv, butterfly, w_u, w_v, w_o)

    recv2 = lax.all_to_all(back, SEQ, 0, 0).reshape(8, 4, 2, 2 * PL, BLK)

    own, *gives = call(
        core_sum_kernel, [(quarter, F32)] + [(quarter, BF)] * 3, moved=1e6, smem=(0,)
    )(place, keep, swapped(give))
    slice_ = call(dp_sum_kernel, [(quarter, BF)], moved=3e5)(own, *rotated(gives, "dp"))[0]
    for bit in (1, 2, 4):
        slice_ = call(pair_sum_kernel, [(quarter, BF)], moved=2e5)(
            slice_, swapped(slice_, "z", bit)
        )[0]
    mine_y = call(gather_kernel, [((4,) + quarter, BF)], moved=4e5, smem=(0,))(
        place, slice_, *rotated(slice_, "dp")
    )[0]
    part = call(local_kernel, [((BLK, BLK), BF)], flops=1.3e8, moved=1.2e6)(recv2, u)[0]
    mine_y, part = lax.optimization_barrier((mine_y, part))
    halves = [mine_y] + rotated(mine_y, "y")
    others = [swapped(half) for half in halves]

    mixed, dx = call(
        last_kernel, [(wide, BF), (wide, BF)], scratch=[pltpu.VMEM(wide, F32)],
        flops=6e8, moved=8e6,
    )(recv2, x, gain2, act, dgd, w_u, w_v, w_o, local_factor)
    grad_local = call(
        ordered_sum_kernel,
        [((BLK, BLK), F32)],
        scratch=[pltpu.VMEM((4, BLK, BLK), BF)],
        moved=8e5,
        smem=(0,),
    )(place, part, *rotated(part, "dp"))[0]
    mixed, dx, grad_local, others = lax.optimization_barrier((mixed, dx, grad_local, others))

    shape = (GROUPS, BLK, BLK)
    gu, gv, go, grad_gain, grad_bfly = call(
        place_kernel,
        [(shape, F32)] * 3 + [(gain2.shape, F32), (butterfly.shape, F32)],
        moved=5e6,
        smem=(0,),
    )(place, w_u, w_v, gain2, *halves, *others)

    return (
        mixed.reshape(tokens.shape),
        dx.reshape(tokens.shape),
        gu,
        gv,
        go,
        grad_gain.reshape(gain.shape),
        grad_local,
        grad_bfly,
    )


def solution(mesh):
    fine = Mesh(mesh.devices.reshape(4, 8, 4, 2), ("dp", "z", "y", "c"))
    block = P("dp", SEQ, None)
    return jax.shard_map(
        per_device,
        mesh=fine,
        in_specs=(block, block, P(), P(), P(), P(), P(SEQ, None), P()),
        out_specs=(block, block, P(), P(), P(), P(), P(SEQ, None), P()),
        check_vma=False,
    )
```

```python
import functools

import jax
import jax.numpy as jnp
from jax import lax
from jax.experimental import pallas as pl
from jax.experimental.pallas import tpu as pltpu
from jax.sharding import Mesh, PartitionSpec as P

BF = jnp.bfloat16
F32 = jnp.float32
GROUPS = 4
BLK = 256
BLOCKS = 64
PL = 16
SEQ = ("z", "y", "c")


def dot(a, b, dims):
    return lax.dot_general(a, b, (dims, ((), ())), preferred_element_type=F32)


def mm(a, b):
    return dot(a, b, ((1,), (0,)))


def mm_nt(a, b):
    return dot(a, b, ((1,), (1,)))


def mm_tn(a, b):
    return dot(a, b, ((0,), (0,)))


def lanes(g):
    return slice(g * BLK, (g + 1) * BLK)


def inv_rms(x_ref):
    total = jnp.zeros((BLK, 1), F32)
    for g in range(GROUPS):
        x = x_ref[:, lanes(g)].astype(F32)
        total = total + jnp.sum(x * x, axis=-1, keepdims=True)
    return lax.rsqrt(total * (1.0 / (GROUPS * BLK)) + 1e-06)


def first_kernel(x_hbm, cot_hbm, gain_ref, local_hbm, send_ref, x_ref, cot_ref, local_ref, sems):
    copies = [
        pltpu.make_async_copy(src, dst, sems.at[at])
        for at, (src, dst) in enumerate(
            ((x_hbm, x_ref), (local_hbm, local_ref), (cot_hbm, cot_ref))
        )
    ]
    for copy in copies:
        copy.start()

    def put(g, at, value):
        send_ref[g, :, at * PL : (at + 1) * PL, :] = value.reshape(16, PL, BLK)

    copies[0].wait()
    r = inv_rms(x_ref)
    copies[1].wait()
    local = local_ref[...]
    for g in range(GROUPS):
        xn = (x_ref[:, lanes(g)].astype(F32) * r * gain_ref[:, lanes(g)]).astype(BF)
        put(g, 1, xn)
        put(g, 0, mm(local, xn).astype(BF))
    copies[2].wait()
    for g in range(GROUPS):
        put(g, 2, cot_ref[:, lanes(g)])


def side_kernel(x_ref, cot_ref, gain_ref, wu_ref, wv_ref, wo_ref, u_ref, act_ref, dgd_ref):
    r = inv_rms(x_ref)
    for g in range(GROUPS):
        xn = (x_ref[:, lanes(g)].astype(F32) * r * gain_ref[:, lanes(g)]).astype(BF)
        u_ref[:, lanes(g)] = mm(xn, wu_ref[g]).astype(BF)
        v = mm(xn, wv_ref[g])
        sig = jax.nn.sigmoid(v)
        act_ref[:, lanes(g)] = v * sig
        dg = mm_nt(cot_ref[:, lanes(g)], wo_ref[g])
        dgd_ref[:, lanes(g)] = dg * (sig * (1.0 + v * (1.0 - sig)))


def tiles_of(value):
    split = value.reshape(16, 2, 8, BLK)
    return split[..., :128], split[..., 128:]


def from_tiles(ref, at):
    part = ref[pl.ds(at * 16, 16)]
    return jnp.concatenate([part[:, :, 0], part[:, :, 1]], axis=-1).reshape(BLK, BLK)


def mid_kernel(
    place_ref, recv_hbm, coef_hbm, wu_hbm, wv_hbm, wo_hbm,
    send_hbm, keep_ref, give_ref,
    recv_ref, send_ref, coef_ref, wu_ref, wv_ref, wo_ref,
    z0, zs, es, act_s, dgd_s, coef, acc, gsum, in_sems, out_sems, sems,
):
    group = place_ref[1]

    def fetch(at):
        here = pl.ds(at * 16, 16)
        return pltpu.make_async_copy(recv_hbm.at[here], recv_ref.at[here], in_sems.at[at])

    def deliver(at):
        here = pl.ds(at * 16, 16)
        return pltpu.make_async_copy(send_ref.at[here], send_hbm.at[here], out_sems.at[at])

    mine = pl.ds(pl.multiple_of(group * BLK, BLK), BLK)
    weights = [
        pltpu.make_async_copy(src.at[group], dst, sems.at[at])
        for at, (src, dst) in enumerate(
            ((wu_hbm, wu_ref), (wv_hbm, wv_ref), (wo_hbm, wo_ref))
        )
    ]
    coefs = pltpu.make_async_copy(coef_hbm.at[:, :, :, mine], coef_ref, sems.at[3])
    for copy in (fetch(0), *weights, coefs, fetch(1), fetch(2), fetch(3)):
        copy.start()
    acc[...] = jnp.zeros_like(acc)
    gsum[...] = jnp.zeros_like(gsum)
    coefs.wait()
    for row in range(24):
        for lh in range(2):
            coef[row, lh] = jnp.broadcast_to(
                coef_ref[row // 4, row // 2 % 2, row % 2 : row % 2 + 1, lh * 128 : (lh + 1) * 128],
                (8, 128),
            )
    for copy in weights:
        copy.wait()

    def rows(at, which):
        return recv_ref[pl.ds(at * 16, 16), which * PL : (which + 1) * PL, :].reshape(BLK, BLK)

    @pl.loop(0, 4)
    def _(at):
        fetch(at).wait()
        here = pl.ds(at * 16, 16)
        p = mm(rows(at, 0), wu_ref[...]).astype(BF).astype(F32)
        v = mm(rows(at, 1), wv_ref[...])
        dg = mm_nt(rows(at, 2), wo_ref[...])
        sig = jax.nn.sigmoid(v)
        act = v * sig
        e = (dg * act).astype(BF).astype(F32)
        act_s[pl.ds(at * BLK, BLK), :] = act
        dgd_s[pl.ds(at * BLK, BLK), :] = dg * (sig * (1.0 + v * (1.0 - sig)))
        for lh, (pt, et) in enumerate(zip(tiles_of(p), tiles_of(e))):
            z0[here, :, lh] = pt
            es[here, :, lh] = et

    def place(t):
        return t >> 2, (t >> 1) & 1, t & 1

    def forward(z, bits, lh):
        states = [z]
        for j, k in enumerate(bits):
            z = [
                coef[4 * k + 2 * (i >> j & 1), lh] * z[i]
                + coef[4 * k + 2 * (i >> j & 1) + 1, lh] * z[i ^ (1 << j)]
                for i in range(8)
            ]
            states.append(z)
        return states

    def backward(e, states, bits, lh):
        for j, k in reversed(tuple(enumerate(bits))):
            z = states[j]
            for b in range(2):
                at = [i for i in range(8) if (i >> j & 1) == b]
                acc[4 * k + 2 * b, lh] += sum(e[i] * z[i] for i in at)
                acc[4 * k + 2 * b + 1, lh] += sum(e[i] * z[i ^ (1 << j)] for i in at)
            e = [
                coef[4 * k + 2 * (i >> j & 1), lh] * e[i]
                + coef[4 * k + 2 * (1 - (i >> j & 1)) + 1, lh] * e[i ^ (1 << j)]
                for i in range(8)
            ]
        return e

    low, high = (0, 1, 2), (3, 4, 5)

    @pl.loop(0, 32)
    def _(t):
        hi, rh, lh = place(t)
        z = forward([z0[hi * 8 + i, rh, lh] for i in range(8)], low, lh)[-1]
        for i in range(8):
            zs[hi * 8 + i, rh, lh] = z[i]

    @pl.loop(0, 32)
    def _(t):
        lo, rh, lh = place(t)
        states = forward([zs[i * 8 + lo, rh, lh] for i in range(8)], high, lh)
        for i in range(8):
            zs[i * 8 + lo, rh, lh] = states[3][i]
        e = backward([es[i * 8 + lo, rh, lh] for i in range(8)], states, high, lh)
        for i in range(8):
            es[i * 8 + lo, rh, lh] = e[i]

    @pl.loop(0, 32)
    def _(t):
        hi, rh, lh = place(t)
        states = forward([z0[hi * 8 + i, rh, lh] for i in range(8)], low, lh)
        e = backward([es[hi * 8 + i, rh, lh] for i in range(8)], states, low, lh)
        for i in range(8):
            es[hi * 8 + i, rh, lh] = e[i]

    @pl.loop(0, 4)
    def _(at):
        here = pl.ds(at * 16, 16)
        z = from_tiles(zs, at).astype(BF)
        e = from_tiles(es, at).astype(BF)
        send_ref[here, :PL, :] = z.reshape(16, PL, BLK)
        send_ref[here, PL:, :] = e.reshape(16, PL, BLK)
        deliver(at).start()
        zf = z.astype(F32)
        gated = (zf * act_s[pl.ds(at * BLK, BLK), :]).astype(BF)
        dv = (zf * dgd_s[pl.ds(at * BLK, BLK), :]).astype(BF)
        gsum[0] += mm_tn(rows(at, 0), e)
        gsum[1] += mm_tn(rows(at, 1), dv)
        gsum[2] += mm_tn(gated, rows(at, 2))

    own = place_ref[2]
    for ref, half in ((keep_ref, own), (give_ref, 1 - own)):
        cut = pl.ds(pl.multiple_of(half * 128, 128), 128)
        for w in range(3):
            ref[:, w * 8 : (w + 1) * 8] = (
                gsum[w, :, cut].reshape(4, 8, 8, 128).astype(ref.dtype)
            )
        for part in range(3):
            sums = jnp.sum(acc[part * 8 : (part + 1) * 8, half], axis=1)
            ref[part, 24] = sums.astype(ref.dtype)
        ref[3, 24] = jnp.zeros((8, 128), ref.dtype)
    for at in range(4):
        deliver(at).wait()


def core_sum_kernel(place_ref, keep_ref, got_ref, own_ref, *give_refs):
    def piece(k):
        d = (place_ref[0] + k) & 3
        return keep_ref[d] + got_ref[d].astype(F32)

    own_ref[...] = piece(0)
    for k, ref in enumerate(give_refs, 1):
        ref[...] = piece(k).astype(BF)


def dp_sum_kernel(own_ref, *refs):
    *got, out_ref = refs
    total = own_ref[...]
    for ref in got:
        total = total + ref[...].astype(F32)
    out_ref[...] = total.astype(BF)


def pair_sum_kernel(a_ref, b_ref, out_ref):
    out_ref[...] = (a_ref[...].astype(F32) + b_ref[...].astype(F32)).astype(out_ref.dtype)


def ordered_sum_kernel(place_ref, *refs):
    *parts, out_ref, held = refs
    for k, ref in enumerate(parts):
        held[(place_ref[0] + 4 - k) & 3] = ref[...]
    total = held[0].astype(F32)
    for at in range(1, 4):
        total = total + held[at].astype(F32)
    out_ref[...] = total


def gather_kernel(place_ref, *refs):
    *parts, out_ref = refs
    for k, ref in enumerate(parts):
        out_ref[(place_ref[1] + 4 - k) & 3] = ref[...]


def group_of(recv_ref, g, which):
    return recv_ref[g, :, which * PL : (which + 1) * PL, :].reshape(BLK, BLK)


def local_kernel(recv_ref, u_ref, out_ref):
    total = jnp.zeros((BLK, BLK), F32)
    for g in range(GROUPS):
        total = total + mm_nt(group_of(recv_ref, g, 1), u_ref[:, lanes(g)])
    out_ref[...] = total.astype(BF)


def last_kernel(
    recv_ref, x_ref, gain_ref, act_ref, dgd_ref, wu_ref, wv_ref, wo_ref, local_ref,
    mixed_ref, dx_ref, scaled_ref,
):
    r = inv_rms(x_ref)
    local = local_ref[...]
    inner = jnp.zeros((BLK, 1), F32)
    for g in range(GROUPS):
        z = group_of(recv_ref, g, 0).astype(F32)
        gated = (z * act_ref[:, lanes(g)]).astype(BF)
        mixed_ref[:, lanes(g)] = mm(gated, wo_ref[g]).astype(BF)
        dv = (z * dgd_ref[:, lanes(g)]).astype(BF)
        du = mm_tn(local, group_of(recv_ref, g, 1)).astype(BF)
        scaled = (mm_nt(du, wu_ref[g]) + mm_nt(dv, wv_ref[g])) * gain_ref[:, lanes(g)]
        scaled_ref[:, lanes(g)] = scaled
        inner = inner + jnp.sum(scaled * x_ref[:, lanes(g)].astype(F32), axis=-1, keepdims=True)
    shift = r * r * inner * (1.0 / (GROUPS * BLK))
    for g in range(GROUPS):
        x = x_ref[:, lanes(g)].astype(F32)
        dx_ref[:, lanes(g)] = (r * (scaled_ref[:, lanes(g)] - x * shift)).astype(BF)


def place_kernel(place_ref, wu_ref, wv_ref, gain_ref, *refs):
    own, other = refs[:4], refs[4:8]
    gu_ref, gv_ref, go_ref, gain_out, bfly_ref = refs[8:]
    for k in range(4):
        d = (place_ref[0] + 4 - k) & 3
        rows = pl.ds(pl.multiple_of(d * 64, 64), 64)
        for parts, half in ((own, place_ref[2]), (other, 1 - place_ref[2])):
            cut = pl.ds(pl.multiple_of(half * 128, 128), 128)
            for w, out in enumerate((gu_ref, gv_ref, go_ref)):
                out[:, rows, cut] = (
                    parts[k][:, w * 8 : (w + 1) * 8].astype(F32).reshape(GROUPS, 64, 128)
                )

            @pl.when(d < 3)
            def _():
                for g in range(GROUPS):
                    wide = pl.ds(pl.multiple_of(g * BLK + half * 128, 128), 128)
                    tile = parts[k][g, 24].astype(F32)
                    for s in range(8):
                        bfly_ref[2 * d + s // 4, s // 2 % 2, s % 2 : s % 2 + 1, wide] = (
                            tile[s : s + 1]
                        )

    ones = jnp.ones((8, BLK), F32)
    for g in range(GROUPS):
        product = gu_ref[g] * wu_ref[g].astype(F32) + gv_ref[g] * wv_ref[g].astype(F32)
        sums = lax.dot_general(
            ones, product, (((1,), (1,)), ((), ())),
            precision=lax.Precision.HIGHEST, preferred_element_type=F32,
        )
        gain_out[:, lanes(g)] = sums[:1] / gain_ref[:, lanes(g)]


def call(kernel, outs, scratch=(), flops=0, moved=0, vmem=24, smem=(), hbm=(), hbm_out=(), free=()):
    shapes = [jax.ShapeDtypeStruct(shape, dtype) for shape, dtype in outs]
    whole = pl.BlockSpec(memory_space=pltpu.VMEM)

    def run(*args):
        specs = [whole] * len(args)
        for at in smem:
            specs[at] = pl.BlockSpec(memory_space=pltpu.SMEM)
        for at in hbm:
            specs[at] = pl.BlockSpec(memory_space=pltpu.HBM)
        for at in free:
            specs[at] = pl.BlockSpec(memory_space=pl.ANY)
        return pl.pallas_call(
            kernel,
            out_shape=shapes,
            in_specs=specs,
            out_specs=[
                pl.BlockSpec(memory_space=pltpu.HBM) if at in hbm_out else whole
                for at in range(len(shapes))
            ],
            scratch_shapes=list(scratch),
            compiler_params=pltpu.CompilerParams(vmem_limit_bytes=vmem << 20),
            cost_estimate=pl.CostEstimate(
                flops=int(flops), bytes_accessed=int(moved), transcendentals=0
            ),
        )(*args)

    return run


def rotated(values, axis, step=1):
    n = lax.axis_size(axis)
    if not isinstance(values, (list, tuple)):
        values = [values] * (n // step - 1)
    return [
        lax.ppermute(value, axis, [(s, (s + k * step) % n) for s in range(n)])
        for k, value in enumerate(values, 1)
    ]


def swapped(value, axis="c", bit=1):
    return lax.ppermute(value, axis, [(s, s ^ bit) for s in range(lax.axis_size(axis))])


def per_device(tokens, cotangent, gain, w_u, w_v, w_o, local_factor, butterfly):
    x = tokens.reshape(BLK, -1)
    cot = cotangent.reshape(BLK, -1)
    gain2 = gain.reshape(1, -1)
    wide = (BLK, GROUPS * BLK)
    place = jnp.stack(
        [lax.axis_index("dp"), lax.axis_index("z") >> 1, lax.axis_index("c")]
    ).astype(jnp.int32)

    send = call(
        first_kernel,
        [((GROUPS, 16, 3 * PL, BLK), BF)],
        scratch=[
            pltpu.VMEM(wide, BF),
            pltpu.VMEM(wide, BF),
            pltpu.VMEM((BLK, BLK), BF),
            pltpu.SemaphoreType.DMA((3,)),
        ],
        flops=1.4e8,
        moved=4e6,
        hbm=(0, 1, 3),
        vmem=58,
    )(x, cot, gain2, local_factor)[0]
    recv = lax.all_to_all(send.reshape(BLOCKS, 3 * PL, BLK), SEQ, 0, 0)

    u, act, dgd = call(
        side_kernel, [(wide, BF), (wide, F32), (wide, F32)], flops=4e8, moved=8e6, vmem=63
    )(x, cot, gain2, w_u, w_v, w_o)
    recv, u, act, dgd = lax.optimization_barrier((recv, u, act, dgd))

    tiled = (BLOCKS, 2, 2, 8, 128)
    quarter = (25, 8, 128)
    back, keep, give = call(
        mid_kernel,
        [((BLOCKS, 2 * PL, BLK), BF), ((4,) + quarter, F32), ((4,) + quarter, BF)],
        scratch=[
            pltpu.VMEM((BLOCKS, 3 * PL, BLK), BF),
            pltpu.VMEM((BLOCKS, 2 * PL, BLK), BF),
            pltpu.VMEM(butterfly.shape[:3] + (BLK,), F32),
            pltpu.VMEM((BLK, BLK), BF),
            pltpu.VMEM((BLK, BLK), BF),
            pltpu.VMEM((BLK, BLK), BF),
            pltpu.VMEM(tiled, F32),
            pltpu.VMEM(tiled, F32),
            pltpu.VMEM(tiled, F32),
            pltpu.VMEM((BLOCKS * PL, BLK), F32),
            pltpu.VMEM((BLOCKS * PL, BLK), F32),
            pltpu.VMEM((24, 2, 8, 128), F32),
            pltpu.VMEM((24, 2, 8, 128), F32),
            pltpu.VMEM((3, BLK, BLK), F32),
            pltpu.SemaphoreType.DMA((4,)),
            pltpu.SemaphoreType.DMA((4,)),
            pltpu.SemaphoreType.DMA((4,)),
        ],
        flops=8e8,
        moved=4e6,
        vmem=63,
        smem=(0,),
        hbm=(2, 3, 4, 5),
        free=(1,),
        hbm_out=(0,),
    )(place, recv, butterfly, w_u, w_v, w_o)

    recv2 = lax.all_to_all(back, SEQ, 0, 0).reshape(GROUPS, 16, 2 * PL, BLK)

    own, *gives = call(
        core_sum_kernel, [(quarter, F32)] + [(quarter, BF)] * 3, moved=1e6, smem=(0,)
    )(place, keep, swapped(give))
    slice_ = call(dp_sum_kernel, [(quarter, BF)], moved=3e5)(own, *rotated(gives, "dp"))[0]
    for axis, bit in (("y", 1), ("y", 2), ("z", 1)):
        slice_ = call(pair_sum_kernel, [(quarter, BF)], moved=2e5)(
            slice_, swapped(slice_, axis, bit)
        )[0]
    part = call(local_kernel, [((BLK, BLK), BF)], flops=1.3e8, moved=1.2e6)(recv2, u)[0]
    slice_, part = lax.optimization_barrier((slice_, part))
    mine_d = call(gather_kernel, [((4,) + quarter, BF)], moved=4e5, smem=(0,))(
        place, slice_, *rotated(slice_, "z", 2)
    )[0]
    halves = [mine_d] + rotated(mine_d, "dp")
    others = [swapped(half) for half in halves]

    mixed, dx = call(
        last_kernel, [(wide, BF), (wide, BF)], scratch=[pltpu.VMEM(wide, F32)],
        flops=6e8, moved=8e6,
    )(recv2, x, gain2, act, dgd, w_u, w_v, w_o, local_factor)
    grad_local = call(
        ordered_sum_kernel,
        [((BLK, BLK), F32)],
        scratch=[pltpu.VMEM((4, BLK, BLK), BF)],
        moved=8e5,
        smem=(0,),
    )(place, part, *rotated(part, "dp"))[0]
    mixed, dx, grad_local, others = lax.optimization_barrier((mixed, dx, grad_local, others))

    shape = (GROUPS, BLK, BLK)
    gu, gv, go, grad_gain, grad_bfly = call(
        place_kernel,
        [(shape, F32)] * 3 + [(gain2.shape, F32), (butterfly.shape, F32)],
        moved=5e6,
        smem=(0,),
    )(place, w_u, w_v, gain2, *halves, *others)

    return (
        mixed.reshape(tokens.shape),
        dx.reshape(tokens.shape),
        gu,
        gv,
        go,
        grad_gain.reshape(gain.shape),
        grad_local,
        grad_bfly,
    )


def solution(mesh):
    fine = Mesh(mesh.devices.reshape(4, 8, 4, 2), ("dp", "z", "y", "c"))
    block = P("dp", SEQ, None)
    return jax.shard_map(
        per_device,
        mesh=fine,
        in_specs=(block, block, P(), P(), P(), P(), P(SEQ, None), P()),
        out_specs=(block, block, P(), P(), P(), P(), P(SEQ, None), P()),
        check_vma=False,
    )
```

```python
import functools

import jax
import jax.numpy as jnp
from jax import lax
from jax.experimental import pallas as pl
from jax.experimental.pallas import tpu as pltpu
from jax.sharding import Mesh, PartitionSpec as P

BF = jnp.bfloat16
F32 = jnp.float32
GROUPS = 4
BLK = 256
BLOCKS = 64
PL = 16
SEQ = ("z", "y", "c")


def dot(a, b, dims):
    return lax.dot_general(a, b, (dims, ((), ())), preferred_element_type=F32)


def mm(a, b):
    return dot(a, b, ((1,), (0,)))


def mm_nt(a, b):
    return dot(a, b, ((1,), (1,)))


def mm_tn(a, b):
    return dot(a, b, ((0,), (0,)))


def lanes(g):
    return slice(g * BLK, (g + 1) * BLK)


def inv_rms(x_ref):
    total = jnp.zeros((BLK, 1), F32)
    for g in range(GROUPS):
        x = x_ref[:, lanes(g)].astype(F32)
        total = total + jnp.sum(x * x, axis=-1, keepdims=True)
    return lax.rsqrt(total * (1.0 / (GROUPS * BLK)) + 1e-06)


def first_kernel(x_hbm, cot_hbm, gain_ref, local_hbm, send_ref, x_ref, cot_ref, local_ref, sems):
    copies = [
        pltpu.make_async_copy(src, dst, sems.at[at])
        for at, (src, dst) in enumerate(
            ((x_hbm, x_ref), (local_hbm, local_ref), (cot_hbm, cot_ref))
        )
    ]
    for copy in copies:
        copy.start()

    def put(g, at, value):
        send_ref[g, :, at * PL : (at + 1) * PL, :] = value.reshape(16, PL, BLK)

    copies[0].wait()
    r = inv_rms(x_ref)
    copies[1].wait()
    local = local_ref[...]
    for g in range(GROUPS):
        xn = (x_ref[:, lanes(g)].astype(F32) * r * gain_ref[:, lanes(g)]).astype(BF)
        put(g, 1, xn)
        put(g, 0, mm(local, xn).astype(BF))
    copies[2].wait()
    for g in range(GROUPS):
        put(g, 2, cot_ref[:, lanes(g)])


def side_kernel(x_ref, cot_ref, gain_ref, wu_ref, wv_ref, wo_ref, u_ref, act_ref, dgd_ref):
    r = inv_rms(x_ref)
    for g in range(GROUPS):
        xn = (x_ref[:, lanes(g)].astype(F32) * r * gain_ref[:, lanes(g)]).astype(BF)
        u_ref[:, lanes(g)] = mm(xn, wu_ref[g]).astype(BF)
        v = mm(xn, wv_ref[g])
        sig = jax.nn.sigmoid(v)
        act_ref[:, lanes(g)] = v * sig
        dg = mm_nt(cot_ref[:, lanes(g)], wo_ref[g])
        dgd_ref[:, lanes(g)] = dg * (sig * (1.0 + v * (1.0 - sig)))


def tiles_of(value):
    split = value.reshape(16, 2, 8, BLK)
    return split[..., :128], split[..., 128:]


def from_tiles(ref, at):
    part = ref[pl.ds(at * 16, 16)]
    return jnp.concatenate([part[:, :, 0], part[:, :, 1]], axis=-1).reshape(BLK, BLK)


def mid_kernel(
    place_ref, recv_hbm, coef_hbm, wu_hbm, wv_hbm, wo_hbm,
    send_hbm, keep_ref, give_ref,
    recv_ref, send_ref, coef_ref, wu_ref, wv_ref, wo_ref,
    z0, zs, es, act_s, dgd_s, coef, acc, gsum, in_sems, out_sems, sems,
):
    group = place_ref[1]

    def fetch(at):
        here = pl.ds(at * 16, 16)
        return pltpu.make_async_copy(recv_hbm.at[here], recv_ref.at[here], in_sems.at[at])

    def deliver(at):
        here = pl.ds(at * 16, 16)
        return pltpu.make_async_copy(send_ref.at[here], send_hbm.at[here], out_sems.at[at])

    mine = pl.ds(pl.multiple_of(group * BLK, BLK), BLK)
    weights = [
        pltpu.make_async_copy(src.at[group], dst, sems.at[at])
        for at, (src, dst) in enumerate(
            ((wu_hbm, wu_ref), (wv_hbm, wv_ref), (wo_hbm, wo_ref))
        )
    ]
    coefs = pltpu.make_async_copy(coef_hbm.at[:, :, :, mine], coef_ref, sems.at[3])
    for copy in (fetch(0), *weights, coefs, fetch(1), fetch(2), fetch(3)):
        copy.start()
    acc[...] = jnp.zeros_like(acc)
    gsum[...] = jnp.zeros_like(gsum)
    coefs.wait()
    for row in range(24):
        for lh in range(2):
            coef[row, lh] = jnp.broadcast_to(
                coef_ref[row // 4, row // 2 % 2, row % 2 : row % 2 + 1, lh * 128 : (lh + 1) * 128],
                (8, 128),
            )
    for copy in weights:
        copy.wait()

    def rows(at, which):
        return recv_ref[pl.ds(at * 16, 16), which * PL : (which + 1) * PL, :].reshape(BLK, BLK)

    @pl.loop(0, 4)
    def _(at):
        fetch(at).wait()
        here = pl.ds(at * 16, 16)
        p = mm(rows(at, 0), wu_ref[...]).astype(BF).astype(F32)
        v = mm(rows(at, 1), wv_ref[...])
        dg = mm_nt(rows(at, 2), wo_ref[...])
        sig = jax.nn.sigmoid(v)
        act = v * sig
        e = (dg * act).astype(BF).astype(F32)
        act_s[pl.ds(at * BLK, BLK), :] = act
        dgd_s[pl.ds(at * BLK, BLK), :] = dg * (sig * (1.0 + v * (1.0 - sig)))
        for lh, (pt, et) in enumerate(zip(tiles_of(p), tiles_of(e))):
            z0[here, :, lh] = pt
            es[here, :, lh] = et

    def place(t):
        return t >> 2, (t >> 1) & 1, t & 1

    def forward(z, bits, lh):
        states = [z]
        for j, k in enumerate(bits):
            z = [
                coef[4 * k + 2 * (i >> j & 1), lh] * z[i]
                + coef[4 * k + 2 * (i >> j & 1) + 1, lh] * z[i ^ (1 << j)]
                for i in range(8)
            ]
            states.append(z)
        return states

    def backward(e, states, bits, lh):
        for j, k in reversed(tuple(enumerate(bits))):
            z = states[j]
            for b in range(2):
                at = [i for i in range(8) if (i >> j & 1) == b]
                acc[4 * k + 2 * b, lh] += sum(e[i] * z[i] for i in at)
                acc[4 * k + 2 * b + 1, lh] += sum(e[i] * z[i ^ (1 << j)] for i in at)
            e = [
                coef[4 * k + 2 * (i >> j & 1), lh] * e[i]
                + coef[4 * k + 2 * (1 - (i >> j & 1)) + 1, lh] * e[i ^ (1 << j)]
                for i in range(8)
            ]
        return e

    low, high = (0, 1, 2), (3, 4, 5)

    @pl.loop(0, 32)
    def _(t):
        hi, rh, lh = place(t)
        z = forward([z0[hi * 8 + i, rh, lh] for i in range(8)], low, lh)[-1]
        for i in range(8):
            zs[hi * 8 + i, rh, lh] = z[i]

    @pl.loop(0, 32)
    def _(t):
        lo, rh, lh = place(t)
        states = forward([zs[i * 8 + lo, rh, lh] for i in range(8)], high, lh)
        for i in range(8):
            zs[i * 8 + lo, rh, lh] = states[3][i]
        e = backward([es[i * 8 + lo, rh, lh] for i in range(8)], states, high, lh)
        for i in range(8):
            es[i * 8 + lo, rh, lh] = e[i]

    @pl.loop(0, 32)
    def _(t):
        hi, rh, lh = place(t)
        states = forward([z0[hi * 8 + i, rh, lh] for i in range(8)], low, lh)
        e = backward([es[hi * 8 + i, rh, lh] for i in range(8)], states, low, lh)
        for i in range(8):
            es[hi * 8 + i, rh, lh] = e[i]

    @pl.loop(0, 4)
    def _(at):
        here = pl.ds(at * 16, 16)
        z = from_tiles(zs, at).astype(BF)
        e = from_tiles(es, at).astype(BF)
        send_ref[here, :PL, :] = z.reshape(16, PL, BLK)
        send_ref[here, PL:, :] = e.reshape(16, PL, BLK)
        deliver(at).start()
        zf = z.astype(F32)
        gated = (zf * act_s[pl.ds(at * BLK, BLK), :]).astype(BF)
        dv = (zf * dgd_s[pl.ds(at * BLK, BLK), :]).astype(BF)
        gsum[0] += mm_tn(rows(at, 0), e)
        gsum[1] += mm_tn(rows(at, 1), dv)
        gsum[2] += mm_tn(gated, rows(at, 2))

    own = place_ref[2]
    for ref, half in ((keep_ref, own), (give_ref, 1 - own)):
        cut = pl.ds(pl.multiple_of(half * 128, 128), 128)
        for w in range(3):
            ref[:, w * 8 : (w + 1) * 8] = (
                gsum[w, :, cut].reshape(4, 8, 8, 128).astype(ref.dtype)
            )
        for part in range(3):
            sums = jnp.sum(acc[part * 8 : (part + 1) * 8, half], axis=1)
            ref[part, 24] = sums.astype(ref.dtype)
        ref[3, 24] = jnp.zeros((8, 128), ref.dtype)
    for at in range(4):
        deliver(at).wait()


def core_sum_kernel(place_ref, keep_ref, got_ref, own_ref, *give_refs):
    def piece(k):
        d = (place_ref[0] + k) & 3
        return keep_ref[d] + got_ref[d].astype(F32)

    own_ref[...] = piece(0)
    for k, ref in enumerate(give_refs, 1):
        ref[...] = piece(k).astype(BF)


def dp_sum_kernel(own_ref, *refs):
    *got, out_ref = refs
    total = own_ref[...]
    for ref in got:
        total = total + ref[...].astype(F32)
    out_ref[...] = total.astype(BF)


def pair_sum_kernel(a_ref, b_ref, out_ref):
    out_ref[...] = (a_ref[...].astype(F32) + b_ref[...].astype(F32)).astype(out_ref.dtype)


def ordered_sum_kernel(place_ref, *refs):
    *parts, out_ref, held = refs
    for k, ref in enumerate(parts):
        held[(place_ref[0] + 4 - k) & 3] = ref[...]
    total = held[0].astype(F32)
    for at in range(1, 4):
        total = total + held[at].astype(F32)
    out_ref[...] = total


def gather_kernel(place_ref, *refs):
    *parts, out_ref = refs
    for k, ref in enumerate(parts):
        out_ref[(place_ref[1] + 4 - k) & 3] = ref[...]


def group_of(recv_ref, g, which):
    return recv_ref[g, :, which * PL : (which + 1) * PL, :].reshape(BLK, BLK)


def local_kernel(recv_ref, u_ref, out_ref):
    total = jnp.zeros((BLK, BLK), F32)
    for g in range(GROUPS):
        total = total + mm_nt(group_of(recv_ref, g, 1), u_ref[:, lanes(g)])
    out_ref[...] = total.astype(BF)


def last_kernel(
    recv_ref, x_ref, gain_ref, act_ref, dgd_ref, wu_ref, wv_ref, wo_ref, local_ref,
    mixed_ref, dx_ref, scaled_ref,
):
    r = inv_rms(x_ref)
    local = local_ref[...]
    inner = jnp.zeros((BLK, 1), F32)
    for g in range(GROUPS):
        z = group_of(recv_ref, g, 0).astype(F32)
        gated = (z * act_ref[:, lanes(g)]).astype(BF)
        mixed_ref[:, lanes(g)] = mm(gated, wo_ref[g]).astype(BF)
        dv = (z * dgd_ref[:, lanes(g)]).astype(BF)
        du = mm_tn(local, group_of(recv_ref, g, 1)).astype(BF)
        scaled = (mm_nt(du, wu_ref[g]) + mm_nt(dv, wv_ref[g])) * gain_ref[:, lanes(g)]
        scaled_ref[:, lanes(g)] = scaled
        inner = inner + jnp.sum(scaled * x_ref[:, lanes(g)].astype(F32), axis=-1, keepdims=True)
    shift = r * r * inner * (1.0 / (GROUPS * BLK))
    for g in range(GROUPS):
        x = x_ref[:, lanes(g)].astype(F32)
        dx_ref[:, lanes(g)] = (r * (scaled_ref[:, lanes(g)] - x * shift)).astype(BF)


def place_kernel(place_ref, wu_ref, wv_ref, gain_ref, *refs):
    own, other = refs[:4], refs[4:8]
    gu_ref, gv_ref, go_ref, gain_out, bfly_ref = refs[8:]
    for k in range(4):
        d = (place_ref[0] + 4 - k) & 3
        rows = pl.ds(pl.multiple_of(d * 64, 64), 64)
        for parts, half in ((own, place_ref[2]), (other, 1 - place_ref[2])):
            cut = pl.ds(pl.multiple_of(half * 128, 128), 128)
            for w, out in enumerate((gu_ref, gv_ref, go_ref)):
                out[:, rows, cut] = (
                    parts[k][:, w * 8 : (w + 1) * 8].astype(F32).reshape(GROUPS, 64, 128)
                )

            @pl.when(d < 3)
            def _():
                for g in range(GROUPS):
                    wide = pl.ds(pl.multiple_of(g * BLK + half * 128, 128), 128)
                    tile = parts[k][g, 24].astype(F32)
                    for s in range(8):
                        bfly_ref[2 * d + s // 4, s // 2 % 2, s % 2 : s % 2 + 1, wide] = (
                            tile[s : s + 1]
                        )

    ones = jnp.ones((8, BLK), F32)
    for g in range(GROUPS):
        product = gu_ref[g] * wu_ref[g].astype(F32) + gv_ref[g] * wv_ref[g].astype(F32)
        sums = lax.dot_general(
            ones, product, (((1,), (1,)), ((), ())),
            precision=lax.Precision.HIGHEST, preferred_element_type=F32,
        )
        gain_out[:, lanes(g)] = sums[:1] / gain_ref[:, lanes(g)]


def call(kernel, outs, scratch=(), flops=0, moved=0, vmem=24, smem=(), hbm=(), hbm_out=(), free=()):
    shapes = [jax.ShapeDtypeStruct(shape, dtype) for shape, dtype in outs]
    whole = pl.BlockSpec(memory_space=pltpu.VMEM)

    def run(*args):
        specs = [whole] * len(args)
        for at in smem:
            specs[at] = pl.BlockSpec(memory_space=pltpu.SMEM)
        for at in hbm:
            specs[at] = pl.BlockSpec(memory_space=pltpu.HBM)
        for at in free:
            specs[at] = pl.BlockSpec(memory_space=pl.ANY)
        return pl.pallas_call(
            kernel,
            out_shape=shapes,
            in_specs=specs,
            out_specs=[
                pl.BlockSpec(memory_space=pltpu.HBM) if at in hbm_out else whole
                for at in range(len(shapes))
            ],
            scratch_shapes=list(scratch),
            compiler_params=pltpu.CompilerParams(vmem_limit_bytes=vmem << 20),
            cost_estimate=pl.CostEstimate(
                flops=int(flops), bytes_accessed=int(moved), transcendentals=0
            ),
        )(*args)

    return run


def rotated(values, axis, step=1):
    n = lax.axis_size(axis)
    if not isinstance(values, (list, tuple)):
        values = [values] * (n // step - 1)
    return [
        lax.ppermute(value, axis, [(s, (s + k * step) % n) for s in range(n)])
        for k, value in enumerate(values, 1)
    ]


def swapped(value, axis="c", bit=1):
    return lax.ppermute(value, axis, [(s, s ^ bit) for s in range(lax.axis_size(axis))])


def per_device(tokens, cotangent, gain, w_u, w_v, w_o, local_factor, butterfly):
    x = tokens.reshape(BLK, -1)
    cot = cotangent.reshape(BLK, -1)
    gain2 = gain.reshape(1, -1)
    wide = (BLK, GROUPS * BLK)
    place = jnp.stack(
        [lax.axis_index("dp"), lax.axis_index("z") >> 1, lax.axis_index("c")]
    ).astype(jnp.int32)

    send = call(
        first_kernel,
        [((GROUPS, 16, 3 * PL, BLK), BF)],
        scratch=[
            pltpu.VMEM(wide, BF),
            pltpu.VMEM(wide, BF),
            pltpu.VMEM((BLK, BLK), BF),
            pltpu.SemaphoreType.DMA((3,)),
        ],
        flops=1.4e8,
        moved=4e6,
        hbm=(0, 1, 3),
        vmem=58,
    )(x, cot, gain2, local_factor)[0]
    recv = lax.all_to_all(send.reshape(BLOCKS, 3 * PL, BLK), SEQ, 0, 0)

    u, act, dgd = call(
        side_kernel, [(wide, BF), (wide, F32), (wide, F32)], flops=4e8, moved=8e6, vmem=63
    )(x, cot, gain2, w_u, w_v, w_o)
    recv, u, act, dgd = lax.optimization_barrier((recv, u, act, dgd))

    tiled = (BLOCKS, 2, 2, 8, 128)
    quarter = (25, 8, 128)
    back, keep, give = call(
        mid_kernel,
        [((BLOCKS, 2 * PL, BLK), BF), ((4,) + quarter, F32), ((4,) + quarter, BF)],
        scratch=[
            pltpu.VMEM((BLOCKS, 3 * PL, BLK), BF),
            pltpu.VMEM((BLOCKS, 2 * PL, BLK), BF),
            pltpu.VMEM(butterfly.shape[:3] + (BLK,), F32),
            pltpu.VMEM((BLK, BLK), BF),
            pltpu.VMEM((BLK, BLK), BF),
            pltpu.VMEM((BLK, BLK), BF),
            pltpu.VMEM(tiled, F32),
            pltpu.VMEM(tiled, F32),
            pltpu.VMEM(tiled, F32),
            pltpu.VMEM((BLOCKS * PL, BLK), F32),
            pltpu.VMEM((BLOCKS * PL, BLK), F32),
            pltpu.VMEM((24, 2, 8, 128), F32),
            pltpu.VMEM((24, 2, 8, 128), F32),
            pltpu.VMEM((3, BLK, BLK), F32),
            pltpu.SemaphoreType.DMA((4,)),
            pltpu.SemaphoreType.DMA((4,)),
            pltpu.SemaphoreType.DMA((4,)),
        ],
        flops=8e8,
        moved=4e6,
        vmem=63,
        smem=(0,),
        hbm=(2, 3, 4, 5),
        free=(1,),
        hbm_out=(0,),
    )(place, recv, butterfly, w_u, w_v, w_o)

    recv2 = lax.all_to_all(back, SEQ, 0, 0).reshape(GROUPS, 16, 2 * PL, BLK)

    own, *gives = call(
        core_sum_kernel, [(quarter, F32)] + [(quarter, BF)] * 3, moved=1e6, smem=(0,)
    )(place, keep, swapped(give))
    slice_ = call(dp_sum_kernel, [(quarter, BF)], moved=3e5)(own, *rotated(gives, "dp"))[0]
    for axis, bit in (("y", 1), ("y", 2), ("z", 1)):
        slice_ = call(pair_sum_kernel, [(quarter, BF)], moved=2e5)(
            slice_, swapped(slice_, axis, bit)
        )[0]
    got_z = rotated(slice_, "z", 2)

    part = call(local_kernel, [((BLK, BLK), BF)], flops=1.3e8, moved=1.2e6)(recv2, u)[0]
    parts = rotated(part, "dp")
    mixed, dx = call(
        last_kernel, [(wide, BF), (wide, BF)], scratch=[pltpu.VMEM(wide, F32)],
        flops=6e8, moved=8e6,
    )(recv2, x, gain2, act, dgd, w_u, w_v, w_o, local_factor)
    got_z, mixed, dx = lax.optimization_barrier((got_z, mixed, dx))

    mine_d = call(gather_kernel, [((4,) + quarter, BF)], moved=4e5, smem=(0,))(
        place, slice_, *got_z
    )[0]
    mine_d, parts = lax.optimization_barrier((mine_d, parts))
    halves = [mine_d] + rotated(mine_d, "dp")
    grad_local = call(
        ordered_sum_kernel,
        [((BLK, BLK), F32)],
        scratch=[pltpu.VMEM((4, BLK, BLK), BF)],
        moved=8e5,
        smem=(0,),
    )(place, part, *parts)[0]
    others = [swapped(half) for half in halves]
    others, grad_local = lax.optimization_barrier((others, grad_local))

    shape = (GROUPS, BLK, BLK)
    gu, gv, go, grad_gain, grad_bfly = call(
        place_kernel,
        [(shape, F32)] * 3 + [(gain2.shape, F32), (butterfly.shape, F32)],
        moved=5e6,
        smem=(0,),
    )(place, w_u, w_v, gain2, *halves, *others)

    return (
        mixed.reshape(tokens.shape),
        dx.reshape(tokens.shape),
        gu,
        gv,
        go,
        grad_gain.reshape(gain.shape),
        grad_local,
        grad_bfly,
    )


def solution(mesh):
    fine = Mesh(mesh.devices.reshape(4, 8, 4, 2), ("dp", "z", "y", "c"))
    block = P("dp", SEQ, None)
    return jax.shard_map(
        per_device,
        mesh=fine,
        in_specs=(block, block, P(), P(), P(), P(), P(SEQ, None), P()),
        out_specs=(block, block, P(), P(), P(), P(), P(SEQ, None), P()),
        check_vma=False,
    )
```

```python
import functools

import jax
import jax.numpy as jnp
from jax import lax
from jax.experimental import pallas as pl
from jax.experimental.pallas import tpu as pltpu
from jax.sharding import Mesh, PartitionSpec as P

BF = jnp.bfloat16
F32 = jnp.float32
GROUPS = 4
BLK = 256
BLOCKS = 64
PL = 16
SEQ = ("z", "y", "c")


def dot(a, b, dims):
    return lax.dot_general(a, b, (dims, ((), ())), preferred_element_type=F32)


def mm(a, b):
    return dot(a, b, ((1,), (0,)))


def mm_nt(a, b):
    return dot(a, b, ((1,), (1,)))


def mm_tn(a, b):
    return dot(a, b, ((0,), (0,)))


def lanes(g):
    return slice(g * BLK, (g + 1) * BLK)


def inv_rms(x_ref):
    total = jnp.zeros((BLK, 1), F32)
    for g in range(GROUPS):
        x = x_ref[:, lanes(g)].astype(F32)
        total = total + jnp.sum(x * x, axis=-1, keepdims=True)
    return lax.rsqrt(total * (1.0 / (GROUPS * BLK)) + 1e-06)


def first_kernel(x_hbm, cot_hbm, gain_ref, local_hbm, send_hbm, x_ref, local_ref, send_ref, sems):
    fetch_x = pltpu.make_async_copy(x_hbm, x_ref, sems.at[0])
    fetch_local = pltpu.make_async_copy(local_hbm, local_ref, sems.at[1])
    passed = [
        pltpu.make_async_copy(
            cot_hbm.at[:, :, lanes(g)], send_hbm.at[g, :, 2 * PL :, :], sems.at[2 + g]
        )
        for g in range(GROUPS)
    ]
    made = [
        pltpu.make_async_copy(
            send_ref.at[g], send_hbm.at[g, :, : 2 * PL, :], sems.at[6 + g]
        )
        for g in range(GROUPS)
    ]
    for copy in (fetch_x, fetch_local, *passed):
        copy.start()
    fetch_x.wait()
    r = inv_rms(x_ref)
    fetch_local.wait()
    local = local_ref[...]
    for g in range(GROUPS):
        xn = (x_ref[:, lanes(g)].astype(F32) * r * gain_ref[:, lanes(g)]).astype(BF)
        send_ref[g, :, PL:, :] = xn.reshape(16, PL, BLK)
        send_ref[g, :, :PL, :] = mm(local, xn).astype(BF).reshape(16, PL, BLK)
        made[g].start()
    for copy in (*passed, *made):
        copy.wait()


def side_kernel(x_ref, cot_ref, gain_ref, wu_ref, wv_ref, wo_ref, u_ref, act_ref, dgd_ref):
    r = inv_rms(x_ref)
    for g in range(GROUPS):
        xn = (x_ref[:, lanes(g)].astype(F32) * r * gain_ref[:, lanes(g)]).astype(BF)
        u_ref[:, lanes(g)] = mm(xn, wu_ref[g]).astype(BF)
        v = mm(xn, wv_ref[g])
        sig = jax.nn.sigmoid(v)
        act_ref[:, lanes(g)] = v * sig
        dg = mm_nt(cot_ref[:, lanes(g)], wo_ref[g])
        dgd_ref[:, lanes(g)] = dg * (sig * (1.0 + v * (1.0 - sig)))


def tiles_of(value):
    split = value.reshape(16, 2, 8, BLK)
    return split[..., :128], split[..., 128:]


def from_tiles(ref, at):
    part = ref[pl.ds(at * 16, 16)]
    return jnp.concatenate([part[:, :, 0], part[:, :, 1]], axis=-1).reshape(BLK, BLK)


def mid_kernel(
    place_ref, recv_hbm, coef_hbm, wu_hbm, wv_hbm, wo_hbm,
    send_hbm, keep_ref, give_ref,
    recv_ref, send_ref, coef_ref, wu_ref, wv_ref, wo_ref,
    z0, zs, es, act_s, dgd_s, coef, acc, gsum, in_sems, out_sems, sems,
):
    group = place_ref[1]

    def fetch(at):
        here = pl.ds(at * 16, 16)
        return pltpu.make_async_copy(recv_hbm.at[here], recv_ref.at[here], in_sems.at[at])

    def deliver(at):
        here = pl.ds(at * 16, 16)
        return pltpu.make_async_copy(send_ref.at[here], send_hbm.at[here], out_sems.at[at])

    mine = pl.ds(pl.multiple_of(group * BLK, BLK), BLK)
    weights = [
        pltpu.make_async_copy(src.at[group], dst, sems.at[at])
        for at, (src, dst) in enumerate(
            ((wu_hbm, wu_ref), (wv_hbm, wv_ref), (wo_hbm, wo_ref))
        )
    ]
    coefs = pltpu.make_async_copy(coef_hbm.at[:, :, :, mine], coef_ref, sems.at[3])
    for copy in (fetch(0), *weights, coefs, fetch(1), fetch(2), fetch(3)):
        copy.start()
    acc[...] = jnp.zeros_like(acc)
    gsum[...] = jnp.zeros_like(gsum)
    coefs.wait()
    for row in range(24):
        for lh in range(2):
            coef[row, lh] = jnp.broadcast_to(
                coef_ref[row // 4, row // 2 % 2, row % 2 : row % 2 + 1, lh * 128 : (lh + 1) * 128],
                (8, 128),
            )
    for copy in weights:
        copy.wait()

    def rows(at, which):
        return recv_ref[pl.ds(at * 16, 16), which * PL : (which + 1) * PL, :].reshape(BLK, BLK)

    @pl.loop(0, 4, unroll=True)
    def _(at):
        fetch(at).wait()
        here = pl.ds(at * 16, 16)
        p = mm(rows(at, 0), wu_ref[...]).astype(BF).astype(F32)
        v = mm(rows(at, 1), wv_ref[...])
        dg = mm_nt(rows(at, 2), wo_ref[...])
        sig = jax.nn.sigmoid(v)
        act = v * sig
        e = (dg * act).astype(BF).astype(F32)
        act_s[pl.ds(at * BLK, BLK), :] = act
        dgd_s[pl.ds(at * BLK, BLK), :] = dg * (sig * (1.0 + v * (1.0 - sig)))
        for lh, (pt, et) in enumerate(zip(tiles_of(p), tiles_of(e))):
            z0[here, :, lh] = pt
            es[here, :, lh] = et

    def place(t):
        return t >> 2, (t >> 1) & 1, t & 1

    def forward(z, bits, lh):
        states = [z]
        for j, k in enumerate(bits):
            z = [
                coef[4 * k + 2 * (i >> j & 1), lh] * z[i]
                + coef[4 * k + 2 * (i >> j & 1) + 1, lh] * z[i ^ (1 << j)]
                for i in range(8)
            ]
            states.append(z)
        return states

    def backward(e, states, bits, lh):
        for j, k in reversed(tuple(enumerate(bits))):
            z = states[j]
            for b in range(2):
                at = [i for i in range(8) if (i >> j & 1) == b]
                acc[4 * k + 2 * b, lh] += sum(e[i] * z[i] for i in at)
                acc[4 * k + 2 * b + 1, lh] += sum(e[i] * z[i ^ (1 << j)] for i in at)
            e = [
                coef[4 * k + 2 * (i >> j & 1), lh] * e[i]
                + coef[4 * k + 2 * (1 - (i >> j & 1)) + 1, lh] * e[i ^ (1 << j)]
                for i in range(8)
            ]
        return e

    low, high = (0, 1, 2), (3, 4, 5)

    @pl.loop(0, 32, unroll=4)
    def _(t):
        hi, rh, lh = place(t)
        z = forward([z0[hi * 8 + i, rh, lh] for i in range(8)], low, lh)[-1]
        for i in range(8):
            zs[hi * 8 + i, rh, lh] = z[i]

    @pl.loop(0, 32, unroll=4)
    def _(t):
        lo, rh, lh = place(t)
        states = forward([zs[i * 8 + lo, rh, lh] for i in range(8)], high, lh)
        for i in range(8):
            zs[i * 8 + lo, rh, lh] = states[3][i]
        e = backward([es[i * 8 + lo, rh, lh] for i in range(8)], states, high, lh)
        for i in range(8):
            es[i * 8 + lo, rh, lh] = e[i]

    @pl.loop(0, 32, unroll=4)
    def _(t):
        hi, rh, lh = place(t)
        states = forward([z0[hi * 8 + i, rh, lh] for i in range(8)], low, lh)
        e = backward([es[hi * 8 + i, rh, lh] for i in range(8)], states, low, lh)
        for i in range(8):
            es[hi * 8 + i, rh, lh] = e[i]

    @pl.loop(0, 4, unroll=True)
    def _(at):
        here = pl.ds(at * 16, 16)
        z = from_tiles(zs, at).astype(BF)
        e = from_tiles(es, at).astype(BF)
        send_ref[here, :PL, :] = z.reshape(16, PL, BLK)
        send_ref[here, PL:, :] = e.reshape(16, PL, BLK)
        deliver(at).start()
        zf = z.astype(F32)
        gated = (zf * act_s[pl.ds(at * BLK, BLK), :]).astype(BF)
        dv = (zf * dgd_s[pl.ds(at * BLK, BLK), :]).astype(BF)
        gsum[0] += mm_tn(rows(at, 0), e)
        gsum[1] += mm_tn(rows(at, 1), dv)
        gsum[2] += mm_tn(gated, rows(at, 2))

    own = place_ref[2]
    for ref, half in ((keep_ref, own), (give_ref, 1 - own)):
        cut = pl.ds(pl.multiple_of(half * 128, 128), 128)
        for w in range(3):
            ref[:, w * 8 : (w + 1) * 8] = (
                gsum[w, :, cut].reshape(4, 8, 8, 128).astype(ref.dtype)
            )
        for part in range(3):
            sums = jnp.sum(acc[part * 8 : (part + 1) * 8, half], axis=1)
            ref[part, 24] = sums.astype(ref.dtype)
        ref[3, 24] = jnp.zeros((8, 128), ref.dtype)
    for at in range(4):
        deliver(at).wait()


def core_sum_kernel(place_ref, keep_ref, got_ref, own_ref, *give_refs):
    def piece(k):
        d = (place_ref[0] + k) & 3
        return keep_ref[d] + got_ref[d].astype(F32)

    own_ref[...] = piece(0)
    for k, ref in enumerate(give_refs, 1):
        ref[...] = piece(k).astype(BF)


def dp_sum_kernel(own_ref, *refs):
    *got, out_ref = refs
    total = own_ref[...]
    for ref in got:
        total = total + ref[...].astype(F32)
    out_ref[...] = total.astype(BF)


def pair_sum_kernel(a_ref, b_ref, out_ref):
    out_ref[...] = (a_ref[...].astype(F32) + b_ref[...].astype(F32)).astype(out_ref.dtype)


def ordered_sum_kernel(place_ref, *refs):
    *parts, out_ref, held = refs
    for k, ref in enumerate(parts):
        held[(place_ref[0] + 4 - k) & 3] = ref[...]
    total = held[0].astype(F32)
    for at in range(1, 4):
        total = total + held[at].astype(F32)
    out_ref[...] = total


def gather_kernel(place_ref, *refs):
    *parts, out_ref = refs
    for k, ref in enumerate(parts):
        out_ref[(place_ref[1] + 4 - k) & 3] = ref[...]


def group_of(recv_ref, g, which):
    return recv_ref[g, :, which * PL : (which + 1) * PL, :].reshape(BLK, BLK)


def local_kernel(recv_ref, u_ref, out_ref):
    total = jnp.zeros((BLK, BLK), F32)
    for g in range(GROUPS):
        total = total + mm_nt(group_of(recv_ref, g, 1), u_ref[:, lanes(g)])
    out_ref[...] = total.astype(BF)


def last_kernel(
    recv_ref, x_ref, gain_ref, act_ref, dgd_ref, wu_ref, wv_ref, wo_ref, local_ref,
    mixed_ref, dx_ref, scaled_ref,
):
    r = inv_rms(x_ref)
    local = local_ref[...]
    inner = jnp.zeros((BLK, 1), F32)
    for g in range(GROUPS):
        z = group_of(recv_ref, g, 0).astype(F32)
        gated = (z * act_ref[:, lanes(g)]).astype(BF)
        mixed_ref[:, lanes(g)] = mm(gated, wo_ref[g]).astype(BF)
        dv = (z * dgd_ref[:, lanes(g)]).astype(BF)
        du = mm_tn(local, group_of(recv_ref, g, 1)).astype(BF)
        scaled = (mm_nt(du, wu_ref[g]) + mm_nt(dv, wv_ref[g])) * gain_ref[:, lanes(g)]
        scaled_ref[:, lanes(g)] = scaled
        inner = inner + jnp.sum(scaled * x_ref[:, lanes(g)].astype(F32), axis=-1, keepdims=True)
    shift = r * r * inner * (1.0 / (GROUPS * BLK))
    for g in range(GROUPS):
        x = x_ref[:, lanes(g)].astype(F32)
        dx_ref[:, lanes(g)] = (r * (scaled_ref[:, lanes(g)] - x * shift)).astype(BF)


def place_kernel(place_ref, wu_ref, wv_ref, gain_ref, *refs):
    own, other = refs[:4], refs[4:8]
    gu_ref, gv_ref, go_ref, gain_out, bfly_ref = refs[8:]
    for k in range(4):
        d = (place_ref[0] + 4 - k) & 3
        rows = pl.ds(pl.multiple_of(d * 64, 64), 64)
        for parts, half in ((own, place_ref[2]), (other, 1 - place_ref[2])):
            cut = pl.ds(pl.multiple_of(half * 128, 128), 128)
            for w, out in enumerate((gu_ref, gv_ref, go_ref)):
                out[:, rows, cut] = (
                    parts[k][:, w * 8 : (w + 1) * 8].astype(F32).reshape(GROUPS, 64, 128)
                )

            @pl.when(d < 3)
            def _():
                for g in range(GROUPS):
                    wide = pl.ds(pl.multiple_of(g * BLK + half * 128, 128), 128)
                    tile = parts[k][g, 24].astype(F32)
                    for s in range(8):
                        bfly_ref[2 * d + s // 4, s // 2 % 2, s % 2 : s % 2 + 1, wide] = (
                            tile[s : s + 1]
                        )

    ones = jnp.ones((8, BLK), F32)
    for g in range(GROUPS):
        product = gu_ref[g] * wu_ref[g].astype(F32) + gv_ref[g] * wv_ref[g].astype(F32)
        sums = lax.dot_general(
            ones, product, (((1,), (1,)), ((), ())),
            precision=lax.Precision.HIGHEST, preferred_element_type=F32,
        )
        gain_out[:, lanes(g)] = sums[:1] / gain_ref[:, lanes(g)]


def call(kernel, outs, scratch=(), flops=0, moved=0, vmem=24, smem=(), hbm=(), hbm_out=(), free=()):
    shapes = [jax.ShapeDtypeStruct(shape, dtype) for shape, dtype in outs]
    whole = pl.BlockSpec(memory_space=pltpu.VMEM)

    def run(*args):
        specs = [whole] * len(args)
        for at in smem:
            specs[at] = pl.BlockSpec(memory_space=pltpu.SMEM)
        for at in hbm:
            specs[at] = pl.BlockSpec(memory_space=pltpu.HBM)
        for at in free:
            specs[at] = pl.BlockSpec(memory_space=pl.ANY)
        return pl.pallas_call(
            kernel,
            out_shape=shapes,
            in_specs=specs,
            out_specs=[
                pl.BlockSpec(memory_space=pltpu.HBM) if at in hbm_out else whole
                for at in range(len(shapes))
            ],
            scratch_shapes=list(scratch),
            compiler_params=pltpu.CompilerParams(vmem_limit_bytes=vmem << 20),
            cost_estimate=pl.CostEstimate(
                flops=int(flops), bytes_accessed=int(moved), transcendentals=0
            ),
        )(*args)

    return run


def rotated(values, axis, step=1):
    n = lax.axis_size(axis)
    if not isinstance(values, (list, tuple)):
        values = [values] * (n // step - 1)
    return [
        lax.ppermute(value, axis, [(s, (s + k * step) % n) for s in range(n)])
        for k, value in enumerate(values, 1)
    ]


def swapped(value, axis="c", bit=1):
    return lax.ppermute(value, axis, [(s, s ^ bit) for s in range(lax.axis_size(axis))])


def per_device(tokens, cotangent, gain, w_u, w_v, w_o, local_factor, butterfly):
    x = tokens.reshape(BLK, -1)
    cot = cotangent.reshape(BLK, -1)
    gain2 = gain.reshape(1, -1)
    wide = (BLK, GROUPS * BLK)
    place = jnp.stack(
        [lax.axis_index("dp"), lax.axis_index("z") >> 1, lax.axis_index("c")]
    ).astype(jnp.int32)

    send = call(
        first_kernel,
        [((GROUPS, 16, 3 * PL, BLK), BF)],
        scratch=[
            pltpu.VMEM(wide, BF),
            pltpu.VMEM((BLK, BLK), BF),
            pltpu.VMEM((GROUPS, 16, 2 * PL, BLK), BF),
            pltpu.SemaphoreType.DMA((10,)),
        ],
        flops=1.4e8,
        moved=4e6,
        hbm=(0, 1, 3),
        hbm_out=(0,),
        vmem=58,
    )(x, cot.reshape(16, PL, -1), gain2, local_factor)[0]
    recv = lax.all_to_all(send.reshape(BLOCKS, 3 * PL, BLK), SEQ, 0, 0)

    u, act, dgd = call(
        side_kernel, [(wide, BF), (wide, F32), (wide, F32)], flops=4e8, moved=8e6, vmem=63
    )(x, cot, gain2, w_u, w_v, w_o)
    recv, u, act, dgd = lax.optimization_barrier((recv, u, act, dgd))

    tiled = (BLOCKS, 2, 2, 8, 128)
    quarter = (25, 8, 128)
    back, keep, give = call(
        mid_kernel,
        [((BLOCKS, 2 * PL, BLK), BF), ((4,) + quarter, F32), ((4,) + quarter, BF)],
        scratch=[
            pltpu.VMEM((BLOCKS, 3 * PL, BLK), BF),
            pltpu.VMEM((BLOCKS, 2 * PL, BLK), BF),
            pltpu.VMEM(butterfly.shape[:3] + (BLK,), F32),
            pltpu.VMEM((BLK, BLK), BF),
            pltpu.VMEM((BLK, BLK), BF),
            pltpu.VMEM((BLK, BLK), BF),
            pltpu.VMEM(tiled, F32),
            pltpu.VMEM(tiled, F32),
            pltpu.VMEM(tiled, F32),
            pltpu.VMEM((BLOCKS * PL, BLK), F32),
            pltpu.VMEM((BLOCKS * PL, BLK), F32),
            pltpu.VMEM((24, 2, 8, 128), F32),
            pltpu.VMEM((24, 2, 8, 128), F32),
            pltpu.VMEM((3, BLK, BLK), F32),
            pltpu.SemaphoreType.DMA((4,)),
            pltpu.SemaphoreType.DMA((4,)),
            pltpu.SemaphoreType.DMA((4,)),
        ],
        flops=8e8,
        moved=4e6,
        vmem=63,
        smem=(0,),
        hbm=(2, 3, 4, 5),
        free=(1,),
        hbm_out=(0,),
    )(place, recv, butterfly, w_u, w_v, w_o)

    recv2 = lax.all_to_all(back, SEQ, 0, 0).reshape(GROUPS, 16, 2 * PL, BLK)

    own, *gives = call(
        core_sum_kernel, [(quarter, F32)] + [(quarter, BF)] * 3, moved=1e6, smem=(0,)
    )(place, keep, swapped(give))
    slice_ = call(dp_sum_kernel, [(quarter, BF)], moved=3e5)(own, *rotated(gives, "dp"))[0]
    for axis, bit in (("y", 1), ("y", 2), ("z", 1)):
        slice_ = call(pair_sum_kernel, [(quarter, BF)], moved=2e5)(
            slice_, swapped(slice_, axis, bit)
        )[0]
    got_z = rotated(slice_, "z", 2)

    recv2, slice_ = lax.optimization_barrier((recv2, slice_))
    part = call(local_kernel, [((BLK, BLK), BF)], flops=1.3e8, moved=1.2e6)(recv2, u)[0]
    parts = rotated(part, "dp")
    mine_d = call(gather_kernel, [((4,) + quarter, BF)], moved=4e5, smem=(0,))(
        place, slice_, *got_z
    )[0]
    mine_d, parts = lax.optimization_barrier((mine_d, parts))
    got_d = rotated(mine_d, "dp")
    grad_local = call(
        ordered_sum_kernel,
        [((BLK, BLK), F32)],
        scratch=[pltpu.VMEM((4, BLK, BLK), BF)],
        moved=8e5,
        smem=(0,),
    )(place, part, *parts)[0]
    mixed, dx = call(
        last_kernel, [(wide, BF), (wide, BF)], scratch=[pltpu.VMEM(wide, F32)],
        flops=6e8, moved=8e6,
    )(recv2, x, gain2, act, dgd, w_u, w_v, w_o, local_factor)
    got_d, grad_local, mixed, dx = lax.optimization_barrier((got_d, grad_local, mixed, dx))
    halves = [mine_d] + got_d
    others = [swapped(half) for half in halves]

    shape = (GROUPS, BLK, BLK)
    gu, gv, go, grad_gain, grad_bfly = call(
        place_kernel,
        [(shape, F32)] * 3 + [(gain2.shape, F32), (butterfly.shape, F32)],
        moved=5e6,
        smem=(0,),
    )(place, w_u, w_v, gain2, *halves, *others)

    return (
        mixed.reshape(tokens.shape),
        dx.reshape(tokens.shape),
        gu,
        gv,
        go,
        grad_gain.reshape(gain.shape),
        grad_local,
        grad_bfly,
    )


def solution(mesh):
    fine = Mesh(mesh.devices.reshape(4, 8, 4, 2), ("dp", "z", "y", "c"))
    block = P("dp", SEQ, None)
    return jax.shard_map(
        per_device,
        mesh=fine,
        in_specs=(block, block, P(), P(), P(), P(), P(SEQ, None), P()),
        out_specs=(block, block, P(), P(), P(), P(), P(SEQ, None), P()),
        check_vma=False,
    )
```

```python
import functools

import jax
import jax.numpy as jnp
from jax import lax
from jax.experimental import pallas as pl
from jax.experimental.pallas import tpu as pltpu
from jax.sharding import Mesh, PartitionSpec as P

BF = jnp.bfloat16
F32 = jnp.float32
GROUPS = 4
BLK = 256
BLOCKS = 64
PL = 16
SEQ = ("z", "y", "c")


def dot(a, b, dims):
    return lax.dot_general(a, b, (dims, ((), ())), preferred_element_type=F32)


def mm(a, b):
    return dot(a, b, ((1,), (0,)))


def mm_nt(a, b):
    return dot(a, b, ((1,), (1,)))


def mm_tn(a, b):
    return dot(a, b, ((0,), (0,)))


def lanes(g):
    return slice(g * BLK, (g + 1) * BLK)


def inv_rms(x_ref):
    total = jnp.zeros((BLK, 1), F32)
    for g in range(GROUPS):
        x = x_ref[:, lanes(g)].astype(F32)
        total = total + jnp.sum(x * x, axis=-1, keepdims=True)
    return lax.rsqrt(total * (1.0 / (GROUPS * BLK)) + 1e-06)


def first_kernel(
    x_hbm, cot_hbm, gain_ref, local_hbm, send_hbm, x_ref, cot_ref, local_ref, send_ref, sems
):
    fetches = [
        pltpu.make_async_copy(src, dst, sems.at[at])
        for at, (src, dst) in enumerate(
            ((x_hbm, x_ref), (local_hbm, local_ref), (cot_hbm, cot_ref))
        )
    ]
    made = [
        pltpu.make_async_copy(send_ref.at[g], send_hbm.at[g], sems.at[3 + g])
        for g in range(GROUPS)
    ]
    for copy in fetches:
        copy.start()

    def put(g, at, value):
        send_ref[g, :, at * PL : (at + 1) * PL, :] = value.reshape(16, PL, BLK)

    fetches[0].wait()
    r = inv_rms(x_ref)
    fetches[1].wait()
    fetches[2].wait()
    local = local_ref[...]
    for g in range(GROUPS):
        xn = (x_ref[:, lanes(g)].astype(F32) * r * gain_ref[:, lanes(g)]).astype(BF)
        put(g, 0, mm(local, xn).astype(BF))
        put(g, 1, xn)
        put(g, 2, cot_ref[:, lanes(g)])
        made[g].start()
    for copy in made:
        copy.wait()


def side_kernel(x_ref, cot_ref, gain_ref, wu_ref, wv_ref, wo_ref, u_ref, act_ref, dgd_ref):
    r = inv_rms(x_ref)
    for g in range(GROUPS):
        xn = (x_ref[:, lanes(g)].astype(F32) * r * gain_ref[:, lanes(g)]).astype(BF)
        u_ref[:, lanes(g)] = mm(xn, wu_ref[g]).astype(BF)
        v = mm(xn, wv_ref[g])
        sig = jax.nn.sigmoid(v)
        act_ref[:, lanes(g)] = v * sig
        dg = mm_nt(cot_ref[:, lanes(g)], wo_ref[g])
        dgd_ref[:, lanes(g)] = dg * (sig * (1.0 + v * (1.0 - sig)))


def tiles_of(value):
    split = value.reshape(16, 2, 8, BLK)
    return split[..., :128], split[..., 128:]


def from_tiles(ref, at):
    part = ref[pl.ds(at * 16, 16)]
    return jnp.concatenate([part[:, :, 0], part[:, :, 1]], axis=-1).reshape(BLK, BLK)


def mid_kernel(
    place_ref, recv_hbm, coef_hbm, wu_hbm, wv_hbm, wo_hbm,
    send_hbm, keep_ref, give_ref,
    recv_ref, send_ref, coef_ref, wu_ref, wv_ref, wo_ref,
    z0, zs, es, act_s, dgd_s, coef, acc, gsum, in_sems, out_sems, sems,
):
    group = place_ref[1]

    def fetch(at):
        here = pl.ds(at * 16, 16)
        return pltpu.make_async_copy(recv_hbm.at[here], recv_ref.at[here], in_sems.at[at])

    def deliver(at):
        here = pl.ds(at * 16, 16)
        return pltpu.make_async_copy(send_ref.at[here], send_hbm.at[here], out_sems.at[at])

    mine = pl.ds(pl.multiple_of(group * BLK, BLK), BLK)
    weights = [
        pltpu.make_async_copy(src.at[group], dst, sems.at[at])
        for at, (src, dst) in enumerate(
            ((wu_hbm, wu_ref), (wv_hbm, wv_ref), (wo_hbm, wo_ref))
        )
    ]
    coefs = pltpu.make_async_copy(coef_hbm.at[:, :, :, mine], coef_ref, sems.at[3])
    for copy in (fetch(0), *weights, coefs, fetch(1), fetch(2), fetch(3)):
        copy.start()
    acc[...] = jnp.zeros_like(acc)
    gsum[...] = jnp.zeros_like(gsum)
    coefs.wait()
    for row in range(24):
        for lh in range(2):
            coef[row, lh] = jnp.broadcast_to(
                coef_ref[row // 4, row // 2 % 2, row % 2 : row % 2 + 1, lh * 128 : (lh + 1) * 128],
                (8, 128),
            )
    for copy in weights:
        copy.wait()

    def rows(at, which):
        return recv_ref[pl.ds(at * 16, 16), which * PL : (which + 1) * PL, :].reshape(BLK, BLK)

    @pl.loop(0, 4, unroll=True)
    def _(at):
        fetch(at).wait()
        here = pl.ds(at * 16, 16)
        p = mm(rows(at, 0), wu_ref[...]).astype(BF).astype(F32)
        v = mm(rows(at, 1), wv_ref[...])
        dg = mm_nt(rows(at, 2), wo_ref[...])
        sig = jax.nn.sigmoid(v)
        act = v * sig
        e = (dg * act).astype(BF).astype(F32)
        act_s[pl.ds(at * BLK, BLK), :] = act
        dgd_s[pl.ds(at * BLK, BLK), :] = dg * (sig * (1.0 + v * (1.0 - sig)))
        for lh, (pt, et) in enumerate(zip(tiles_of(p), tiles_of(e))):
            z0[here, :, lh] = pt
            es[here, :, lh] = et

    def place(t):
        return t >> 2, (t >> 1) & 1, t & 1

    def forward(z, bits, lh):
        states = [z]
        for j, k in enumerate(bits):
            z = [
                coef[4 * k + 2 * (i >> j & 1), lh] * z[i]
                + coef[4 * k + 2 * (i >> j & 1) + 1, lh] * z[i ^ (1 << j)]
                for i in range(8)
            ]
            states.append(z)
        return states

    def backward(e, states, bits, lh):
        for j, k in reversed(tuple(enumerate(bits))):
            z = states[j]
            for b in range(2):
                at = [i for i in range(8) if (i >> j & 1) == b]
                acc[4 * k + 2 * b, lh] += sum(e[i] * z[i] for i in at)
                acc[4 * k + 2 * b + 1, lh] += sum(e[i] * z[i ^ (1 << j)] for i in at)
            e = [
                coef[4 * k + 2 * (i >> j & 1), lh] * e[i]
                + coef[4 * k + 2 * (1 - (i >> j & 1)) + 1, lh] * e[i ^ (1 << j)]
                for i in range(8)
            ]
        return e

    low, high = (0, 1, 2), (3, 4, 5)

    @pl.loop(0, 32, unroll=4)
    def _(t):
        hi, rh, lh = place(t)
        z = forward([z0[hi * 8 + i, rh, lh] for i in range(8)], low, lh)[-1]
        for i in range(8):
            zs[hi * 8 + i, rh, lh] = z[i]

    @pl.loop(0, 32, unroll=4)
    def _(t):
        lo, rh, lh = place(t)
        states = forward([zs[i * 8 + lo, rh, lh] for i in range(8)], high, lh)
        for i in range(8):
            zs[i * 8 + lo, rh, lh] = states[3][i]
        e = backward([es[i * 8 + lo, rh, lh] for i in range(8)], states, high, lh)
        for i in range(8):
            es[i * 8 + lo, rh, lh] = e[i]

    @pl.loop(0, 32, unroll=4)
    def _(t):
        hi, rh, lh = place(t)
        states = forward([z0[hi * 8 + i, rh, lh] for i in range(8)], low, lh)
        e = backward([es[hi * 8 + i, rh, lh] for i in range(8)], states, low, lh)
        for i in range(8):
            es[hi * 8 + i, rh, lh] = e[i]

    @pl.loop(0, 4, unroll=True)
    def _(at):
        here = pl.ds(at * 16, 16)
        z = from_tiles(zs, at).astype(BF)
        e = from_tiles(es, at).astype(BF)
        send_ref[here, :PL, :] = z.reshape(16, PL, BLK)
        send_ref[here, PL:, :] = e.reshape(16, PL, BLK)
        deliver(at).start()
        zf = z.astype(F32)
        gated = (zf * act_s[pl.ds(at * BLK, BLK), :]).astype(BF)
        dv = (zf * dgd_s[pl.ds(at * BLK, BLK), :]).astype(BF)
        gsum[0] += mm_tn(rows(at, 0), e)
        gsum[1] += mm_tn(rows(at, 1), dv)
        gsum[2] += mm_tn(gated, rows(at, 2))

    own = place_ref[2]
    for ref, half in ((keep_ref, own), (give_ref, 1 - own)):
        cut = pl.ds(pl.multiple_of(half * 128, 128), 128)
        for w in range(3):
            ref[:, w * 8 : (w + 1) * 8] = (
                gsum[w, :, cut].reshape(4, 8, 8, 128).astype(ref.dtype)
            )
        for part in range(3):
            sums = jnp.sum(acc[part * 8 : (part + 1) * 8, half], axis=1)
            ref[part, 24] = sums.astype(ref.dtype)
        ref[3, 24] = jnp.zeros((8, 128), ref.dtype)
    for at in range(4):
        deliver(at).wait()


def core_sum_kernel(place_ref, keep_ref, got_ref, own_ref, *give_refs):
    def piece(k):
        d = (place_ref[0] + k) & 3
        return keep_ref[d] + got_ref[d].astype(F32)

    own_ref[...] = piece(0)
    for k, ref in enumerate(give_refs, 1):
        ref[...] = piece(k).astype(BF)


def dp_sum_kernel(own_ref, *refs):
    *got, out_ref = refs
    total = own_ref[...]
    for ref in got:
        total = total + ref[...].astype(F32)
    out_ref[...] = total.astype(BF)


def pair_sum_kernel(a_ref, b_ref, out_ref):
    out_ref[...] = (a_ref[...].astype(F32) + b_ref[...].astype(F32)).astype(out_ref.dtype)


def ordered_sum_kernel(place_ref, *refs):
    *parts, out_ref, held = refs
    for k, ref in enumerate(parts):
        held[(place_ref[0] + 4 - k) & 3] = ref[...]
    total = held[0].astype(F32)
    for at in range(1, 4):
        total = total + held[at].astype(F32)
    out_ref[...] = total


def gather_kernel(place_ref, *refs):
    *parts, out_ref = refs
    for k, ref in enumerate(parts):
        out_ref[(place_ref[1] + 4 - k) & 3] = ref[...]


def group_of(recv_ref, g, which):
    return recv_ref[g, :, which * PL : (which + 1) * PL, :].reshape(BLK, BLK)


def local_kernel(recv_ref, u_ref, out_ref):
    total = jnp.zeros((BLK, BLK), F32)
    for g in range(GROUPS):
        total = total + mm_nt(group_of(recv_ref, g, 1), u_ref[:, lanes(g)])
    out_ref[...] = total.astype(BF)


def last_kernel(
    recv_ref, x_ref, gain_ref, act_ref, dgd_ref, wu_ref, wv_ref, wo_ref, local_ref,
    mixed_ref, dx_ref, scaled_ref,
):
    r = inv_rms(x_ref)
    local = local_ref[...]
    inner = jnp.zeros((BLK, 1), F32)
    for g in range(GROUPS):
        z = group_of(recv_ref, g, 0).astype(F32)
        gated = (z * act_ref[:, lanes(g)]).astype(BF)
        mixed_ref[:, lanes(g)] = mm(gated, wo_ref[g]).astype(BF)
        dv = (z * dgd_ref[:, lanes(g)]).astype(BF)
        du = mm_tn(local, group_of(recv_ref, g, 1)).astype(BF)
        scaled = (mm_nt(du, wu_ref[g]) + mm_nt(dv, wv_ref[g])) * gain_ref[:, lanes(g)]
        scaled_ref[:, lanes(g)] = scaled
        inner = inner + jnp.sum(scaled * x_ref[:, lanes(g)].astype(F32), axis=-1, keepdims=True)
    shift = r * r * inner * (1.0 / (GROUPS * BLK))
    for g in range(GROUPS):
        x = x_ref[:, lanes(g)].astype(F32)
        dx_ref[:, lanes(g)] = (r * (scaled_ref[:, lanes(g)] - x * shift)).astype(BF)


def place_kernel(place_ref, wu_ref, wv_ref, gain_ref, *refs):
    own, other = refs[:4], refs[4:8]
    gu_ref, gv_ref, go_ref, gain_out, bfly_ref = refs[8:]
    for k in range(4):
        d = (place_ref[0] + 4 - k) & 3
        rows = pl.ds(pl.multiple_of(d * 64, 64), 64)
        for parts, half in ((own, place_ref[2]), (other, 1 - place_ref[2])):
            cut = pl.ds(pl.multiple_of(half * 128, 128), 128)
            for w, out in enumerate((gu_ref, gv_ref, go_ref)):
                out[:, rows, cut] = (
                    parts[k][:, w * 8 : (w + 1) * 8].astype(F32).reshape(GROUPS, 64, 128)
                )

            @pl.when(d < 3)
            def _():
                for g in range(GROUPS):
                    wide = pl.ds(pl.multiple_of(g * BLK + half * 128, 128), 128)
                    tile = parts[k][g, 24].astype(F32)
                    for s in range(8):
                        bfly_ref[2 * d + s // 4, s // 2 % 2, s % 2 : s % 2 + 1, wide] = (
                            tile[s : s + 1]
                        )

    ones = jnp.ones((8, BLK), F32)
    for g in range(GROUPS):
        product = gu_ref[g] * wu_ref[g].astype(F32) + gv_ref[g] * wv_ref[g].astype(F32)
        sums = lax.dot_general(
            ones, product, (((1,), (1,)), ((), ())),
            precision=lax.Precision.HIGHEST, preferred_element_type=F32,
        )
        gain_out[:, lanes(g)] = sums[:1] / gain_ref[:, lanes(g)]


def call(kernel, outs, scratch=(), flops=0, moved=0, vmem=24, smem=(), hbm=(), hbm_out=(), free=()):
    shapes = [jax.ShapeDtypeStruct(shape, dtype) for shape, dtype in outs]
    whole = pl.BlockSpec(memory_space=pltpu.VMEM)

    def run(*args):
        specs = [whole] * len(args)
        for at in smem:
            specs[at] = pl.BlockSpec(memory_space=pltpu.SMEM)
        for at in hbm:
            specs[at] = pl.BlockSpec(memory_space=pltpu.HBM)
        for at in free:
            specs[at] = pl.BlockSpec(memory_space=pl.ANY)
        return pl.pallas_call(
            kernel,
            out_shape=shapes,
            in_specs=specs,
            out_specs=[
                pl.BlockSpec(memory_space=pltpu.HBM) if at in hbm_out else whole
                for at in range(len(shapes))
            ],
            scratch_shapes=list(scratch),
            compiler_params=pltpu.CompilerParams(vmem_limit_bytes=vmem << 20),
            cost_estimate=pl.CostEstimate(
                flops=int(flops), bytes_accessed=int(moved), transcendentals=0
            ),
        )(*args)

    return run


def rotated(values, axis, step=1):
    n = lax.axis_size(axis)
    if not isinstance(values, (list, tuple)):
        values = [values] * (n // step - 1)
    return [
        lax.ppermute(value, axis, [(s, (s + k * step) % n) for s in range(n)])
        for k, value in enumerate(values, 1)
    ]


def swapped(value, axis="c", bit=1):
    return lax.ppermute(value, axis, [(s, s ^ bit) for s in range(lax.axis_size(axis))])


def per_device(tokens, cotangent, gain, w_u, w_v, w_o, local_factor, butterfly):
    x = tokens.reshape(BLK, -1)
    cot = cotangent.reshape(BLK, -1)
    gain2 = gain.reshape(1, -1)
    wide = (BLK, GROUPS * BLK)
    place = jnp.stack(
        [lax.axis_index("dp"), lax.axis_index("z") >> 1, lax.axis_index("c")]
    ).astype(jnp.int32)

    send = call(
        first_kernel,
        [((GROUPS, 16, 3 * PL, BLK), BF)],
        scratch=[
            pltpu.VMEM(wide, BF),
            pltpu.VMEM(wide, BF),
            pltpu.VMEM((BLK, BLK), BF),
            pltpu.VMEM((GROUPS, 16, 3 * PL, BLK), BF),
            pltpu.SemaphoreType.DMA((7,)),
        ],
        flops=1.4e8,
        moved=4e6,
        hbm=(0, 1, 3),
        hbm_out=(0,),
        vmem=58,
    )(x, cot, gain2, local_factor)[0]
    recv = lax.all_to_all(send.reshape(BLOCKS, 3 * PL, BLK), SEQ, 0, 0)

    u, act, dgd = call(
        side_kernel, [(wide, BF), (wide, F32), (wide, F32)], flops=4e8, moved=8e6, vmem=63
    )(x, cot, gain2, w_u, w_v, w_o)
    recv, u, act, dgd = lax.optimization_barrier((recv, u, act, dgd))

    tiled = (BLOCKS, 2, 2, 8, 128)
    quarter = (25, 8, 128)
    back, keep, give = call(
        mid_kernel,
        [((BLOCKS, 2 * PL, BLK), BF), ((4,) + quarter, F32), ((4,) + quarter, BF)],
        scratch=[
            pltpu.VMEM((BLOCKS, 3 * PL, BLK), BF),
            pltpu.VMEM((BLOCKS, 2 * PL, BLK), BF),
            pltpu.VMEM(butterfly.shape[:3] + (BLK,), F32),
            pltpu.VMEM((BLK, BLK), BF),
            pltpu.VMEM((BLK, BLK), BF),
            pltpu.VMEM((BLK, BLK), BF),
            pltpu.VMEM(tiled, F32),
            pltpu.VMEM(tiled, F32),
            pltpu.VMEM(tiled, F32),
            pltpu.VMEM((BLOCKS * PL, BLK), F32),
            pltpu.VMEM((BLOCKS * PL, BLK), F32),
            pltpu.VMEM((24, 2, 8, 128), F32),
            pltpu.VMEM((24, 2, 8, 128), F32),
            pltpu.VMEM((3, BLK, BLK), F32),
            pltpu.SemaphoreType.DMA((4,)),
            pltpu.SemaphoreType.DMA((4,)),
            pltpu.SemaphoreType.DMA((4,)),
        ],
        flops=8e8,
        moved=4e6,
        vmem=63,
        smem=(0,),
        hbm=(2, 3, 4, 5),
        free=(1,),
        hbm_out=(0,),
    )(place, recv, butterfly, w_u, w_v, w_o)

    recv2 = lax.all_to_all(back, SEQ, 0, 0).reshape(GROUPS, 16, 2 * PL, BLK)

    own, *gives = call(
        core_sum_kernel, [(quarter, F32)] + [(quarter, BF)] * 3, moved=1e6, smem=(0,)
    )(place, keep, swapped(give))
    slice_ = call(dp_sum_kernel, [(quarter, BF)], moved=3e5)(own, *rotated(gives, "dp"))[0]
    for axis, bit in (("y", 1), ("y", 2), ("z", 1)):
        slice_ = call(pair_sum_kernel, [(quarter, BF)], moved=2e5)(
            slice_, swapped(slice_, axis, bit)
        )[0]
    got_z = rotated(slice_, "z", 2)

    recv2, got_z = lax.optimization_barrier((recv2, got_z))
    part = call(local_kernel, [((BLK, BLK), BF)], flops=1.3e8, moved=1.2e6)(recv2, u)[0]
    parts = rotated(part, "dp")
    mine_d = call(gather_kernel, [((4,) + quarter, BF)], moved=4e5, smem=(0,))(
        place, slice_, *got_z
    )[0]
    got_d = rotated(mine_d, "dp")
    grad_local = call(
        ordered_sum_kernel,
        [((BLK, BLK), F32)],
        scratch=[pltpu.VMEM((4, BLK, BLK), BF)],
        moved=8e5,
        smem=(0,),
    )(place, part, *parts)[0]
    mixed, dx = call(
        last_kernel, [(wide, BF), (wide, BF)], scratch=[pltpu.VMEM(wide, F32)],
        flops=6e8, moved=8e6,
    )(recv2, x, gain2, act, dgd, w_u, w_v, w_o, local_factor)
    got_d, grad_local, mixed, dx = lax.optimization_barrier((got_d, grad_local, mixed, dx))
    halves = [mine_d] + got_d
    others = [swapped(half) for half in halves]

    shape = (GROUPS, BLK, BLK)
    gu, gv, go, grad_gain, grad_bfly = call(
        place_kernel,
        [(shape, F32)] * 3 + [(gain2.shape, F32), (butterfly.shape, F32)],
        moved=5e6,
        smem=(0,),
    )(place, w_u, w_v, gain2, *halves, *others)

    return (
        mixed.reshape(tokens.shape),
        dx.reshape(tokens.shape),
        gu,
        gv,
        go,
        grad_gain.reshape(gain.shape),
        grad_local,
        grad_bfly,
    )


def solution(mesh):
    fine = Mesh(mesh.devices.reshape(4, 8, 4, 2), ("dp", "z", "y", "c"))
    block = P("dp", SEQ, None)
    return jax.shard_map(
        per_device,
        mesh=fine,
        in_specs=(block, block, P(), P(), P(), P(), P(SEQ, None), P()),
        out_specs=(block, block, P(), P(), P(), P(), P(SEQ, None), P()),
        check_vma=False,
    )
```

```python
import functools

import jax
import jax.numpy as jnp
from jax import lax
from jax.experimental import pallas as pl
from jax.experimental.pallas import tpu as pltpu
from jax.sharding import Mesh, PartitionSpec as P

BF = jnp.bfloat16
F32 = jnp.float32
GROUPS = 4
BLK = 256
BLOCKS = 64
PL = 16
SEQ = ("z", "y", "c")


def dot(a, b, dims):
    return lax.dot_general(a, b, (dims, ((), ())), preferred_element_type=F32)


def mm(a, b):
    return dot(a, b, ((1,), (0,)))


def mm_nt(a, b):
    return dot(a, b, ((1,), (1,)))


def mm_tn(a, b):
    return dot(a, b, ((0,), (0,)))


def lanes(g):
    return slice(g * BLK, (g + 1) * BLK)


def inv_rms(x_ref):
    total = jnp.zeros((BLK, 1), F32)
    for g in range(GROUPS):
        x = x_ref[:, lanes(g)].astype(F32)
        total = total + jnp.sum(x * x, axis=-1, keepdims=True)
    return lax.rsqrt(total * (1.0 / (GROUPS * BLK)) + 1e-06)


def first_kernel(
    x_hbm, cot_hbm, gain_ref, local_hbm, send_hbm, x_ref, cot_ref, local_ref, send_ref, sems
):
    fetches = [
        pltpu.make_async_copy(src, dst, sems.at[at])
        for at, (src, dst) in enumerate(
            ((x_hbm, x_ref), (local_hbm, local_ref), (cot_hbm, cot_ref))
        )
    ]
    made = [
        pltpu.make_async_copy(send_ref.at[g], send_hbm.at[g], sems.at[3 + g])
        for g in range(GROUPS)
    ]
    for copy in fetches:
        copy.start()

    def put(g, at, value):
        send_ref[g, :, at * PL : (at + 1) * PL, :] = value.reshape(16, PL, BLK)

    fetches[0].wait()
    r = inv_rms(x_ref)
    fetches[1].wait()
    fetches[2].wait()
    local = local_ref[...]
    for g in range(GROUPS):
        xn = (x_ref[:, lanes(g)].astype(F32) * r * gain_ref[:, lanes(g)]).astype(BF)
        put(g, 0, mm(local, xn).astype(BF))
        put(g, 1, xn)
        put(g, 2, cot_ref[:, lanes(g)])
        made[g].start()
    for copy in made:
        copy.wait()


def side_kernel(x_ref, cot_ref, gain_ref, wu_ref, wv_ref, wo_ref, u_ref, act_ref, dgd_ref):
    r = inv_rms(x_ref)
    for g in range(GROUPS):
        xn = (x_ref[:, lanes(g)].astype(F32) * r * gain_ref[:, lanes(g)]).astype(BF)
        u_ref[:, lanes(g)] = mm(xn, wu_ref[g]).astype(BF)
        v = mm(xn, wv_ref[g])
        sig = jax.nn.sigmoid(v)
        act_ref[:, lanes(g)] = v * sig
        dg = mm_nt(cot_ref[:, lanes(g)], wo_ref[g])
        dgd_ref[:, lanes(g)] = dg * (sig * (1.0 + v * (1.0 - sig)))


def tiles_of(value):
    split = value.reshape(16, 2, 8, BLK)
    return split[..., :128], split[..., 128:]


def from_tiles(ref, at):
    part = ref[pl.ds(at * 16, 16)]
    return jnp.concatenate([part[:, :, 0], part[:, :, 1]], axis=-1).reshape(BLK, BLK)


def mid_kernel(
    place_ref, recv_hbm, coef_hbm, wu_hbm, wv_hbm, wo_hbm,
    send_hbm, keep_ref, give_ref,
    recv_ref, send_ref, coef_ref, wu_ref, wv_ref, wo_ref,
    z0, zs, es, act_s, dgd_s, coef, acc, gsum, in_sems, out_sems, sems,
):
    group = place_ref[1] >> 1

    def fetch(at):
        here = pl.ds(at * 16, 16)
        return pltpu.make_async_copy(recv_hbm.at[here], recv_ref.at[here], in_sems.at[at])

    def deliver(at):
        here = pl.ds(at * 16, 16)
        return pltpu.make_async_copy(send_ref.at[here], send_hbm.at[here], out_sems.at[at])

    mine = pl.ds(pl.multiple_of(group * BLK, BLK), BLK)
    weights = [
        pltpu.make_async_copy(src.at[group], dst, sems.at[at])
        for at, (src, dst) in enumerate(
            ((wu_hbm, wu_ref), (wv_hbm, wv_ref), (wo_hbm, wo_ref))
        )
    ]
    coefs = pltpu.make_async_copy(coef_hbm.at[:, :, :, mine], coef_ref, sems.at[3])
    for copy in (fetch(0), *weights, coefs, fetch(1), fetch(2), fetch(3)):
        copy.start()
    acc[...] = jnp.zeros_like(acc)
    gsum[...] = jnp.zeros_like(gsum)
    coefs.wait()
    for row in range(24):
        for lh in range(2):
            coef[row, lh] = jnp.broadcast_to(
                coef_ref[row // 4, row // 2 % 2, row % 2 : row % 2 + 1, lh * 128 : (lh + 1) * 128],
                (8, 128),
            )
    for copy in weights:
        copy.wait()

    def rows(at, which):
        return recv_ref[pl.ds(at * 16, 16), which * PL : (which + 1) * PL, :].reshape(BLK, BLK)

    @pl.loop(0, 4, unroll=True)
    def _(at):
        fetch(at).wait()
        here = pl.ds(at * 16, 16)
        p = mm(rows(at, 0), wu_ref[...]).astype(BF).astype(F32)
        v = mm(rows(at, 1), wv_ref[...])
        dg = mm_nt(rows(at, 2), wo_ref[...])
        sig = jax.nn.sigmoid(v)
        act = v * sig
        e = (dg * act).astype(BF).astype(F32)
        act_s[pl.ds(at * BLK, BLK), :] = act
        dgd_s[pl.ds(at * BLK, BLK), :] = dg * (sig * (1.0 + v * (1.0 - sig)))
        for lh, (pt, et) in enumerate(zip(tiles_of(p), tiles_of(e))):
            z0[here, :, lh] = pt
            es[here, :, lh] = et

    def place(t):
        return t >> 2, (t >> 1) & 1, t & 1

    def forward(z, bits, lh):
        states = [z]
        for j, k in enumerate(bits):
            z = [
                coef[4 * k + 2 * (i >> j & 1), lh] * z[i]
                + coef[4 * k + 2 * (i >> j & 1) + 1, lh] * z[i ^ (1 << j)]
                for i in range(8)
            ]
            states.append(z)
        return states

    def backward(e, states, bits, lh):
        for j, k in reversed(tuple(enumerate(bits))):
            z = states[j]
            for b in range(2):
                at = [i for i in range(8) if (i >> j & 1) == b]
                acc[4 * k + 2 * b, lh] += sum(e[i] * z[i] for i in at)
                acc[4 * k + 2 * b + 1, lh] += sum(e[i] * z[i ^ (1 << j)] for i in at)
            e = [
                coef[4 * k + 2 * (i >> j & 1), lh] * e[i]
                + coef[4 * k + 2 * (1 - (i >> j & 1)) + 1, lh] * e[i ^ (1 << j)]
                for i in range(8)
            ]
        return e

    low, high = (0, 1, 2), (3, 4, 5)

    @pl.loop(0, 32, unroll=4)
    def _(t):
        hi, rh, lh = place(t)
        z = forward([z0[hi * 8 + i, rh, lh] for i in range(8)], low, lh)[-1]
        for i in range(8):
            zs[hi * 8 + i, rh, lh] = z[i]

    @pl.loop(0, 32, unroll=4)
    def _(t):
        lo, rh, lh = place(t)
        states = forward([zs[i * 8 + lo, rh, lh] for i in range(8)], high, lh)
        for i in range(8):
            zs[i * 8 + lo, rh, lh] = states[3][i]
        e = backward([es[i * 8 + lo, rh, lh] for i in range(8)], states, high, lh)
        for i in range(8):
            es[i * 8 + lo, rh, lh] = e[i]

    @pl.loop(0, 32, unroll=4)
    def _(t):
        hi, rh, lh = place(t)
        states = forward([z0[hi * 8 + i, rh, lh] for i in range(8)], low, lh)
        e = backward([es[hi * 8 + i, rh, lh] for i in range(8)], states, low, lh)
        for i in range(8):
            es[hi * 8 + i, rh, lh] = e[i]

    @pl.loop(0, 4, unroll=True)
    def _(at):
        here = pl.ds(at * 16, 16)
        z = from_tiles(zs, at).astype(BF)
        e = from_tiles(es, at).astype(BF)
        send_ref[here, :PL, :] = z.reshape(16, PL, BLK)
        send_ref[here, PL:, :] = e.reshape(16, PL, BLK)
        deliver(at).start()
        zf = z.astype(F32)
        gated = (zf * act_s[pl.ds(at * BLK, BLK), :]).astype(BF)
        dv = (zf * dgd_s[pl.ds(at * BLK, BLK), :]).astype(BF)
        gsum[0] += mm_tn(rows(at, 0), e)
        gsum[1] += mm_tn(rows(at, 1), dv)
        gsum[2] += mm_tn(gated, rows(at, 2))

    own = place_ref[2]
    for ref, half in ((keep_ref, own), (give_ref, 1 - own)):
        cut = pl.ds(pl.multiple_of(half * 128, 128), 128)
        for w in range(3):
            ref[:, w * 8 : (w + 1) * 8] = (
                gsum[w, :, cut].reshape(4, 8, 8, 128).astype(ref.dtype)
            )
        for part in range(3):
            sums = jnp.sum(acc[part * 8 : (part + 1) * 8, half], axis=1)
            ref[part, 24] = sums.astype(ref.dtype)
        ref[3, 24] = jnp.zeros((8, 128), ref.dtype)
    for at in range(4):
        deliver(at).wait()


def core_sum_kernel(place_ref, keep_ref, got_ref, own_ref, *give_refs):
    def piece(k):
        d = (place_ref[0] + k) & 3
        return keep_ref[d] + got_ref[d].astype(F32)

    own_ref[...] = piece(0)
    for k, ref in enumerate(give_refs, 1):
        ref[...] = piece(k).astype(BF)


def quarter_sum_kernel(own_ref, *refs):
    *got, out_ref = refs
    total = own_ref[...]
    for ref in got:
        total = total + ref[...].astype(F32)
    out_ref[...] = total.astype(BF)


def pair_sum_kernel(a_ref, b_ref, out_ref):
    out_ref[...] = (a_ref[...].astype(F32) + b_ref[...].astype(F32)).astype(out_ref.dtype)


def ordered_sum_kernel(place_ref, *refs):
    *parts, out_ref, held = refs
    for k, ref in enumerate(parts):
        held[(place_ref[3] + 4 - k) & 3] = ref[...]
    total = held[0].astype(F32)
    for at in range(1, 4):
        total = total + held[at].astype(F32)
    out_ref[...] = total


def gather_kernel(place_ref, *refs):
    *parts, out_ref = refs
    for k, ref in enumerate(parts):
        out_ref[((place_ref[1] >> 1) + 4 - k) & 3] = ref[...]


def group_of(recv_ref, g, which):
    return recv_ref[g, :, which * PL : (which + 1) * PL, :].reshape(BLK, BLK)


def local_kernel(recv_ref, u_ref, out_ref):
    total = jnp.zeros((BLK, BLK), F32)
    for g in range(GROUPS):
        total = total + mm_nt(group_of(recv_ref, g, 1), u_ref[:, lanes(g)])
    out_ref[...] = total.astype(BF)


def last_kernel(
    recv_ref, x_ref, gain_ref, act_ref, dgd_ref, wu_ref, wv_ref, wo_ref, local_ref,
    mixed_ref, dx_ref, scaled_ref,
):
    r = inv_rms(x_ref)
    local = local_ref[...]
    inner = jnp.zeros((BLK, 1), F32)
    for g in range(GROUPS):
        z = group_of(recv_ref, g, 0).astype(F32)
        gated = (z * act_ref[:, lanes(g)]).astype(BF)
        mixed_ref[:, lanes(g)] = mm(gated, wo_ref[g]).astype(BF)
        dv = (z * dgd_ref[:, lanes(g)]).astype(BF)
        du = mm_tn(local, group_of(recv_ref, g, 1)).astype(BF)
        scaled = (mm_nt(du, wu_ref[g]) + mm_nt(dv, wv_ref[g])) * gain_ref[:, lanes(g)]
        scaled_ref[:, lanes(g)] = scaled
        inner = inner + jnp.sum(scaled * x_ref[:, lanes(g)].astype(F32), axis=-1, keepdims=True)
    shift = r * r * inner * (1.0 / (GROUPS * BLK))
    for g in range(GROUPS):
        x = x_ref[:, lanes(g)].astype(F32)
        dx_ref[:, lanes(g)] = (r * (scaled_ref[:, lanes(g)] - x * shift)).astype(BF)


def place_kernel(place_ref, wu_ref, wv_ref, gain_ref, *refs):
    own, other = refs[:4], refs[4:8]
    gu_ref, gv_ref, go_ref, gain_out, bfly_ref = refs[8:]
    for k in range(4):
        d = (place_ref[0] + 4 - k) & 3
        rows = pl.ds(pl.multiple_of(d * 64, 64), 64)
        for parts, half in ((own, place_ref[2]), (other, 1 - place_ref[2])):
            cut = pl.ds(pl.multiple_of(half * 128, 128), 128)
            for w, out in enumerate((gu_ref, gv_ref, go_ref)):
                out[:, rows, cut] = (
                    parts[k][:, w * 8 : (w + 1) * 8].astype(F32).reshape(GROUPS, 64, 128)
                )

            @pl.when(d < 3)
            def _():
                for g in range(GROUPS):
                    wide = pl.ds(pl.multiple_of(g * BLK + half * 128, 128), 128)
                    tile = parts[k][g, 24].astype(F32)
                    for s in range(8):
                        bfly_ref[2 * d + s // 4, s // 2 % 2, s % 2 : s % 2 + 1, wide] = (
                            tile[s : s + 1]
                        )

    ones = jnp.ones((8, BLK), F32)
    for g in range(GROUPS):
        product = gu_ref[g] * wu_ref[g].astype(F32) + gv_ref[g] * wv_ref[g].astype(F32)
        sums = lax.dot_general(
            ones, product, (((1,), (1,)), ((), ())),
            precision=lax.Precision.HIGHEST, preferred_element_type=F32,
        )
        gain_out[:, lanes(g)] = sums[:1] / gain_ref[:, lanes(g)]


def call(kernel, outs, scratch=(), flops=0, moved=0, vmem=24, smem=(), hbm=(), hbm_out=(), free=()):
    shapes = [jax.ShapeDtypeStruct(shape, dtype) for shape, dtype in outs]
    whole = pl.BlockSpec(memory_space=pltpu.VMEM)

    def run(*args):
        specs = [whole] * len(args)
        for at in smem:
            specs[at] = pl.BlockSpec(memory_space=pltpu.SMEM)
        for at in hbm:
            specs[at] = pl.BlockSpec(memory_space=pltpu.HBM)
        for at in free:
            specs[at] = pl.BlockSpec(memory_space=pl.ANY)
        return pl.pallas_call(
            kernel,
            out_shape=shapes,
            in_specs=specs,
            out_specs=[
                pl.BlockSpec(memory_space=pltpu.HBM) if at in hbm_out else whole
                for at in range(len(shapes))
            ],
            scratch_shapes=list(scratch),
            compiler_params=pltpu.CompilerParams(vmem_limit_bytes=vmem << 20),
            cost_estimate=pl.CostEstimate(
                flops=int(flops), bytes_accessed=int(moved), transcendentals=0
            ),
        )(*args)

    return run


def rotated(values, axis, step=1):
    n = lax.axis_size(axis)
    if not isinstance(values, (list, tuple)):
        values = [values] * (n // step - 1)
    return [
        lax.ppermute(value, axis, [(s, (s + k * step) % n) for s in range(n)])
        for k, value in enumerate(values, 1)
    ]


def swapped(value, axis="c", bit=1):
    return lax.ppermute(value, axis, [(s, s ^ bit) for s in range(lax.axis_size(axis))])


def per_device(tokens, cotangent, gain, w_u, w_v, w_o, local_factor, butterfly):
    x = tokens.reshape(BLK, -1)
    cot = cotangent.reshape(BLK, -1)
    gain2 = gain.reshape(1, -1)
    wide = (BLK, GROUPS * BLK)
    place = jnp.stack(
        [lax.axis_index(a) for a in ("y", "z", "c", "dp")]
    ).astype(jnp.int32)

    send = call(
        first_kernel,
        [((GROUPS, 16, 3 * PL, BLK), BF)],
        scratch=[
            pltpu.VMEM(wide, BF),
            pltpu.VMEM(wide, BF),
            pltpu.VMEM((BLK, BLK), BF),
            pltpu.VMEM((GROUPS, 16, 3 * PL, BLK), BF),
            pltpu.SemaphoreType.DMA((7,)),
        ],
        flops=1.4e8,
        moved=4e6,
        hbm=(0, 1, 3),
        hbm_out=(0,),
        vmem=58,
    )(x, cot, gain2, local_factor)[0]
    recv = lax.all_to_all(send.reshape(BLOCKS, 3 * PL, BLK), SEQ, 0, 0)

    u, act, dgd = call(
        side_kernel, [(wide, BF), (wide, F32), (wide, F32)], flops=4e8, moved=8e6, vmem=63
    )(x, cot, gain2, w_u, w_v, w_o)
    recv, u, act, dgd = lax.optimization_barrier((recv, u, act, dgd))

    tiled = (BLOCKS, 2, 2, 8, 128)
    quarter = (25, 8, 128)
    back, keep, give = call(
        mid_kernel,
        [((BLOCKS, 2 * PL, BLK), BF), ((4,) + quarter, F32), ((4,) + quarter, BF)],
        scratch=[
            pltpu.VMEM((BLOCKS, 3 * PL, BLK), BF),
            pltpu.VMEM((BLOCKS, 2 * PL, BLK), BF),
            pltpu.VMEM(butterfly.shape[:3] + (BLK,), F32),
            pltpu.VMEM((BLK, BLK), BF),
            pltpu.VMEM((BLK, BLK), BF),
            pltpu.VMEM((BLK, BLK), BF),
            pltpu.VMEM(tiled, F32),
            pltpu.VMEM(tiled, F32),
            pltpu.VMEM(tiled, F32),
            pltpu.VMEM((BLOCKS * PL, BLK), F32),
            pltpu.VMEM((BLOCKS * PL, BLK), F32),
            pltpu.VMEM((24, 2, 8, 128), F32),
            pltpu.VMEM((24, 2, 8, 128), F32),
            pltpu.VMEM((3, BLK, BLK), F32),
            pltpu.SemaphoreType.DMA((4,)),
            pltpu.SemaphoreType.DMA((4,)),
            pltpu.SemaphoreType.DMA((4,)),
        ],
        flops=8e8,
        moved=4e6,
        vmem=63,
        smem=(0,),
        hbm=(2, 3, 4, 5),
        free=(1,),
        hbm_out=(0,),
    )(place, recv, butterfly, w_u, w_v, w_o)

    recv2 = lax.all_to_all(back, SEQ, 0, 0).reshape(GROUPS, 16, 2 * PL, BLK)

    own, *gives = call(
        core_sum_kernel, [(quarter, F32)] + [(quarter, BF)] * 3, moved=1e6, smem=(0,)
    )(place, keep, swapped(give))
    slice_ = call(quarter_sum_kernel, [(quarter, BF)], moved=3e5)(own, *rotated(gives, "y"))[0]
    for axis, bit in (("dp", 1), ("dp", 2), ("z", 1)):
        slice_ = call(pair_sum_kernel, [(quarter, BF)], moved=2e5)(
            slice_, swapped(slice_, axis, bit)
        )[0]
    got_z = rotated(slice_, "z", 2)

    recv2, got_z = lax.optimization_barrier((recv2, got_z))
    part = call(local_kernel, [((BLK, BLK), BF)], flops=1.3e8, moved=1.2e6)(recv2, u)[0]
    parts = rotated(part, "dp")
    mine_y = call(gather_kernel, [((4,) + quarter, BF)], moved=4e5, smem=(0,))(
        place, slice_, *got_z
    )[0]
    got_y = rotated(mine_y, "y")
    grad_local = call(
        ordered_sum_kernel,
        [((BLK, BLK), F32)],
        scratch=[pltpu.VMEM((4, BLK, BLK), BF)],
        moved=8e5,
        smem=(0,),
    )(place, part, *parts)[0]
    mixed, dx = call(
        last_kernel, [(wide, BF), (wide, BF)], scratch=[pltpu.VMEM(wide, F32)],
        flops=6e8, moved=8e6,
    )(recv2, x, gain2, act, dgd, w_u, w_v, w_o, local_factor)
    got_y, mixed, dx = lax.optimization_barrier((got_y, mixed, dx))
    halves = [mine_y] + got_y
    others = [swapped(half) for half in halves]
    others, grad_local = lax.optimization_barrier((others, grad_local))

    shape = (GROUPS, BLK, BLK)
    gu, gv, go, grad_gain, grad_bfly = call(
        place_kernel,
        [(shape, F32)] * 3 + [(gain2.shape, F32), (butterfly.shape, F32)],
        moved=5e6,
        smem=(0,),
    )(place, w_u, w_v, gain2, *halves, *others)

    return (
        mixed.reshape(tokens.shape),
        dx.reshape(tokens.shape),
        gu,
        gv,
        go,
        grad_gain.reshape(gain.shape),
        grad_local,
        grad_bfly,
    )


def solution(mesh):
    fine = Mesh(mesh.devices.reshape(4, 8, 4, 2), ("dp", "z", "y", "c"))
    block = P("dp", SEQ, None)
    return jax.shard_map(
        per_device,
        mesh=fine,
        in_specs=(block, block, P(), P(), P(), P(), P(SEQ, None), P()),
        out_specs=(block, block, P(), P(), P(), P(), P(SEQ, None), P()),
        check_vma=False,
    )
```

```python
import functools

import jax
import jax.numpy as jnp
from jax import lax
from jax.experimental import pallas as pl
from jax.experimental.pallas import tpu as pltpu
from jax.sharding import Mesh, PartitionSpec as P

BF = jnp.bfloat16
F32 = jnp.float32
GROUPS = 4
BLK = 256
BLOCKS = 64
PL = 16
SEQ = ("z", "y", "c")


def dot(a, b, dims):
    return lax.dot_general(a, b, (dims, ((), ())), preferred_element_type=F32)


def mm(a, b):
    return dot(a, b, ((1,), (0,)))


def mm_nt(a, b):
    return dot(a, b, ((1,), (1,)))


def mm_tn(a, b):
    return dot(a, b, ((0,), (0,)))


def lanes(g):
    return slice(g * BLK, (g + 1) * BLK)


def inv_rms(x_ref):
    total = jnp.zeros((BLK, 1), F32)
    for g in range(GROUPS):
        x = x_ref[:, lanes(g)].astype(F32)
        total = total + jnp.sum(x * x, axis=-1, keepdims=True)
    return lax.rsqrt(total * (1.0 / (GROUPS * BLK)) + 1e-06)


def first_kernel(
    x_hbm, cot_hbm, gain_ref, local_hbm, send_hbm, x_ref, cot_ref, local_ref, send_ref, sems
):
    fetches = [
        pltpu.make_async_copy(src, dst, sems.at[at])
        for at, (src, dst) in enumerate(
            ((x_hbm, x_ref), (local_hbm, local_ref), (cot_hbm, cot_ref))
        )
    ]
    made = [
        pltpu.make_async_copy(send_ref.at[g], send_hbm.at[g], sems.at[3 + g])
        for g in range(GROUPS)
    ]
    for copy in fetches:
        copy.start()

    def put(g, at, value):
        send_ref[g, :, at * PL : (at + 1) * PL, :] = value.reshape(16, PL, BLK)

    fetches[0].wait()
    r = inv_rms(x_ref)
    fetches[1].wait()
    fetches[2].wait()
    local = local_ref[...]
    for g in range(GROUPS):
        xn = (x_ref[:, lanes(g)].astype(F32) * r * gain_ref[:, lanes(g)]).astype(BF)
        put(g, 0, mm(local, xn).astype(BF))
        put(g, 1, xn)
        put(g, 2, cot_ref[:, lanes(g)])
        made[g].start()
    for copy in made:
        copy.wait()


def side_kernel(x_ref, cot_ref, gain_ref, wu_ref, wv_ref, wo_ref, u_ref, act_ref, dgd_ref):
    r = inv_rms(x_ref)
    for g in range(GROUPS):
        xn = (x_ref[:, lanes(g)].astype(F32) * r * gain_ref[:, lanes(g)]).astype(BF)
        u_ref[:, lanes(g)] = mm(xn, wu_ref[g]).astype(BF)
        v = mm(xn, wv_ref[g])
        sig = jax.nn.sigmoid(v)
        act_ref[:, lanes(g)] = v * sig
        dg = mm_nt(cot_ref[:, lanes(g)], wo_ref[g])
        dgd_ref[:, lanes(g)] = dg * (sig * (1.0 + v * (1.0 - sig)))


def tiles_of(value):
    split = value.reshape(16, 2, 8, BLK)
    return split[..., :128], split[..., 128:]


def from_tiles(ref, at):
    part = ref[pl.ds(at * 16, 16)]
    return jnp.concatenate([part[:, :, 0], part[:, :, 1]], axis=-1).reshape(BLK, BLK)


def mid_kernel(
    place_ref, recv_hbm, coef_hbm, wu_hbm, wv_hbm, wo_hbm,
    send_hbm, keep_ref, give_ref,
    recv_ref, send_ref, coef_ref, wu_ref, wv_ref, wo_ref,
    z0, zs, es, act_s, dgd_s, coef, acc, gsum, in_sems, out_sems, sems,
):
    group = place_ref[1] >> 1

    def fetch(at):
        here = pl.ds(at * 16, 16)
        return pltpu.make_async_copy(recv_hbm.at[here], recv_ref.at[here], in_sems.at[at])

    def deliver(at):
        here = pl.ds(at * 16, 16)
        return pltpu.make_async_copy(send_ref.at[here], send_hbm.at[here], out_sems.at[at])

    mine = pl.ds(pl.multiple_of(group * BLK, BLK), BLK)
    weights = [
        pltpu.make_async_copy(src.at[group], dst, sems.at[at])
        for at, (src, dst) in enumerate(
            ((wu_hbm, wu_ref), (wv_hbm, wv_ref), (wo_hbm, wo_ref))
        )
    ]
    coefs = pltpu.make_async_copy(coef_hbm.at[:, :, :, mine], coef_ref, sems.at[3])
    for copy in (fetch(0), *weights, coefs, fetch(1), fetch(2), fetch(3)):
        copy.start()
    acc[...] = jnp.zeros_like(acc)
    gsum[...] = jnp.zeros_like(gsum)
    coefs.wait()
    for row in range(24):
        for lh in range(2):
            coef[row, lh] = jnp.broadcast_to(
                coef_ref[row // 4, row // 2 % 2, row % 2 : row % 2 + 1, lh * 128 : (lh + 1) * 128],
                (8, 128),
            )
    for copy in weights:
        copy.wait()

    def rows(at, which):
        return recv_ref[pl.ds(at * 16, 16), which * PL : (which + 1) * PL, :].reshape(BLK, BLK)

    @pl.loop(0, 4, unroll=True)
    def _(at):
        fetch(at).wait()
        here = pl.ds(at * 16, 16)
        p = mm(rows(at, 0), wu_ref[...]).astype(BF).astype(F32)
        v = mm(rows(at, 1), wv_ref[...])
        dg = mm_nt(rows(at, 2), wo_ref[...])
        sig = jax.nn.sigmoid(v)
        act = v * sig
        e = (dg * act).astype(BF).astype(F32)
        act_s[pl.ds(at * BLK, BLK), :] = act
        dgd_s[pl.ds(at * BLK, BLK), :] = dg * (sig * (1.0 + v * (1.0 - sig)))
        for lh, (pt, et) in enumerate(zip(tiles_of(p), tiles_of(e))):
            z0[here, :, lh] = pt
            es[here, :, lh] = et

    def place(t):
        return t >> 2, (t >> 1) & 1, t & 1

    def forward(z, bits, lh):
        states = [z]
        for j, k in enumerate(bits):
            z = [
                coef[4 * k + 2 * (i >> j & 1), lh] * z[i]
                + coef[4 * k + 2 * (i >> j & 1) + 1, lh] * z[i ^ (1 << j)]
                for i in range(8)
            ]
            states.append(z)
        return states

    def backward(e, states, bits, lh):
        for j, k in reversed(tuple(enumerate(bits))):
            z = states[j]
            for b in range(2):
                at = [i for i in range(8) if (i >> j & 1) == b]
                acc[4 * k + 2 * b, lh] += sum(e[i] * z[i] for i in at)
                acc[4 * k + 2 * b + 1, lh] += sum(e[i] * z[i ^ (1 << j)] for i in at)
            e = [
                coef[4 * k + 2 * (i >> j & 1), lh] * e[i]
                + coef[4 * k + 2 * (1 - (i >> j & 1)) + 1, lh] * e[i ^ (1 << j)]
                for i in range(8)
            ]
        return e

    low, high = (0, 1, 2), (3, 4, 5)

    @pl.loop(0, 32, unroll=4)
    def _(t):
        hi, rh, lh = place(t)
        z = forward([z0[hi * 8 + i, rh, lh] for i in range(8)], low, lh)[-1]
        for i in range(8):
            zs[hi * 8 + i, rh, lh] = z[i]

    @pl.loop(0, 32, unroll=4)
    def _(t):
        lo, rh, lh = place(t)
        states = forward([zs[i * 8 + lo, rh, lh] for i in range(8)], high, lh)
        for i in range(8):
            zs[i * 8 + lo, rh, lh] = states[3][i]
        e = backward([es[i * 8 + lo, rh, lh] for i in range(8)], states, high, lh)
        for i in range(8):
            es[i * 8 + lo, rh, lh] = e[i]

    @pl.loop(0, 32, unroll=4)
    def _(t):
        hi, rh, lh = place(t)
        states = forward([z0[hi * 8 + i, rh, lh] for i in range(8)], low, lh)
        e = backward([es[hi * 8 + i, rh, lh] for i in range(8)], states, low, lh)
        for i in range(8):
            es[hi * 8 + i, rh, lh] = e[i]

    @pl.loop(0, 4, unroll=True)
    def _(at):
        here = pl.ds(at * 16, 16)
        z = from_tiles(zs, at).astype(BF)
        e = from_tiles(es, at).astype(BF)
        send_ref[here, :PL, :] = z.reshape(16, PL, BLK)
        send_ref[here, PL:, :] = e.reshape(16, PL, BLK)
        deliver(at).start()
        zf = z.astype(F32)
        gated = (zf * act_s[pl.ds(at * BLK, BLK), :]).astype(BF)
        dv = (zf * dgd_s[pl.ds(at * BLK, BLK), :]).astype(BF)
        gsum[0] += mm_tn(rows(at, 0), e)
        gsum[1] += mm_tn(rows(at, 1), dv)
        gsum[2] += mm_tn(gated, rows(at, 2))

    own = place_ref[2]
    for ref, half in ((keep_ref, own), (give_ref, 1 - own)):
        cut = pl.ds(pl.multiple_of(half * 128, 128), 128)
        for w in range(3):
            ref[:, w * 8 : (w + 1) * 8] = (
                gsum[w, :, cut].reshape(4, 8, 8, 128).astype(ref.dtype)
            )
        for part in range(3):
            sums = jnp.sum(acc[part * 8 : (part + 1) * 8, half], axis=1)
            ref[part, 24] = sums.astype(ref.dtype)
        ref[3, 24] = jnp.zeros((8, 128), ref.dtype)
    for at in range(4):
        deliver(at).wait()


def core_sum_kernel(place_ref, keep_ref, got_ref, own_ref, *give_refs):
    def piece(k):
        d = (place_ref[0] + k) & 3
        return keep_ref[d] + got_ref[d].astype(F32)

    own_ref[...] = piece(0)
    for k, ref in enumerate(give_refs, 1):
        ref[...] = piece(k).astype(BF)


def quarter_sum_kernel(own_ref, *refs):
    *got, out_ref = refs
    total = own_ref[...]
    for ref in got:
        total = total + ref[...].astype(F32)
    out_ref[...] = total.astype(BF)


def pair_sum_kernel(a_ref, b_ref, out_ref):
    out_ref[...] = (a_ref[...].astype(F32) + b_ref[...].astype(F32)).astype(out_ref.dtype)


def gather_kernel(place_ref, *refs):
    *parts, out_ref = refs
    for k, ref in enumerate(parts):
        out_ref[((place_ref[1] >> 1) + 4 - k) & 3] = ref[...]


def group_of(recv_ref, g, which):
    return recv_ref[g, :, which * PL : (which + 1) * PL, :].reshape(BLK, BLK)


def local_kernel(recv_ref, u_ref, out_ref):
    total = jnp.zeros((BLK, BLK), F32)
    for g in range(GROUPS):
        total = total + mm_nt(group_of(recv_ref, g, 1), u_ref[:, lanes(g)])
    out_ref[...] = total.astype(BF)


def last_kernel(
    recv_ref, x_ref, gain_ref, act_ref, dgd_ref, wu_ref, wv_ref, wo_ref, local_ref,
    mixed_ref, dx_ref, scaled_ref,
):
    r = inv_rms(x_ref)
    local = local_ref[...]
    inner = jnp.zeros((BLK, 1), F32)
    for g in range(GROUPS):
        z = group_of(recv_ref, g, 0).astype(F32)
        gated = (z * act_ref[:, lanes(g)]).astype(BF)
        mixed_ref[:, lanes(g)] = mm(gated, wo_ref[g]).astype(BF)
        dv = (z * dgd_ref[:, lanes(g)]).astype(BF)
        du = mm_tn(local, group_of(recv_ref, g, 1)).astype(BF)
        scaled = (mm_nt(du, wu_ref[g]) + mm_nt(dv, wv_ref[g])) * gain_ref[:, lanes(g)]
        scaled_ref[:, lanes(g)] = scaled
        inner = inner + jnp.sum(scaled * x_ref[:, lanes(g)].astype(F32), axis=-1, keepdims=True)
    shift = r * r * inner * (1.0 / (GROUPS * BLK))
    for g in range(GROUPS):
        x = x_ref[:, lanes(g)].astype(F32)
        dx_ref[:, lanes(g)] = (r * (scaled_ref[:, lanes(g)] - x * shift)).astype(BF)


def place_kernel(place_ref, wu_ref, wv_ref, gain_ref, *refs):
    own, other = refs[:4], refs[4:8]
    *grads_hbm, gain_out, bfly_ref, gu_ref, gv_ref, go_ref, sems = refs[8:]
    outs = [
        pltpu.make_async_copy(src, dst, sems.at[at])
        for at, (src, dst) in enumerate(zip((gu_ref, gv_ref, go_ref), grads_hbm))
    ]
    pieces = [
        (parts[k], (place_ref[0] + 4 - k) & 3, half)
        for k in range(4)
        for parts, half in ((own, place_ref[2]), (other, 1 - place_ref[2]))
    ]
    for w, out in enumerate((gu_ref, gv_ref, go_ref)):
        for part, d, half in pieces:
            rows = pl.ds(pl.multiple_of(d * 64, 64), 64)
            cut = pl.ds(pl.multiple_of(half * 128, 128), 128)
            out[:, rows, cut] = (
                part[:, w * 8 : (w + 1) * 8].astype(F32).reshape(GROUPS, 64, 128)
            )
        outs[w].start()
    for part, d, half in pieces:

        @pl.when(d < 3)
        def _(part=part, d=d, half=half):
            for g in range(GROUPS):
                wide = pl.ds(pl.multiple_of(g * BLK + half * 128, 128), 128)
                tile = part[g, 24].astype(F32)
                for s in range(8):
                    bfly_ref[2 * d + s // 4, s // 2 % 2, s % 2 : s % 2 + 1, wide] = tile[s : s + 1]

    ones = jnp.ones((8, BLK), F32)
    for g in range(GROUPS):
        product = gu_ref[g] * wu_ref[g].astype(F32) + gv_ref[g] * wv_ref[g].astype(F32)
        sums = lax.dot_general(
            ones, product, (((1,), (1,)), ((), ())),
            precision=lax.Precision.HIGHEST, preferred_element_type=F32,
        )
        gain_out[:, lanes(g)] = sums[:1] / gain_ref[:, lanes(g)]
    for copy in outs:
        copy.wait()


def call(kernel, outs, scratch=(), flops=0, moved=0, vmem=24, smem=(), hbm=(), hbm_out=(), free=()):
    shapes = [jax.ShapeDtypeStruct(shape, dtype) for shape, dtype in outs]
    whole = pl.BlockSpec(memory_space=pltpu.VMEM)

    def run(*args):
        specs = [whole] * len(args)
        for at in smem:
            specs[at] = pl.BlockSpec(memory_space=pltpu.SMEM)
        for at in hbm:
            specs[at] = pl.BlockSpec(memory_space=pltpu.HBM)
        for at in free:
            specs[at] = pl.BlockSpec(memory_space=pl.ANY)
        return pl.pallas_call(
            kernel,
            out_shape=shapes,
            in_specs=specs,
            out_specs=[
                pl.BlockSpec(memory_space=pltpu.HBM) if at in hbm_out else whole
                for at in range(len(shapes))
            ],
            scratch_shapes=list(scratch),
            compiler_params=pltpu.CompilerParams(vmem_limit_bytes=vmem << 20),
            cost_estimate=pl.CostEstimate(
                flops=int(flops), bytes_accessed=int(moved), transcendentals=0
            ),
        )(*args)

    return run


def rotated(values, axis, step=1):
    n = lax.axis_size(axis)
    if not isinstance(values, (list, tuple)):
        values = [values] * (n // step - 1)
    return [
        lax.ppermute(value, axis, [(s, (s + k * step) % n) for s in range(n)])
        for k, value in enumerate(values, 1)
    ]


def swapped(value, axis="c", bit=1):
    return lax.ppermute(value, axis, [(s, s ^ bit) for s in range(lax.axis_size(axis))])


def per_device(tokens, cotangent, gain, w_u, w_v, w_o, local_factor, butterfly):
    x = tokens.reshape(BLK, -1)
    cot = cotangent.reshape(BLK, -1)
    gain2 = gain.reshape(1, -1)
    wide = (BLK, GROUPS * BLK)
    place = jnp.stack(
        [lax.axis_index(a) for a in ("y", "z", "c")]
    ).astype(jnp.int32)

    send = call(
        first_kernel,
        [((GROUPS, 16, 3 * PL, BLK), BF)],
        scratch=[
            pltpu.VMEM(wide, BF),
            pltpu.VMEM(wide, BF),
            pltpu.VMEM((BLK, BLK), BF),
            pltpu.VMEM((GROUPS, 16, 3 * PL, BLK), BF),
            pltpu.SemaphoreType.DMA((7,)),
        ],
        flops=1.4e8,
        moved=4e6,
        hbm=(0, 1, 3),
        hbm_out=(0,),
        vmem=58,
    )(x, cot, gain2, local_factor)[0]
    recv = lax.all_to_all(send.reshape(BLOCKS, 3 * PL, BLK), SEQ, 0, 0)

    u, act, dgd = call(
        side_kernel, [(wide, BF), (wide, F32), (wide, F32)], flops=4e8, moved=8e6, vmem=63
    )(x, cot, gain2, w_u, w_v, w_o)
    recv, u, act, dgd = lax.optimization_barrier((recv, u, act, dgd))

    tiled = (BLOCKS, 2, 2, 8, 128)
    quarter = (25, 8, 128)
    back, keep, give = call(
        mid_kernel,
        [((BLOCKS, 2 * PL, BLK), BF), ((4,) + quarter, F32), ((4,) + quarter, BF)],
        scratch=[
            pltpu.VMEM((BLOCKS, 3 * PL, BLK), BF),
            pltpu.VMEM((BLOCKS, 2 * PL, BLK), BF),
            pltpu.VMEM(butterfly.shape[:3] + (BLK,), F32),
            pltpu.VMEM((BLK, BLK), BF),
            pltpu.VMEM((BLK, BLK), BF),
            pltpu.VMEM((BLK, BLK), BF),
            pltpu.VMEM(tiled, F32),
            pltpu.VMEM(tiled, F32),
            pltpu.VMEM(tiled, F32),
            pltpu.VMEM((BLOCKS * PL, BLK), F32),
            pltpu.VMEM((BLOCKS * PL, BLK), F32),
            pltpu.VMEM((24, 2, 8, 128), F32),
            pltpu.VMEM((24, 2, 8, 128), F32),
            pltpu.VMEM((3, BLK, BLK), F32),
            pltpu.SemaphoreType.DMA((4,)),
            pltpu.SemaphoreType.DMA((4,)),
            pltpu.SemaphoreType.DMA((4,)),
        ],
        flops=8e8,
        moved=4e6,
        vmem=63,
        smem=(0,),
        hbm=(2, 3, 4, 5),
        free=(1,),
        hbm_out=(0,),
    )(place, recv, butterfly, w_u, w_v, w_o)

    recv2 = lax.all_to_all(back, SEQ, 0, 0).reshape(GROUPS, 16, 2 * PL, BLK)

    own, *gives = call(
        core_sum_kernel, [(quarter, F32)] + [(quarter, BF)] * 3, moved=1e6, smem=(0,)
    )(place, keep, swapped(give))
    slice_ = call(quarter_sum_kernel, [(quarter, BF)], moved=3e5)(own, *rotated(gives, "y"))[0]
    for axis, bit in (("dp", 1), ("dp", 2), ("z", 1)):
        slice_ = call(pair_sum_kernel, [(quarter, BF)], moved=2e5)(
            slice_, swapped(slice_, axis, bit)
        )[0]
    got_z = rotated(slice_, "z", 2)

    recv2, slice_ = lax.optimization_barrier((recv2, slice_))
    part = call(local_kernel, [((BLK, BLK), BF)], flops=1.3e8, moved=1.2e6)(recv2, u)[0]
    got_z, part = lax.optimization_barrier((got_z, part))
    pair = call(pair_sum_kernel, [((BLK, BLK), BF)], moved=4e5)(part, swapped(part, "dp", 1))[0]
    other_pair = swapped(pair, "dp", 2)
    mine_y = call(gather_kernel, [((4,) + quarter, BF)], moved=4e5, smem=(0,))(
        place, slice_, *got_z
    )[0]
    got_y = rotated(mine_y, "y")
    grad_local = call(pair_sum_kernel, [((BLK, BLK), F32)], moved=5e5)(pair, other_pair)[0]
    mixed, dx = call(
        last_kernel, [(wide, BF), (wide, BF)], scratch=[pltpu.VMEM(wide, F32)],
        flops=6e8, moved=8e6,
    )(recv2, x, gain2, act, dgd, w_u, w_v, w_o, local_factor)
    got_y, mixed, dx, pair = lax.optimization_barrier((got_y, mixed, dx, pair))
    halves = [mine_y] + got_y
    others = [swapped(half) for half in halves]
    others, grad_local = lax.optimization_barrier((others, grad_local))

    shape = (GROUPS, BLK, BLK)
    gu, gv, go, grad_gain, grad_bfly = call(
        place_kernel,
        [(shape, F32)] * 3 + [(gain2.shape, F32), (butterfly.shape, F32)],
        scratch=[pltpu.VMEM(shape, F32)] * 3 + [pltpu.SemaphoreType.DMA((3,))],
        moved=5e6,
        smem=(0,),
        hbm_out=(0, 1, 2),
    )(place, w_u, w_v, gain2, *halves, *others)

    return (
        mixed.reshape(tokens.shape),
        dx.reshape(tokens.shape),
        gu,
        gv,
        go,
        grad_gain.reshape(gain.shape),
        grad_local,
        grad_bfly,
    )


def solution(mesh):
    fine = Mesh(mesh.devices.reshape(4, 8, 4, 2), ("dp", "z", "y", "c"))
    block = P("dp", SEQ, None)
    return jax.shard_map(
        per_device,
        mesh=fine,
        in_specs=(block, block, P(), P(), P(), P(), P(SEQ, None), P()),
        out_specs=(block, block, P(), P(), P(), P(), P(SEQ, None), P()),
        check_vma=False,
    )
```

```python
import functools

import jax
import jax.numpy as jnp
from jax import lax
from jax.experimental import pallas as pl
from jax.experimental.pallas import tpu as pltpu
from jax.sharding import Mesh, PartitionSpec as P

BF = jnp.bfloat16
F32 = jnp.float32
GROUPS = 4
BLK = 256
BLOCKS = 64
PL = 16
SEQ = ("z", "y", "c")


def dot(a, b, dims):
    return lax.dot_general(a, b, (dims, ((), ())), preferred_element_type=F32)


def mm(a, b):
    return dot(a, b, ((1,), (0,)))


def mm_nt(a, b):
    return dot(a, b, ((1,), (1,)))


def mm_tn(a, b):
    return dot(a, b, ((0,), (0,)))


def lanes(g):
    return slice(g * BLK, (g + 1) * BLK)


def inv_rms(x_ref):
    total = jnp.zeros((BLK, 1), F32)
    for g in range(GROUPS):
        x = x_ref[:, lanes(g)].astype(F32)
        total = total + jnp.sum(x * x, axis=-1, keepdims=True)
    return lax.rsqrt(total * (1.0 / (GROUPS * BLK)) + 1e-06)


def first_kernel(
    x_hbm, cot_hbm, gain_ref, local_hbm, send_hbm, x_ref, cot_ref, local_ref, send_ref, sems
):
    fetches = [
        pltpu.make_async_copy(src, dst, sems.at[at])
        for at, (src, dst) in enumerate(
            ((x_hbm, x_ref), (local_hbm, local_ref), (cot_hbm, cot_ref))
        )
    ]
    made = [
        pltpu.make_async_copy(send_ref.at[g], send_hbm.at[g], sems.at[3 + g])
        for g in range(GROUPS)
    ]
    for copy in fetches:
        copy.start()

    def put(g, at, value):
        send_ref[g, :, at * PL : (at + 1) * PL, :] = value.reshape(16, PL, BLK)

    fetches[0].wait()
    r = inv_rms(x_ref)
    fetches[1].wait()
    fetches[2].wait()
    local = local_ref[...]
    for g in range(GROUPS):
        xn = (x_ref[:, lanes(g)].astype(F32) * r * gain_ref[:, lanes(g)]).astype(BF)
        put(g, 0, mm(local, xn).astype(BF))
        put(g, 1, xn)
        put(g, 2, cot_ref[:, lanes(g)])
        made[g].start()
    for copy in made:
        copy.wait()


def side_kernel(x_ref, cot_ref, gain_ref, wu_ref, wv_ref, wo_ref, u_ref, act_ref, dgd_ref):
    r = inv_rms(x_ref)
    for g in range(GROUPS):
        xn = (x_ref[:, lanes(g)].astype(F32) * r * gain_ref[:, lanes(g)]).astype(BF)
        u_ref[:, lanes(g)] = mm(xn, wu_ref[g]).astype(BF)
        v = mm(xn, wv_ref[g])
        sig = jax.nn.sigmoid(v)
        act_ref[:, lanes(g)] = v * sig
        dg = mm_nt(cot_ref[:, lanes(g)], wo_ref[g])
        dgd_ref[:, lanes(g)] = dg * (sig * (1.0 + v * (1.0 - sig)))


def tiles_of(value):
    split = value.reshape(16, 2, 8, BLK)
    return split[..., :128], split[..., 128:]


def from_tiles(ref, at):
    part = ref[pl.ds(at * 16, 16)]
    return jnp.concatenate([part[:, :, 0], part[:, :, 1]], axis=-1).reshape(BLK, BLK)


def mid_kernel(
    place_ref, recv_hbm, coef_hbm, wu_hbm, wv_hbm, wo_hbm,
    send_hbm, keep_ref, give_ref,
    recv_ref, send_ref, coef_ref, wu_ref, wv_ref, wo_ref,
    z0, zs, es, act_s, dgd_s, coef, acc, gsum, in_sems, out_sems, sems,
):
    group = place_ref[1] >> 1

    def fetch(at):
        here = pl.ds(at * 16, 16)
        return pltpu.make_async_copy(recv_hbm.at[here], recv_ref.at[here], in_sems.at[at])

    def deliver(at):
        here = pl.ds(at * 16, 16)
        return pltpu.make_async_copy(send_ref.at[here], send_hbm.at[here], out_sems.at[at])

    mine = pl.ds(pl.multiple_of(group * BLK, BLK), BLK)
    weights = [
        pltpu.make_async_copy(src.at[group], dst, sems.at[at])
        for at, (src, dst) in enumerate(
            ((wu_hbm, wu_ref), (wv_hbm, wv_ref), (wo_hbm, wo_ref))
        )
    ]
    coefs = pltpu.make_async_copy(coef_hbm.at[:, :, :, mine], coef_ref, sems.at[3])
    for copy in (fetch(0), *weights, coefs, fetch(1), fetch(2), fetch(3)):
        copy.start()
    acc[...] = jnp.zeros_like(acc)
    gsum[...] = jnp.zeros_like(gsum)
    coefs.wait()
    for row in range(24):
        for lh in range(2):
            coef[row, lh] = jnp.broadcast_to(
                coef_ref[row // 4, row // 2 % 2, row % 2 : row % 2 + 1, lh * 128 : (lh + 1) * 128],
                (8, 128),
            )
    for copy in weights:
        copy.wait()

    def rows(at, which):
        return recv_ref[pl.ds(at * 16, 16), which * PL : (which + 1) * PL, :].reshape(BLK, BLK)

    @pl.loop(0, 4, unroll=True)
    def _(at):
        fetch(at).wait()
        here = pl.ds(at * 16, 16)
        p = mm(rows(at, 0), wu_ref[...]).astype(BF).astype(F32)
        v = mm(rows(at, 1), wv_ref[...])
        dg = mm_nt(rows(at, 2), wo_ref[...])
        sig = jax.nn.sigmoid(v)
        act = v * sig
        e = (dg * act).astype(BF).astype(F32)
        act_s[pl.ds(at * BLK, BLK), :] = act
        dgd_s[pl.ds(at * BLK, BLK), :] = dg * (sig * (1.0 + v * (1.0 - sig)))
        for lh, (pt, et) in enumerate(zip(tiles_of(p), tiles_of(e))):
            z0[here, :, lh] = pt
            es[here, :, lh] = et

    def place(t):
        return t >> 2, (t >> 1) & 1, t & 1

    def forward(z, bits, lh):
        states = [z]
        for j, k in enumerate(bits):
            z = [
                coef[4 * k + 2 * (i >> j & 1), lh] * z[i]
                + coef[4 * k + 2 * (i >> j & 1) + 1, lh] * z[i ^ (1 << j)]
                for i in range(8)
            ]
            states.append(z)
        return states

    def backward(e, states, bits, lh):
        for j, k in reversed(tuple(enumerate(bits))):
            z = states[j]
            for b in range(2):
                at = [i for i in range(8) if (i >> j & 1) == b]
                acc[4 * k + 2 * b, lh] += sum(e[i] * z[i] for i in at)
                acc[4 * k + 2 * b + 1, lh] += sum(e[i] * z[i ^ (1 << j)] for i in at)
            e = [
                coef[4 * k + 2 * (i >> j & 1), lh] * e[i]
                + coef[4 * k + 2 * (1 - (i >> j & 1)) + 1, lh] * e[i ^ (1 << j)]
                for i in range(8)
            ]
        return e

    low, high = (0, 1, 2), (3, 4, 5)

    @pl.loop(0, 32, unroll=4)
    def _(t):
        hi, rh, lh = place(t)
        z = forward([z0[hi * 8 + i, rh, lh] for i in range(8)], low, lh)[-1]
        for i in range(8):
            zs[hi * 8 + i, rh, lh] = z[i]

    @pl.loop(0, 32, unroll=4)
    def _(t):
        lo, rh, lh = place(t)
        states = forward([zs[i * 8 + lo, rh, lh] for i in range(8)], high, lh)
        for i in range(8):
            zs[i * 8 + lo, rh, lh] = states[3][i]
        e = backward([es[i * 8 + lo, rh, lh] for i in range(8)], states, high, lh)
        for i in range(8):
            es[i * 8 + lo, rh, lh] = e[i]

    @pl.loop(0, 32, unroll=4)
    def _(t):
        hi, rh, lh = place(t)
        states = forward([z0[hi * 8 + i, rh, lh] for i in range(8)], low, lh)
        e = backward([es[hi * 8 + i, rh, lh] for i in range(8)], states, low, lh)
        for i in range(8):
            es[hi * 8 + i, rh, lh] = e[i]

    @pl.loop(0, 4, unroll=True)
    def _(at):
        here = pl.ds(at * 16, 16)
        z = from_tiles(zs, at).astype(BF)
        e = from_tiles(es, at).astype(BF)
        send_ref[here, :PL, :] = z.reshape(16, PL, BLK)
        send_ref[here, PL:, :] = e.reshape(16, PL, BLK)
        deliver(at).start()
        zf = z.astype(F32)
        gated = (zf * act_s[pl.ds(at * BLK, BLK), :]).astype(BF)
        dv = (zf * dgd_s[pl.ds(at * BLK, BLK), :]).astype(BF)
        gsum[0] += mm_tn(rows(at, 0), e)
        gsum[1] += mm_tn(rows(at, 1), dv)
        gsum[2] += mm_tn(gated, rows(at, 2))

    own = place_ref[2]
    for ref, half in ((keep_ref, own), (give_ref, 1 - own)):
        cut = pl.ds(pl.multiple_of(half * 128, 128), 128)
        for w in range(3):
            ref[:, w * 8 : (w + 1) * 8] = (
                gsum[w, :, cut].reshape(4, 8, 8, 128).astype(ref.dtype)
            )
        for part in range(3):
            sums = jnp.sum(acc[part * 8 : (part + 1) * 8, half], axis=1)
            ref[part, 24] = sums.astype(ref.dtype)
        ref[3, 24] = jnp.zeros((8, 128), ref.dtype)
    for at in range(4):
        deliver(at).wait()


def core_sum_kernel(place_ref, keep_ref, got_ref, own_ref, *give_refs):
    def piece(k):
        d = (place_ref[0] + k) & 3
        return keep_ref[d] + got_ref[d].astype(F32)

    own_ref[...] = piece(0)
    for k, ref in enumerate(give_refs, 1):
        ref[...] = piece(k).astype(BF)


def quarter_sum_kernel(own_ref, *refs):
    *got, out_ref = refs
    total = own_ref[...]
    for ref in got:
        total = total + ref[...].astype(F32)
    out_ref[...] = total.astype(BF)


def pair_sum_kernel(a_ref, b_ref, out_ref):
    out_ref[...] = (a_ref[...].astype(F32) + b_ref[...].astype(F32)).astype(out_ref.dtype)


def gather_kernel(place_ref, *refs):
    *parts, out_ref = refs
    for k, ref in enumerate(parts):
        out_ref[((place_ref[1] >> 1) + 4 - k) & 3] = ref[...]


def group_of(recv_ref, g, which):
    return recv_ref[g, :, which * PL : (which + 1) * PL, :].reshape(BLK, BLK)


def local_kernel(recv_ref, u_ref, out_ref):
    total = jnp.zeros((BLK, BLK), F32)
    for g in range(GROUPS):
        total = total + mm_nt(group_of(recv_ref, g, 1), u_ref[:, lanes(g)])
    out_ref[...] = total.astype(BF)


def last_kernel(
    recv_ref, x_ref, gain_ref, act_ref, dgd_ref, wu_ref, wv_ref, wo_ref, local_ref,
    mixed_ref, dx_ref, scaled_ref,
):
    r = inv_rms(x_ref)
    local = local_ref[...]
    inner = jnp.zeros((BLK, 1), F32)
    for g in range(GROUPS):
        z = group_of(recv_ref, g, 0).astype(F32)
        gated = (z * act_ref[:, lanes(g)]).astype(BF)
        mixed_ref[:, lanes(g)] = mm(gated, wo_ref[g]).astype(BF)
        dv = (z * dgd_ref[:, lanes(g)]).astype(BF)
        du = mm_tn(local, group_of(recv_ref, g, 1)).astype(BF)
        scaled = (mm_nt(du, wu_ref[g]) + mm_nt(dv, wv_ref[g])) * gain_ref[:, lanes(g)]
        scaled_ref[:, lanes(g)] = scaled
        inner = inner + jnp.sum(scaled * x_ref[:, lanes(g)].astype(F32), axis=-1, keepdims=True)
    shift = r * r * inner * (1.0 / (GROUPS * BLK))
    for g in range(GROUPS):
        x = x_ref[:, lanes(g)].astype(F32)
        dx_ref[:, lanes(g)] = (r * (scaled_ref[:, lanes(g)] - x * shift)).astype(BF)


def place_kernel(place_ref, wu_ref, wv_ref, gain_ref, *refs):
    own, other = refs[:4], refs[4:8]
    gu_ref, gv_ref, go_ref, gain_out, bfly_ref = refs[8:]
    pieces = [
        (parts[k], (place_ref[0] + 4 - k) & 3, half)
        for k in range(4)
        for parts, half in ((own, place_ref[2]), (other, 1 - place_ref[2]))
    ]
    for part, d, half in pieces:
        for w, out in enumerate((gu_ref, gv_ref, go_ref)):
            rows = pl.ds(pl.multiple_of(d * 64, 64), 64)
            cut = pl.ds(pl.multiple_of(half * 128, 128), 128)
            out[:, rows, cut] = (
                part[:, w * 8 : (w + 1) * 8].astype(F32).reshape(GROUPS, 64, 128)
            )
    for part, d, half in pieces:

        @pl.when(d < 3)
        def _(part=part, d=d, half=half):
            for g in range(GROUPS):
                wide = pl.ds(pl.multiple_of(g * BLK + half * 128, 128), 128)
                tile = part[g, 24].astype(F32)
                for s in range(8):
                    bfly_ref[2 * d + s // 4, s // 2 % 2, s % 2 : s % 2 + 1, wide] = tile[s : s + 1]

    ones = jnp.ones((8, BLK), F32)
    for g in range(GROUPS):
        product = gu_ref[g] * wu_ref[g].astype(F32) + gv_ref[g] * wv_ref[g].astype(F32)
        sums = lax.dot_general(
            ones, product, (((1,), (1,)), ((), ())),
            precision=lax.Precision.HIGHEST, preferred_element_type=F32,
        )
        gain_out[:, lanes(g)] = sums[:1] / gain_ref[:, lanes(g)]


def call(kernel, outs, scratch=(), flops=0, moved=0, vmem=24, smem=(), hbm=(), hbm_out=(), free=()):
    shapes = [jax.ShapeDtypeStruct(shape, dtype) for shape, dtype in outs]
    whole = pl.BlockSpec(memory_space=pltpu.VMEM)

    def run(*args):
        specs = [whole] * len(args)
        for at in smem:
            specs[at] = pl.BlockSpec(memory_space=pltpu.SMEM)
        for at in hbm:
            specs[at] = pl.BlockSpec(memory_space=pltpu.HBM)
        for at in free:
            specs[at] = pl.BlockSpec(memory_space=pl.ANY)
        return pl.pallas_call(
            kernel,
            out_shape=shapes,
            in_specs=specs,
            out_specs=[
                pl.BlockSpec(memory_space=pltpu.HBM) if at in hbm_out else whole
                for at in range(len(shapes))
            ],
            scratch_shapes=list(scratch),
            compiler_params=pltpu.CompilerParams(vmem_limit_bytes=vmem << 20),
            cost_estimate=pl.CostEstimate(
                flops=int(flops), bytes_accessed=int(moved), transcendentals=0
            ),
        )(*args)

    return run


def rotated(values, axis, step=1):
    n = lax.axis_size(axis)
    if not isinstance(values, (list, tuple)):
        values = [values] * (n // step - 1)
    return [
        lax.ppermute(value, axis, [(s, (s + k * step) % n) for s in range(n)])
        for k, value in enumerate(values, 1)
    ]


def swapped(value, axis="c", bit=1):
    return lax.ppermute(value, axis, [(s, s ^ bit) for s in range(lax.axis_size(axis))])


def per_device(tokens, cotangent, gain, w_u, w_v, w_o, local_factor, butterfly):
    x = tokens.reshape(BLK, -1)
    cot = cotangent.reshape(BLK, -1)
    gain2 = gain.reshape(1, -1)
    wide = (BLK, GROUPS * BLK)
    place = jnp.stack(
        [lax.axis_index(a) for a in ("y", "z", "c")]
    ).astype(jnp.int32)

    send = call(
        first_kernel,
        [((GROUPS, 16, 3 * PL, BLK), BF)],
        scratch=[
            pltpu.VMEM(wide, BF),
            pltpu.VMEM(wide, BF),
            pltpu.VMEM((BLK, BLK), BF),
            pltpu.VMEM((GROUPS, 16, 3 * PL, BLK), BF),
            pltpu.SemaphoreType.DMA((7,)),
        ],
        flops=1.4e8,
        moved=4e6,
        hbm=(0, 1, 3),
        hbm_out=(0,),
        vmem=58,
    )(x, cot, gain2, local_factor)[0]
    recv = lax.all_to_all(send.reshape(BLOCKS, 3 * PL, BLK), SEQ, 0, 0)

    u, act, dgd = call(
        side_kernel, [(wide, BF), (wide, F32), (wide, F32)], flops=4e8, moved=8e6, vmem=63
    )(x, cot, gain2, w_u, w_v, w_o)
    recv, u, act, dgd = lax.optimization_barrier((recv, u, act, dgd))

    tiled = (BLOCKS, 2, 2, 8, 128)
    quarter = (25, 8, 128)
    back, keep, give = call(
        mid_kernel,
        [((BLOCKS, 2 * PL, BLK), BF), ((4,) + quarter, F32), ((4,) + quarter, BF)],
        scratch=[
            pltpu.VMEM((BLOCKS, 3 * PL, BLK), BF),
            pltpu.VMEM((BLOCKS, 2 * PL, BLK), BF),
            pltpu.VMEM(butterfly.shape[:3] + (BLK,), F32),
            pltpu.VMEM((BLK, BLK), BF),
            pltpu.VMEM((BLK, BLK), BF),
            pltpu.VMEM((BLK, BLK), BF),
            pltpu.VMEM(tiled, F32),
            pltpu.VMEM(tiled, F32),
            pltpu.VMEM(tiled, F32),
            pltpu.VMEM((BLOCKS * PL, BLK), F32),
            pltpu.VMEM((BLOCKS * PL, BLK), F32),
            pltpu.VMEM((24, 2, 8, 128), F32),
            pltpu.VMEM((24, 2, 8, 128), F32),
            pltpu.VMEM((3, BLK, BLK), F32),
            pltpu.SemaphoreType.DMA((4,)),
            pltpu.SemaphoreType.DMA((4,)),
            pltpu.SemaphoreType.DMA((4,)),
        ],
        flops=8e8,
        moved=4e6,
        vmem=63,
        smem=(0,),
        hbm=(2, 3, 4, 5),
        free=(1,),
        hbm_out=(0,),
    )(place, recv, butterfly, w_u, w_v, w_o)

    recv2 = lax.all_to_all(back, SEQ, 0, 0).reshape(GROUPS, 16, 2 * PL, BLK)

    own, *gives = call(
        core_sum_kernel, [(quarter, F32)] + [(quarter, BF)] * 3, moved=1e6, smem=(0,)
    )(place, keep, swapped(give))
    slice_ = call(quarter_sum_kernel, [(quarter, BF)], moved=3e5)(own, *rotated(gives, "y"))[0]
    for axis, bit in (("dp", 1), ("dp", 2), ("z", 1)):
        slice_ = call(pair_sum_kernel, [(quarter, BF)], moved=2e5)(
            slice_, swapped(slice_, axis, bit)
        )[0]
    got_z = rotated(slice_, "z", 2)

    recv2, slice_ = lax.optimization_barrier((recv2, slice_))
    part = call(local_kernel, [((BLK, BLK), BF)], flops=1.3e8, moved=1.2e6)(recv2, u)[0]
    got_z, part = lax.optimization_barrier((got_z, part))
    pair = call(pair_sum_kernel, [((BLK, BLK), BF)], moved=4e5)(part, swapped(part, "dp", 1))[0]
    other_pair = swapped(pair, "dp", 2)
    mine_y = call(gather_kernel, [((4,) + quarter, BF)], moved=4e5, smem=(0,))(
        place, slice_, *got_z
    )[0]
    got_y = rotated(mine_y, "y")
    mixed, dx = call(
        last_kernel, [(wide, BF), (wide, BF)], scratch=[pltpu.VMEM(wide, F32)],
        flops=6e8, moved=8e6,
    )(recv2, x, gain2, act, dgd, w_u, w_v, w_o, local_factor)
    got_y, mixed, dx, pair = lax.optimization_barrier((got_y, mixed, dx, pair))
    halves = [mine_y] + got_y
    others = [swapped(half) for half in halves]

    shape = (GROUPS, BLK, BLK)
    gu, gv, go, grad_gain, grad_bfly = call(
        place_kernel,
        [(shape, F32)] * 3 + [(gain2.shape, F32), (butterfly.shape, F32)],
        moved=5e6,
        smem=(0,),
    )(place, w_u, w_v, gain2, *halves, *others)
    other_pair, grad_gain = lax.optimization_barrier((other_pair, grad_gain))
    grad_local = call(pair_sum_kernel, [((BLK, BLK), F32)], moved=5e5)(pair, other_pair)[0]

    return (
        mixed.reshape(tokens.shape),
        dx.reshape(tokens.shape),
        gu,
        gv,
        go,
        grad_gain.reshape(gain.shape),
        grad_local,
        grad_bfly,
    )


def solution(mesh):
    fine = Mesh(mesh.devices.reshape(4, 8, 4, 2), ("dp", "z", "y", "c"))
    block = P("dp", SEQ, None)
    return jax.shard_map(
        per_device,
        mesh=fine,
        in_specs=(block, block, P(), P(), P(), P(), P(SEQ, None), P()),
        out_specs=(block, block, P(), P(), P(), P(), P(SEQ, None), P()),
        check_vma=False,
    )
```

```python
import functools

import jax
import jax.numpy as jnp
from jax import lax
from jax.experimental import pallas as pl
from jax.experimental.pallas import tpu as pltpu
from jax.sharding import Mesh, PartitionSpec as P

BF = jnp.bfloat16
F32 = jnp.float32
GROUPS = 4
BLK = 256
BLOCKS = 64
PL = 16
SEQ = ("z", "y", "c")


def dot(a, b, dims):
    return lax.dot_general(a, b, (dims, ((), ())), preferred_element_type=F32)


def mm(a, b):
    return dot(a, b, ((1,), (0,)))


def mm_nt(a, b):
    return dot(a, b, ((1,), (1,)))


def mm_tn(a, b):
    return dot(a, b, ((0,), (0,)))


def lanes(g):
    return slice(g * BLK, (g + 1) * BLK)


def inv_rms(x_ref):
    total = jnp.zeros((BLK, 1), F32)
    for g in range(GROUPS):
        x = x_ref[:, lanes(g)].astype(F32)
        total = total + jnp.sum(x * x, axis=-1, keepdims=True)
    return lax.rsqrt(total * (1.0 / (GROUPS * BLK)) + 1e-06)


def first_kernel(
    x_hbm, cot_hbm, gain_ref, local_hbm, send_hbm, x_ref, cot_ref, local_ref, send_ref, sems
):
    fetches = [
        pltpu.make_async_copy(src, dst, sems.at[at])
        for at, (src, dst) in enumerate(
            ((x_hbm, x_ref), (local_hbm, local_ref), (cot_hbm, cot_ref))
        )
    ]
    made = [
        pltpu.make_async_copy(send_ref.at[g], send_hbm.at[g], sems.at[3 + g])
        for g in range(GROUPS)
    ]
    for copy in fetches:
        copy.start()

    def put(g, at, value):
        send_ref[g, :, at * PL : (at + 1) * PL, :] = value.reshape(16, PL, BLK)

    fetches[0].wait()
    r = inv_rms(x_ref)
    fetches[1].wait()
    fetches[2].wait()
    local = local_ref[...]
    for g in range(GROUPS):
        xn = (x_ref[:, lanes(g)].astype(F32) * r * gain_ref[:, lanes(g)]).astype(BF)
        put(g, 0, mm(local, xn).astype(BF))
        put(g, 1, xn)
        put(g, 2, cot_ref[:, lanes(g)])
        made[g].start()
    for copy in made:
        copy.wait()


def tiles_of(value):
    split = value.reshape(16, 2, 8, BLK)
    return split[..., :128], split[..., 128:]


def from_tiles(ref, at):
    part = ref[pl.ds(at * 16, 16)]
    return jnp.concatenate([part[:, :, 0], part[:, :, 1]], axis=-1).reshape(BLK, BLK)


def mid_kernel(
    place_ref, recv_hbm, coef_hbm, wu_hbm, wv_hbm, wo_hbm,
    send_hbm, keep_ref, give_ref,
    recv_ref, send_ref, coef_ref, wu_ref, wv_ref, wo_ref,
    z0, zs, es, act_s, dgd_s, coef, acc, gsum, in_sems, out_sems, sems,
):
    group = place_ref[1] >> 1

    def fetch(at):
        here = pl.ds(at * 16, 16)
        return pltpu.make_async_copy(recv_hbm.at[here], recv_ref.at[here], in_sems.at[at])

    def deliver(at):
        here = pl.ds(at * 16, 16)
        return pltpu.make_async_copy(send_ref.at[here], send_hbm.at[here], out_sems.at[at])

    mine = pl.ds(pl.multiple_of(group * BLK, BLK), BLK)
    weights = [
        pltpu.make_async_copy(src.at[group], dst, sems.at[at])
        for at, (src, dst) in enumerate(
            ((wu_hbm, wu_ref), (wv_hbm, wv_ref), (wo_hbm, wo_ref))
        )
    ]
    coefs = pltpu.make_async_copy(coef_hbm.at[:, :, :, mine], coef_ref, sems.at[3])
    for copy in (fetch(0), *weights, coefs, fetch(1), fetch(2), fetch(3)):
        copy.start()
    acc[...] = jnp.zeros_like(acc)
    gsum[...] = jnp.zeros_like(gsum)
    coefs.wait()
    for row in range(24):
        for lh in range(2):
            coef[row, lh] = jnp.broadcast_to(
                coef_ref[row // 4, row // 2 % 2, row % 2 : row % 2 + 1, lh * 128 : (lh + 1) * 128],
                (8, 128),
            )
    for copy in weights:
        copy.wait()

    def rows(at, which):
        return recv_ref[pl.ds(at * 16, 16), which * PL : (which + 1) * PL, :].reshape(BLK, BLK)

    @pl.loop(0, 4, unroll=True)
    def _(at):
        fetch(at).wait()
        here = pl.ds(at * 16, 16)
        p = mm(rows(at, 0), wu_ref[...]).astype(BF).astype(F32)
        v = mm(rows(at, 1), wv_ref[...])
        dg = mm_nt(rows(at, 2), wo_ref[...])
        sig = jax.nn.sigmoid(v)
        act = v * sig
        e = (dg * act).astype(BF).astype(F32)
        act_s[pl.ds(at * BLK, BLK), :] = act
        dgd_s[pl.ds(at * BLK, BLK), :] = dg * (sig * (1.0 + v * (1.0 - sig)))
        for lh, (pt, et) in enumerate(zip(tiles_of(p), tiles_of(e))):
            z0[here, :, lh] = pt
            es[here, :, lh] = et

    def place(t):
        return t >> 2, (t >> 1) & 1, t & 1

    def forward(z, bits, lh):
        states = [z]
        for j, k in enumerate(bits):
            z = [
                coef[4 * k + 2 * (i >> j & 1), lh] * z[i]
                + coef[4 * k + 2 * (i >> j & 1) + 1, lh] * z[i ^ (1 << j)]
                for i in range(8)
            ]
            states.append(z)
        return states

    def backward(e, states, bits, lh):
        for j, k in reversed(tuple(enumerate(bits))):
            z = states[j]
            for b in range(2):
                at = [i for i in range(8) if (i >> j & 1) == b]
                acc[4 * k + 2 * b, lh] += sum(e[i] * z[i] for i in at)
                acc[4 * k + 2 * b + 1, lh] += sum(e[i] * z[i ^ (1 << j)] for i in at)
            e = [
                coef[4 * k + 2 * (i >> j & 1), lh] * e[i]
                + coef[4 * k + 2 * (1 - (i >> j & 1)) + 1, lh] * e[i ^ (1 << j)]
                for i in range(8)
            ]
        return e

    low, high = (0, 1, 2), (3, 4, 5)

    @pl.loop(0, 32, unroll=4)
    def _(t):
        hi, rh, lh = place(t)
        z = forward([z0[hi * 8 + i, rh, lh] for i in range(8)], low, lh)[-1]
        for i in range(8):
            zs[hi * 8 + i, rh, lh] = z[i]

    @pl.loop(0, 32, unroll=4)
    def _(t):
        lo, rh, lh = place(t)
        states = forward([zs[i * 8 + lo, rh, lh] for i in range(8)], high, lh)
        for i in range(8):
            zs[i * 8 + lo, rh, lh] = states[3][i]
        e = backward([es[i * 8 + lo, rh, lh] for i in range(8)], states, high, lh)
        for i in range(8):
            es[i * 8 + lo, rh, lh] = e[i]

    @pl.loop(0, 32, unroll=4)
    def _(t):
        hi, rh, lh = place(t)
        states = forward([z0[hi * 8 + i, rh, lh] for i in range(8)], low, lh)
        e = backward([es[hi * 8 + i, rh, lh] for i in range(8)], states, low, lh)
        for i in range(8):
            es[hi * 8 + i, rh, lh] = e[i]

    @pl.loop(0, 4, unroll=True)
    def _(at):
        here = pl.ds(at * 16, 16)
        z = from_tiles(zs, at).astype(BF)
        e = from_tiles(es, at).astype(BF)
        send_ref[here, :PL, :] = z.reshape(16, PL, BLK)
        send_ref[here, PL:, :] = e.reshape(16, PL, BLK)
        deliver(at).start()
        zf = z.astype(F32)
        gated = (zf * act_s[pl.ds(at * BLK, BLK), :]).astype(BF)
        dv = (zf * dgd_s[pl.ds(at * BLK, BLK), :]).astype(BF)
        gsum[0] += mm_tn(rows(at, 0), e)
        gsum[1] += mm_tn(rows(at, 1), dv)
        gsum[2] += mm_tn(gated, rows(at, 2))

    own = place_ref[2]
    for ref, half in ((keep_ref, own), (give_ref, 1 - own)):
        cut = pl.ds(pl.multiple_of(half * 128, 128), 128)
        for w in range(3):
            ref[:, w * 8 : (w + 1) * 8] = (
                gsum[w, :, cut].reshape(4, 8, 8, 128).astype(ref.dtype)
            )
        for part in range(3):
            sums = jnp.sum(acc[part * 8 : (part + 1) * 8, half], axis=1)
            ref[part, 24] = sums.astype(ref.dtype)
        ref[3, 24] = jnp.zeros((8, 128), ref.dtype)
    for at in range(4):
        deliver(at).wait()


def core_sum_kernel(place_ref, keep_ref, got_ref, own_ref, *give_refs):
    def piece(k):
        d = (place_ref[0] + k) & 3
        return keep_ref[d] + got_ref[d].astype(F32)

    own_ref[...] = piece(0)
    for k, ref in enumerate(give_refs, 1):
        ref[...] = piece(k).astype(BF)


def quarter_sum_kernel(own_ref, *refs):
    *got, out_ref = refs
    total = own_ref[...]
    for ref in got:
        total = total + ref[...].astype(F32)
    out_ref[...] = total.astype(BF)


def pair_sum_kernel(a_ref, b_ref, out_ref):
    out_ref[...] = (a_ref[...].astype(F32) + b_ref[...].astype(F32)).astype(out_ref.dtype)


def gather_kernel(place_ref, *refs):
    *parts, out_ref = refs
    for k, ref in enumerate(parts):
        out_ref[((place_ref[1] >> 1) + 4 - k) & 3] = ref[...]


def group_of(recv_ref, g, which):
    return recv_ref[g, :, which * PL : (which + 1) * PL, :].reshape(BLK, BLK)


def local_kernel(recv_ref, x_ref, gain_ref, wu_ref, out_ref):
    r = inv_rms(x_ref)
    total = jnp.zeros((BLK, BLK), F32)
    for g in range(GROUPS):
        xn = (x_ref[:, lanes(g)].astype(F32) * r * gain_ref[:, lanes(g)]).astype(BF)
        u = mm(xn, wu_ref[g]).astype(BF)
        total = total + mm_nt(group_of(recv_ref, g, 1), u)
    out_ref[...] = total.astype(BF)


def last_kernel(
    recv_ref, x_ref, cot_ref, gain_ref, wu_ref, wv_ref, wo_ref, local_ref,
    mixed_ref, dx_ref, scaled_ref,
):
    r = inv_rms(x_ref)
    local = local_ref[...]
    inner = jnp.zeros((BLK, 1), F32)
    for g in range(GROUPS):
        xn = (x_ref[:, lanes(g)].astype(F32) * r * gain_ref[:, lanes(g)]).astype(BF)
        v = mm(xn, wv_ref[g])
        sig = jax.nn.sigmoid(v)
        z = group_of(recv_ref, g, 0).astype(F32)
        gated = (z * (v * sig)).astype(BF)
        mixed_ref[:, lanes(g)] = mm(gated, wo_ref[g]).astype(BF)
        dg = mm_nt(cot_ref[:, lanes(g)], wo_ref[g])
        dv = (z * (dg * (sig * (1.0 + v * (1.0 - sig))))).astype(BF)
        du = mm_tn(local, group_of(recv_ref, g, 1)).astype(BF)
        scaled = (mm_nt(du, wu_ref[g]) + mm_nt(dv, wv_ref[g])) * gain_ref[:, lanes(g)]
        scaled_ref[:, lanes(g)] = scaled
        inner = inner + jnp.sum(scaled * x_ref[:, lanes(g)].astype(F32), axis=-1, keepdims=True)
    shift = r * r * inner * (1.0 / (GROUPS * BLK))
    for g in range(GROUPS):
        x = x_ref[:, lanes(g)].astype(F32)
        dx_ref[:, lanes(g)] = (r * (scaled_ref[:, lanes(g)] - x * shift)).astype(BF)


def place_kernel(place_ref, wu_ref, wv_ref, gain_ref, *refs):
    own, other = refs[:4], refs[4:8]
    gu_ref, gv_ref, go_ref, gain_out, bfly_ref = refs[8:]
    pieces = [
        (parts[k], (place_ref[0] + 4 - k) & 3, half)
        for k in range(4)
        for parts, half in ((own, place_ref[2]), (other, 1 - place_ref[2]))
    ]
    for part, d, half in pieces:
        for w, out in enumerate((gu_ref, gv_ref, go_ref)):
            rows = pl.ds(pl.multiple_of(d * 64, 64), 64)
            cut = pl.ds(pl.multiple_of(half * 128, 128), 128)
            out[:, rows, cut] = (
                part[:, w * 8 : (w + 1) * 8].astype(F32).reshape(GROUPS, 64, 128)
            )
    for part, d, half in pieces:

        @pl.when(d < 3)
        def _(part=part, d=d, half=half):
            for g in range(GROUPS):
                wide = pl.ds(pl.multiple_of(g * BLK + half * 128, 128), 128)
                tile = part[g, 24].astype(F32)
                for s in range(8):
                    bfly_ref[2 * d + s // 4, s // 2 % 2, s % 2 : s % 2 + 1, wide] = tile[s : s + 1]

    ones = jnp.ones((8, BLK), F32)
    for g in range(GROUPS):
        product = gu_ref[g] * wu_ref[g].astype(F32) + gv_ref[g] * wv_ref[g].astype(F32)
        sums = lax.dot_general(
            ones, product, (((1,), (1,)), ((), ())),
            precision=lax.Precision.HIGHEST, preferred_element_type=F32,
        )
        gain_out[:, lanes(g)] = sums[:1] / gain_ref[:, lanes(g)]


def call(kernel, outs, scratch=(), flops=0, moved=0, vmem=24, smem=(), hbm=(), hbm_out=(), free=()):
    shapes = [jax.ShapeDtypeStruct(shape, dtype) for shape, dtype in outs]
    whole = pl.BlockSpec(memory_space=pltpu.VMEM)

    def run(*args):
        specs = [whole] * len(args)
        for at in smem:
            specs[at] = pl.BlockSpec(memory_space=pltpu.SMEM)
        for at in hbm:
            specs[at] = pl.BlockSpec(memory_space=pltpu.HBM)
        for at in free:
            specs[at] = pl.BlockSpec(memory_space=pl.ANY)
        return pl.pallas_call(
            kernel,
            out_shape=shapes,
            in_specs=specs,
            out_specs=[
                pl.BlockSpec(memory_space=pltpu.HBM) if at in hbm_out else whole
                for at in range(len(shapes))
            ],
            scratch_shapes=list(scratch),
            compiler_params=pltpu.CompilerParams(vmem_limit_bytes=vmem << 20),
            cost_estimate=pl.CostEstimate(
                flops=int(flops), bytes_accessed=int(moved), transcendentals=0
            ),
        )(*args)

    return run


def rotated(values, axis, step=1):
    n = lax.axis_size(axis)
    if not isinstance(values, (list, tuple)):
        values = [values] * (n // step - 1)
    return [
        lax.ppermute(value, axis, [(s, (s + k * step) % n) for s in range(n)])
        for k, value in enumerate(values, 1)
    ]


def swapped(value, axis="c", bit=1):
    return lax.ppermute(value, axis, [(s, s ^ bit) for s in range(lax.axis_size(axis))])


def per_device(tokens, cotangent, gain, w_u, w_v, w_o, local_factor, butterfly):
    x = tokens.reshape(BLK, -1)
    cot = cotangent.reshape(BLK, -1)
    gain2 = gain.reshape(1, -1)
    wide = (BLK, GROUPS * BLK)
    place = jnp.stack(
        [lax.axis_index(a) for a in ("y", "z", "c")]
    ).astype(jnp.int32)

    send = call(
        first_kernel,
        [((GROUPS, 16, 3 * PL, BLK), BF)],
        scratch=[
            pltpu.VMEM(wide, BF),
            pltpu.VMEM(wide, BF),
            pltpu.VMEM((BLK, BLK), BF),
            pltpu.VMEM((GROUPS, 16, 3 * PL, BLK), BF),
            pltpu.SemaphoreType.DMA((7,)),
        ],
        flops=1.4e8,
        moved=4e6,
        hbm=(0, 1, 3),
        hbm_out=(0,),
        vmem=58,
    )(x, cot, gain2, local_factor)[0]
    recv = lax.all_to_all(send.reshape(BLOCKS, 3 * PL, BLK), SEQ, 0, 0)

    tiled = (BLOCKS, 2, 2, 8, 128)
    quarter = (25, 8, 128)
    back, keep, give = call(
        mid_kernel,
        [((BLOCKS, 2 * PL, BLK), BF), ((4,) + quarter, F32), ((4,) + quarter, BF)],
        scratch=[
            pltpu.VMEM((BLOCKS, 3 * PL, BLK), BF),
            pltpu.VMEM((BLOCKS, 2 * PL, BLK), BF),
            pltpu.VMEM(butterfly.shape[:3] + (BLK,), F32),
            pltpu.VMEM((BLK, BLK), BF),
            pltpu.VMEM((BLK, BLK), BF),
            pltpu.VMEM((BLK, BLK), BF),
            pltpu.VMEM(tiled, F32),
            pltpu.VMEM(tiled, F32),
            pltpu.VMEM(tiled, F32),
            pltpu.VMEM((BLOCKS * PL, BLK), F32),
            pltpu.VMEM((BLOCKS * PL, BLK), F32),
            pltpu.VMEM((24, 2, 8, 128), F32),
            pltpu.VMEM((24, 2, 8, 128), F32),
            pltpu.VMEM((3, BLK, BLK), F32),
            pltpu.SemaphoreType.DMA((4,)),
            pltpu.SemaphoreType.DMA((4,)),
            pltpu.SemaphoreType.DMA((4,)),
        ],
        flops=8e8,
        moved=4e6,
        vmem=63,
        smem=(0,),
        hbm=(2, 3, 4, 5),
        free=(1,),
        hbm_out=(0,),
    )(place, recv, butterfly, w_u, w_v, w_o)

    recv2 = lax.all_to_all(back, SEQ, 0, 0).reshape(GROUPS, 16, 2 * PL, BLK)

    own, *gives = call(
        core_sum_kernel, [(quarter, F32)] + [(quarter, BF)] * 3, moved=1e6, smem=(0,)
    )(place, keep, swapped(give))
    slice_ = call(quarter_sum_kernel, [(quarter, BF)], moved=3e5)(own, *rotated(gives, "y"))[0]
    for axis, bit in (("dp", 1), ("dp", 2), ("z", 1)):
        slice_ = call(pair_sum_kernel, [(quarter, BF)], moved=2e5)(
            slice_, swapped(slice_, axis, bit)
        )[0]
    got_z = rotated(slice_, "z", 2)

    recv2, slice_ = lax.optimization_barrier((recv2, slice_))
    part = call(local_kernel, [((BLK, BLK), BF)], flops=1.3e8, moved=1.2e6)(
        recv2, x, gain2, w_u
    )[0]
    got_z, part = lax.optimization_barrier((got_z, part))
    pair = call(pair_sum_kernel, [((BLK, BLK), BF)], moved=4e5)(part, swapped(part, "dp", 1))[0]
    other_pair = swapped(pair, "dp", 2)
    mine_y = call(gather_kernel, [((4,) + quarter, BF)], moved=4e5, smem=(0,))(
        place, slice_, *got_z
    )[0]
    got_y = rotated(mine_y, "y")
    mixed, dx = call(
        last_kernel, [(wide, BF), (wide, BF)], scratch=[pltpu.VMEM(wide, F32)],
        flops=6e8, moved=8e6,
    )(recv2, x, cot, gain2, w_u, w_v, w_o, local_factor)
    got_y, mixed, dx, pair = lax.optimization_barrier((got_y, mixed, dx, pair))
    halves = [mine_y] + got_y
    others = [swapped(half) for half in halves]

    shape = (GROUPS, BLK, BLK)
    gu, gv, go, grad_gain, grad_bfly = call(
        place_kernel,
        [(shape, F32)] * 3 + [(gain2.shape, F32), (butterfly.shape, F32)],
        moved=5e6,
        smem=(0,),
    )(place, w_u, w_v, gain2, *halves, *others)
    other_pair, grad_gain = lax.optimization_barrier((other_pair, grad_gain))
    grad_local = call(pair_sum_kernel, [((BLK, BLK), F32)], moved=5e5)(pair, other_pair)[0]

    return (
        mixed.reshape(tokens.shape),
        dx.reshape(tokens.shape),
        gu,
        gv,
        go,
        grad_gain.reshape(gain.shape),
        grad_local,
        grad_bfly,
    )


def solution(mesh):
    fine = Mesh(mesh.devices.reshape(4, 8, 4, 2), ("dp", "z", "y", "c"))
    block = P("dp", SEQ, None)
    return jax.shard_map(
        per_device,
        mesh=fine,
        in_specs=(block, block, P(), P(), P(), P(), P(SEQ, None), P()),
        out_specs=(block, block, P(), P(), P(), P(), P(SEQ, None), P()),
        check_vma=False,
    )
```

```python
import functools

import jax
import jax.numpy as jnp
from jax import lax
from jax.experimental import pallas as pl
from jax.experimental.pallas import tpu as pltpu
from jax.sharding import Mesh, PartitionSpec as P

BF = jnp.bfloat16
F32 = jnp.float32
GROUPS = 4
BLK = 256
BLOCKS = 64
PL = 16
SEQ = ("z", "y", "c")


def dot(a, b, dims):
    return lax.dot_general(a, b, (dims, ((), ())), preferred_element_type=F32)


def mm(a, b):
    return dot(a, b, ((1,), (0,)))


def mm_nt(a, b):
    return dot(a, b, ((1,), (1,)))


def mm_tn(a, b):
    return dot(a, b, ((0,), (0,)))


def lanes(g):
    return slice(g * BLK, (g + 1) * BLK)


def inv_rms(x_ref):
    total = jnp.zeros((BLK, 1), F32)
    for g in range(GROUPS):
        x = x_ref[:, lanes(g)].astype(F32)
        total = total + jnp.sum(x * x, axis=-1, keepdims=True)
    return lax.rsqrt(total * (1.0 / (GROUPS * BLK)) + 1e-06)


def first_kernel(
    x_hbm, cot_hbm, gain_ref, local_hbm, send_hbm, x_ref, cot_ref, local_ref, send_ref, sems
):
    fetches = [
        pltpu.make_async_copy(src, dst, sems.at[at])
        for at, (src, dst) in enumerate(
            ((x_hbm, x_ref), (local_hbm, local_ref), (cot_hbm, cot_ref))
        )
    ]
    made = [
        pltpu.make_async_copy(send_ref.at[g], send_hbm.at[g], sems.at[3 + g])
        for g in range(GROUPS)
    ]
    for copy in fetches:
        copy.start()

    def put(g, at, value):
        send_ref[g, :, at * PL : (at + 1) * PL, :] = value.reshape(16, PL, BLK)

    fetches[0].wait()
    r = inv_rms(x_ref)
    fetches[1].wait()
    fetches[2].wait()
    local = local_ref[...]
    for g in range(GROUPS):
        xn = (x_ref[:, lanes(g)].astype(F32) * r * gain_ref[:, lanes(g)]).astype(BF)
        put(g, 0, mm(local, xn).astype(BF))
        put(g, 1, xn)
        put(g, 2, cot_ref[:, lanes(g)])
        made[g].start()
    for copy in made:
        copy.wait()


def tiles_of(value):
    split = value.reshape(16, 2, 8, BLK)
    return split[..., :128], split[..., 128:]


def from_tiles(ref, at):
    part = ref[pl.ds(at * 16, 16)]
    return jnp.concatenate([part[:, :, 0], part[:, :, 1]], axis=-1).reshape(BLK, BLK)


def mid_kernel(
    place_ref, recv_hbm, coef_hbm, wu_hbm, wv_hbm, wo_hbm,
    send_hbm, keep_ref, give_ref,
    recv_ref, send_ref, coef_ref, wu_ref, wv_ref, wo_ref,
    z0, zs, es, act_s, dgd_s, coef, acc, gsum, in_sems, out_sems, sems,
):
    group = place_ref[1] >> 1

    def fetch(at):
        here = pl.ds(at * 16, 16)
        return pltpu.make_async_copy(recv_hbm.at[here], recv_ref.at[here], in_sems.at[at])

    def deliver(at):
        here = pl.ds(at * 16, 16)
        return pltpu.make_async_copy(send_ref.at[here], send_hbm.at[here], out_sems.at[at])

    mine = pl.ds(pl.multiple_of(group * BLK, BLK), BLK)
    weights = [
        pltpu.make_async_copy(src.at[group], dst, sems.at[at])
        for at, (src, dst) in enumerate(
            ((wu_hbm, wu_ref), (wv_hbm, wv_ref), (wo_hbm, wo_ref))
        )
    ]
    coefs = pltpu.make_async_copy(coef_hbm.at[:, :, :, mine], coef_ref, sems.at[3])
    for copy in (fetch(0), *weights, coefs, fetch(1), fetch(2), fetch(3)):
        copy.start()
    acc[...] = jnp.zeros_like(acc)
    gsum[...] = jnp.zeros_like(gsum)
    coefs.wait()
    for row in range(24):
        for lh in range(2):
            coef[row, lh] = jnp.broadcast_to(
                coef_ref[row // 4, row // 2 % 2, row % 2 : row % 2 + 1, lh * 128 : (lh + 1) * 128],
                (8, 128),
            )
    for copy in weights:
        copy.wait()

    def rows(at, which):
        return recv_ref[pl.ds(at * 16, 16), which * PL : (which + 1) * PL, :].reshape(BLK, BLK)

    @pl.loop(0, 4, unroll=True)
    def _(at):
        fetch(at).wait()
        here = pl.ds(at * 16, 16)
        p = mm(rows(at, 0), wu_ref[...]).astype(BF).astype(F32)
        v = mm(rows(at, 1), wv_ref[...])
        dg = mm_nt(rows(at, 2), wo_ref[...])
        sig = jax.nn.sigmoid(v)
        act = v * sig
        e = (dg * act).astype(BF).astype(F32)
        act_s[pl.ds(at * BLK, BLK), :] = act
        dgd_s[pl.ds(at * BLK, BLK), :] = dg * (sig * (1.0 + v * (1.0 - sig)))
        for lh, (pt, et) in enumerate(zip(tiles_of(p), tiles_of(e))):
            z0[here, :, lh] = pt
            es[here, :, lh] = et

    def place(t):
        return t >> 2, (t >> 1) & 1, t & 1

    def forward(z, bits, lh):
        states = [z]
        for j, k in enumerate(bits):
            z = [
                coef[4 * k + 2 * (i >> j & 1), lh] * z[i]
                + coef[4 * k + 2 * (i >> j & 1) + 1, lh] * z[i ^ (1 << j)]
                for i in range(8)
            ]
            states.append(z)
        return states

    def backward(e, states, bits, lh):
        for j, k in reversed(tuple(enumerate(bits))):
            z = states[j]
            for b in range(2):
                at = [i for i in range(8) if (i >> j & 1) == b]
                acc[4 * k + 2 * b, lh] += sum(e[i] * z[i] for i in at)
                acc[4 * k + 2 * b + 1, lh] += sum(e[i] * z[i ^ (1 << j)] for i in at)
            e = [
                coef[4 * k + 2 * (i >> j & 1), lh] * e[i]
                + coef[4 * k + 2 * (1 - (i >> j & 1)) + 1, lh] * e[i ^ (1 << j)]
                for i in range(8)
            ]
        return e

    low, high = (0, 1, 2), (3, 4, 5)

    @pl.loop(0, 32, unroll=4)
    def _(t):
        hi, rh, lh = place(t)
        z = forward([z0[hi * 8 + i, rh, lh] for i in range(8)], low, lh)[-1]
        for i in range(8):
            zs[hi * 8 + i, rh, lh] = z[i]

    @pl.loop(0, 32, unroll=4)
    def _(t):
        lo, rh, lh = place(t)
        states = forward([zs[i * 8 + lo, rh, lh] for i in range(8)], high, lh)
        for i in range(8):
            zs[i * 8 + lo, rh, lh] = states[3][i]
        e = backward([es[i * 8 + lo, rh, lh] for i in range(8)], states, high, lh)
        for i in range(8):
            es[i * 8 + lo, rh, lh] = e[i]

    @pl.loop(0, 32, unroll=4)
    def _(t):
        hi, rh, lh = place(t)
        states = forward([z0[hi * 8 + i, rh, lh] for i in range(8)], low, lh)
        e = backward([es[hi * 8 + i, rh, lh] for i in range(8)], states, low, lh)
        for i in range(8):
            es[hi * 8 + i, rh, lh] = e[i]

    @pl.loop(0, 4, unroll=True)
    def _(at):
        here = pl.ds(at * 16, 16)
        z = from_tiles(zs, at).astype(BF)
        e = from_tiles(es, at).astype(BF)
        send_ref[here, :PL, :] = z.reshape(16, PL, BLK)
        send_ref[here, PL:, :] = e.reshape(16, PL, BLK)
        deliver(at).start()
        zf = z.astype(F32)
        gated = (zf * act_s[pl.ds(at * BLK, BLK), :]).astype(BF)
        dv = (zf * dgd_s[pl.ds(at * BLK, BLK), :]).astype(BF)
        gsum[0] += mm_tn(rows(at, 0), e)
        gsum[1] += mm_tn(rows(at, 1), dv)
        gsum[2] += mm_tn(gated, rows(at, 2))

    own = place_ref[2]
    for ref, half in ((keep_ref, own), (give_ref, 1 - own)):
        cut = pl.ds(pl.multiple_of(half * 128, 128), 128)
        for w in range(3):
            ref[:, w * 8 : (w + 1) * 8] = (
                gsum[w, :, cut].reshape(4, 8, 8, 128).astype(ref.dtype)
            )
        for part in range(3):
            sums = jnp.sum(acc[part * 8 : (part + 1) * 8, half], axis=1)
            ref[part, 24] = sums.astype(ref.dtype)
        ref[3, 24] = jnp.zeros((8, 128), ref.dtype)
    for at in range(4):
        deliver(at).wait()


def core_sum_kernel(place_ref, keep_ref, got_ref, own_ref, *give_refs):
    def piece(k):
        d = (place_ref[0] + k) & 3
        return keep_ref[d] + got_ref[d].astype(F32)

    own_ref[...] = piece(0)
    for k, ref in enumerate(give_refs, 1):
        ref[...] = piece(k).astype(BF)


def quarter_sum_kernel(own_ref, *refs):
    *got, out_ref = refs
    total = own_ref[...]
    for ref in got:
        total = total + ref[...].astype(F32)
    out_ref[...] = total.astype(BF)


def pair_sum_kernel(a_ref, b_ref, out_ref):
    out_ref[...] = (a_ref[...].astype(F32) + b_ref[...].astype(F32)).astype(out_ref.dtype)


def gather_kernel(place_ref, *refs):
    *parts, out_ref = refs
    for k, ref in enumerate(parts):
        out_ref[((place_ref[1] >> 1) + 4 - k) & 3] = ref[...]


def group_of(recv_ref, g, which):
    return recv_ref[g, :, which * PL : (which + 1) * PL, :].reshape(BLK, BLK)


def local_kernel(recv_ref, x_ref, gain_ref, wu_ref, out_ref):
    r = inv_rms(x_ref)
    total = jnp.zeros((BLK, BLK), F32)
    for g in range(GROUPS):
        xn = (x_ref[:, lanes(g)].astype(F32) * r * gain_ref[:, lanes(g)]).astype(BF)
        u = mm(xn, wu_ref[g]).astype(BF)
        total = total + mm_nt(group_of(recv_ref, g, 1), u)
    out_ref[...] = total.astype(BF)


def last_kernel(
    recv_ref, x_ref, cot_ref, gain_ref, wu_ref, wv_ref, wo_ref, local_ref,
    mixed_ref, dx_ref, scaled_ref,
):
    r = inv_rms(x_ref)
    local = local_ref[...]
    inner = jnp.zeros((BLK, 1), F32)
    for g in range(GROUPS):
        xn = (x_ref[:, lanes(g)].astype(F32) * r * gain_ref[:, lanes(g)]).astype(BF)
        v = mm(xn, wv_ref[g])
        sig = jax.nn.sigmoid(v)
        z = group_of(recv_ref, g, 0).astype(F32)
        gated = (z * (v * sig)).astype(BF)
        mixed_ref[:, lanes(g)] = mm(gated, wo_ref[g]).astype(BF)
        dg = mm_nt(cot_ref[:, lanes(g)], wo_ref[g])
        dv = (z * (dg * (sig * (1.0 + v * (1.0 - sig))))).astype(BF)
        du = mm_tn(local, group_of(recv_ref, g, 1)).astype(BF)
        scaled = (mm_nt(du, wu_ref[g]) + mm_nt(dv, wv_ref[g])) * gain_ref[:, lanes(g)]
        scaled_ref[:, lanes(g)] = scaled
        inner = inner + jnp.sum(scaled * x_ref[:, lanes(g)].astype(F32), axis=-1, keepdims=True)
    shift = r * r * inner * (1.0 / (GROUPS * BLK))
    for g in range(GROUPS):
        x = x_ref[:, lanes(g)].astype(F32)
        dx_ref[:, lanes(g)] = (r * (scaled_ref[:, lanes(g)] - x * shift)).astype(BF)


def place_kernel(place_ref, wu_ref, wv_ref, gain_ref, *refs):
    own, other = refs[:4], refs[4:8]
    gu_ref, gv_ref, go_ref, gain_out, bfly_ref = refs[8:]
    pieces = [
        (parts[k], (place_ref[0] + 4 - k) & 3, half)
        for k in range(4)
        for parts, half in ((own, place_ref[2]), (other, 1 - place_ref[2]))
    ]
    for part, d, half in pieces:
        for w, out in enumerate((gu_ref, gv_ref, go_ref)):
            rows = pl.ds(pl.multiple_of(d * 64, 64), 64)
            cut = pl.ds(pl.multiple_of(half * 128, 128), 128)
            out[:, rows, cut] = (
                part[:, w * 8 : (w + 1) * 8].astype(F32).reshape(GROUPS, 64, 128)
            )
    for part, d, half in pieces:

        @pl.when(d < 3)
        def _(part=part, d=d, half=half):
            for g in range(GROUPS):
                wide = pl.ds(pl.multiple_of(g * BLK + half * 128, 128), 128)
                tile = part[g, 24].astype(F32)
                for s in range(8):
                    bfly_ref[2 * d + s // 4, s // 2 % 2, s % 2 : s % 2 + 1, wide] = tile[s : s + 1]

    ones = jnp.ones((8, BLK), F32)
    for g in range(GROUPS):
        product = gu_ref[g] * wu_ref[g].astype(F32) + gv_ref[g] * wv_ref[g].astype(F32)
        sums = lax.dot_general(
            ones, product, (((1,), (1,)), ((), ())),
            precision=lax.Precision.HIGHEST, preferred_element_type=F32,
        )
        gain_out[:, lanes(g)] = sums[:1] / gain_ref[:, lanes(g)]


def call(kernel, outs, scratch=(), flops=0, moved=0, vmem=24, smem=(), hbm=(), hbm_out=(), free=()):
    shapes = [jax.ShapeDtypeStruct(shape, dtype) for shape, dtype in outs]
    whole = pl.BlockSpec(memory_space=pltpu.VMEM)

    def run(*args):
        specs = [whole] * len(args)
        for at in smem:
            specs[at] = pl.BlockSpec(memory_space=pltpu.SMEM)
        for at in hbm:
            specs[at] = pl.BlockSpec(memory_space=pltpu.HBM)
        for at in free:
            specs[at] = pl.BlockSpec(memory_space=pl.ANY)
        return pl.pallas_call(
            kernel,
            out_shape=shapes,
            in_specs=specs,
            out_specs=[
                pl.BlockSpec(memory_space=pltpu.HBM) if at in hbm_out else whole
                for at in range(len(shapes))
            ],
            scratch_shapes=list(scratch),
            compiler_params=pltpu.CompilerParams(vmem_limit_bytes=vmem << 20),
            cost_estimate=pl.CostEstimate(
                flops=int(flops), bytes_accessed=int(moved), transcendentals=0
            ),
        )(*args)

    return run


def rotated(values, axis, step=1):
    n = lax.axis_size(axis)
    if not isinstance(values, (list, tuple)):
        values = [values] * (n // step - 1)
    return [
        lax.ppermute(value, axis, [(s, (s + k * step) % n) for s in range(n)])
        for k, value in enumerate(values, 1)
    ]


def swapped(value, axis="c", bit=1):
    return lax.ppermute(value, axis, [(s, s ^ bit) for s in range(lax.axis_size(axis))])


def per_device(tokens, cotangent, gain, w_u, w_v, w_o, local_factor, butterfly):
    x = tokens.reshape(BLK, -1)
    cot = cotangent.reshape(BLK, -1)
    gain2 = gain.reshape(1, -1)
    wide = (BLK, GROUPS * BLK)
    place = jnp.stack(
        [lax.axis_index(a) for a in ("y", "z", "c")]
    ).astype(jnp.int32)

    send = call(
        first_kernel,
        [((GROUPS, 16, 3 * PL, BLK), BF)],
        scratch=[
            pltpu.VMEM(wide, BF),
            pltpu.VMEM(wide, BF),
            pltpu.VMEM((BLK, BLK), BF),
            pltpu.VMEM((GROUPS, 16, 3 * PL, BLK), BF),
            pltpu.SemaphoreType.DMA((7,)),
        ],
        flops=1.4e8,
        moved=4e6,
        hbm=(0, 1, 3),
        hbm_out=(0,),
        vmem=58,
    )(x, cot, gain2, local_factor)[0]
    recv = lax.all_to_all(send.reshape(BLOCKS, 3 * PL, BLK), SEQ, 0, 0)

    tiled = (BLOCKS, 2, 2, 8, 128)
    quarter = (25, 8, 128)
    back, keep, give = call(
        mid_kernel,
        [((BLOCKS, 2 * PL, BLK), BF), ((4,) + quarter, F32), ((4,) + quarter, BF)],
        scratch=[
            pltpu.VMEM((BLOCKS, 3 * PL, BLK), BF),
            pltpu.VMEM((BLOCKS, 2 * PL, BLK), BF),
            pltpu.VMEM(butterfly.shape[:3] + (BLK,), F32),
            pltpu.VMEM((BLK, BLK), BF),
            pltpu.VMEM((BLK, BLK), BF),
            pltpu.VMEM((BLK, BLK), BF),
            pltpu.VMEM(tiled, F32),
            pltpu.VMEM(tiled, F32),
            pltpu.VMEM(tiled, F32),
            pltpu.VMEM((BLOCKS * PL, BLK), F32),
            pltpu.VMEM((BLOCKS * PL, BLK), F32),
            pltpu.VMEM((24, 2, 8, 128), F32),
            pltpu.VMEM((24, 2, 8, 128), F32),
            pltpu.VMEM((3, BLK, BLK), F32),
            pltpu.SemaphoreType.DMA((4,)),
            pltpu.SemaphoreType.DMA((4,)),
            pltpu.SemaphoreType.DMA((4,)),
        ],
        flops=8e8,
        moved=4e6,
        vmem=63,
        smem=(0,),
        hbm=(2, 3, 4, 5),
        free=(1,),
        hbm_out=(0,),
    )(place, recv, butterfly, w_u, w_v, w_o)

    recv2 = lax.all_to_all(back, SEQ, 0, 0).reshape(GROUPS, 16, 2 * PL, BLK)

    own, *gives = call(
        core_sum_kernel, [(quarter, F32)] + [(quarter, BF)] * 3, moved=1e6, smem=(0,)
    )(place, keep, swapped(give))
    slice_ = call(quarter_sum_kernel, [(quarter, BF)], moved=3e5)(own, *rotated(gives, "y"))[0]
    for axis, bit in (("dp", 1), ("dp", 2), ("z", 1)):
        slice_ = call(pair_sum_kernel, [(quarter, BF)], moved=2e5)(
            slice_, swapped(slice_, axis, bit)
        )[0]
    got_z = rotated(slice_, "z", 2)

    recv2, slice_ = lax.optimization_barrier((recv2, slice_))
    part = call(local_kernel, [((BLK, BLK), BF)], flops=1.3e8, moved=1.2e6)(
        recv2, x, gain2, w_u
    )[0]
    got_z, part, got_part = lax.optimization_barrier((got_z, part, swapped(part, "dp", 1)))
    pair = call(pair_sum_kernel, [((BLK, BLK), BF)], moved=4e5)(part, got_part)[0]
    other_pair = swapped(pair, "dp", 2)
    mine_y = call(gather_kernel, [((4,) + quarter, BF)], moved=4e5, smem=(0,))(
        place, slice_, *got_z
    )[0]
    got_y = rotated(mine_y, "y")
    mixed, dx = call(
        last_kernel, [(wide, BF), (wide, BF)], scratch=[pltpu.VMEM(wide, F32)],
        flops=6e8, moved=8e6,
    )(recv2, x, cot, gain2, w_u, w_v, w_o, local_factor)
    got_y, mixed, dx, pair = lax.optimization_barrier((got_y, mixed, dx, pair))
    halves = [mine_y] + got_y
    others = [swapped(half) for half in halves]

    shape = (GROUPS, BLK, BLK)
    gu, gv, go, grad_gain, grad_bfly = call(
        place_kernel,
        [(shape, F32)] * 3 + [(gain2.shape, F32), (butterfly.shape, F32)],
        moved=5e6,
        smem=(0,),
    )(place, w_u, w_v, gain2, *halves, *others)
    other_pair, grad_gain = lax.optimization_barrier((other_pair, grad_gain))
    grad_local = call(pair_sum_kernel, [((BLK, BLK), F32)], moved=5e5)(pair, other_pair)[0]

    return (
        mixed.reshape(tokens.shape),
        dx.reshape(tokens.shape),
        gu,
        gv,
        go,
        grad_gain.reshape(gain.shape),
        grad_local,
        grad_bfly,
    )


def solution(mesh):
    fine = Mesh(mesh.devices.reshape(4, 8, 4, 2), ("dp", "z", "y", "c"))
    block = P("dp", SEQ, None)
    return jax.shard_map(
        per_device,
        mesh=fine,
        in_specs=(block, block, P(), P(), P(), P(), P(SEQ, None), P()),
        out_specs=(block, block, P(), P(), P(), P(), P(SEQ, None), P()),
        check_vma=False,
    )
```
